256 devices in a mesh: dom: 64 (over z, y, core), sect: 4 (over x).
Axes of the slice: x: 4, y: 4, z: 8, core: 2. Of those that a mesh axis runs over, the one named last changes fastest.
Arguments:
- fields: float32 [64, 4, 6, 35, 256], P('dom', 'sect'), may hold values from -6 to 6
- residual: float32 [64, 4, 6, 35, 256], P('dom', 'sect'), may hold values from -3 to 3
- geometry: float32 [64, 4, 9, 256], P('dom', 'sect'), may hold values from -1.5 to 1.5
- normals: float32 [64, 4, 3, 4, 256], P('dom', 'sect'), may hold values from -1 to 1, as said below
- face_scale: float32 [64, 4, 4, 256], P('dom', 'sect'), may hold values from 1 to 4
- derivatives: float32 [3, 35, 35], replicated, may hold values from -1 to 1
- lift_matrix: float32 [35, 60], replicated, may hold values from -0.75 to 0.75
- face_source: int32 [64, 4, 1024], P('dom', 'sect'), may hold values from 0 to 2047, as said below
- face_perm: int32 [64, 4, 1024], P('dom', 'sect'), may hold values from 0 to 5
- send_cycle: int32 [64, 4, 768], P('dom', 'sect'), may hold values from 0 to 1023
- send_layer: int32 [64, 4, 256], P('dom', 'sect'), may hold values from 0 to 1023
- surface_faces: int32 [64, 4, 128], P('dom', 'sect'), may hold values from 0 to 1023
- surface_count: int32 [64, 4], P('dom', 'sect'), may hold values from 0 to 128, as said below
- surface_points: float32 [64, 4, 3, 1920], P('dom', 'sect'), may hold values from -2 to 2
- surface_weights: float32 [64, 4, 1920], P('dom', 'sect'), may hold values from 0.001 to 0.004
- angles: float32 [2, 1024], replicated, may hold values from -3.140625 to 3.140625
Outputs:
- fields_out: float32 [64, 4, 6, 35, 256], P('dom', 'sect')
- residual_out: float32 [64, 4, 6, 35, 256], P('dom', 'sect')
- far_field: float32 [12, 1024], P(None, 'sect')
The draws below stay inside these ranges and needn't reach their ends.
Inputs may be any that keep to these rules, and one draw needn't show every extreme that they name: `face_source`: entries under 4 * 256 name a face f = k * 256 + e of the same partition; 1024 + k * 128 + s names slot s of cycle_in block k; 1792 + s slot s of below (only where g > 0) and 1920 + s slot s of above (only where g < 3). `surface_count`: some partition has exactly 128 live faces. `normals`: unit vectors.
All inputs are finite; a program needn't handle non-finite values.
Results may differ from the reference program's by a relative error of at most 0.0003.
Values sent between devices are 32-bit elements; how exact they have to be, the bound alone decides.
A program may use at most 192 MiB of HBM per device.

```python
import math
import jax
import jax.numpy as jnp
import numpy as np
from jax import lax

NP = 35
NFP = 15
FIELDS = 6
HOPS = 3
ANGLES = 1024
E_DEV = 256
SLOTS = 128
HMAX = 128
PEERS = 64
GROUPS = 4


def draw_normals(key, part):
    key = jax.random.fold_in(key, 7)
    first_key, second_key = jax.random.split(key, 2)
    array_shape = (PEERS, GROUPS, 4, E_DEV)
    polar = jax.random.uniform(first_key, array_shape, jnp.float32, 0.0, math.pi)
    azimuth = jax.random.uniform(second_key, array_shape, jnp.float32, -math.pi, math.pi)
    return jnp.stack([jnp.sin(polar) * jnp.cos(azimuth), jnp.sin(polar) * jnp.sin(azimuth), jnp.cos(polar)], axis=2).astype(jnp.float32)


def draw_face_source(key, part):
    key = jax.random.fold_in(key, 11)
    key_list = jax.random.split(key, 6)
    array_shape = (PEERS, GROUPS, 4 * E_DEV)
    kind_draw = jax.random.randint(key_list[0], array_shape, 0, 100)
    local_face = jax.random.randint(key_list[1], array_shape, 0, 4 * E_DEV)
    cycle_block = jax.random.randint(key_list[2], array_shape, 0, 2 * HOPS)
    cycle_slot = jax.random.randint(key_list[3], array_shape, 0, SLOTS)
    side_draw = jax.random.randint(key_list[4], array_shape, 0, 2)
    layer_slot = jax.random.randint(key_list[5], array_shape, 0, SLOTS)
    group_index = lax.broadcasted_iota(jnp.int32, array_shape, 1)
    layer_side = jnp.where(group_index == 0, 1, jnp.where(group_index == GROUPS - 1, 0, side_draw))
    local_total = 4 * E_DEV
    from_cycle = local_total + cycle_block * SLOTS + cycle_slot
    from_layer = local_total + (2 * HOPS + layer_side) * SLOTS + layer_slot
    result = jnp.where(kind_draw < 8, from_cycle, jnp.where(kind_draw < 11, from_layer, local_face))
    result = result.at[0, 0, 0].set(local_total + (2 * HOPS + 2) * SLOTS - 1)
    result = result.at[0, 0, 1].set(0)
    return result.astype(jnp.int32)


def draw_surface_count(key, part):
    key = jax.random.fold_in(key, 13)
    first_key, second_key, third_key = jax.random.split(key, 3)
    drawn = jax.random.randint(first_key, (PEERS, GROUPS), 1, HMAX + 1)
    empty_draw = jax.random.randint(second_key, (PEERS, GROUPS), 0, 2)
    counts = jnp.where(empty_draw == 0, 0, drawn).reshape(-1)
    chosen = jax.random.randint(third_key, (), 0, PEERS * GROUPS)
    counts = counts.at[chosen].set(HMAX)
    return counts.reshape(PEERS, GROUPS).astype(jnp.int32)


def touch_ends(values, own_key, least, top_value):
    index_at = [jax.random.randint(jax.random.fold_in(own_key, axis), (), 0, length) for axis, length in enumerate(values.shape)]
    widest = values.shape.index(max(values.shape))
    neighbour = index_at[:widest] + [(index_at[widest] + 1) % values.shape[widest]] + index_at[widest + 1:]
    return values.at[tuple(index_at)].set(least).at[tuple(neighbour)].set(top_value)


def shard_levels(rng, extent, pieces, low, top_value):
    gain = 1.0
    for axis_at, blocks in pieces:
        steps = jax.random.uniform(jax.random.fold_in(jax.random.fold_in(rng, 6), axis_at), (blocks,), jnp.float32, low / len(pieces), top_value / len(pieces))
        gain = gain * jnp.repeat(jnp.exp(steps), extent[axis_at] // blocks).reshape((-1,) + (1,) * (len(extent) - 1 - axis_at))
    return gain


def scatter_about(rng, extent, width, bound, pieces=(), held_as=jnp.bfloat16):
    loudness = shard_levels(rng, extent, pieces, -0.22, 0.18) if pieces else 1.0
    values = jax.random.normal(rng, extent, jnp.float32) * width * loudness
    return jnp.minimum(jnp.maximum(values, -bound), bound).astype(held_as)


def setup_inputs(seed: int = 0) -> dict:
    seeds = jax.random.split(jax.random.key(seed), 17)
    fields = scatter_about(seeds[0], (PEERS, GROUPS, FIELDS, NP, E_DEV), 1.0, 6.0, ((0, 64), (1, 4)), jnp.float32)
    residual = scatter_about(seeds[1], (PEERS, GROUPS, FIELDS, NP, E_DEV), 0.5, 3.0, ((0, 64), (1, 4)), jnp.float32)
    geometry = jnp.clip(jax.random.uniform(seeds[2], (PEERS, GROUPS, 9, E_DEV), jnp.float32, -1.5, 1.5) * shard_levels(seeds[2], (PEERS, GROUPS, 9, E_DEV), ((0, 64), (1, 4)), -0.4, 0.0), -1.5, 1.5)
    normals = draw_normals(jax.random.fold_in(seeds[16], 71), 0)
    face_scale = jnp.clip(jnp.exp(math.log(4.0) - 1.3862944 * jax.random.uniform(seeds[4], (PEERS, GROUPS, 4, E_DEV), jnp.float32) ** shard_levels(seeds[4], (PEERS, GROUPS, 4, E_DEV), ((0, 64), (1, 4)), -0.2, 0.2)), 1.0, 4.0)
    derivatives = scatter_about(seeds[5], (3, NP, NP), NP ** -0.5, 1.0, (), jnp.float32)
    lift_matrix = scatter_about(seeds[6], (NP, 4 * NFP), (4 * NFP) ** -0.5, 0.75, (), jnp.float32)
    face_source = draw_face_source(jax.random.fold_in(seeds[16], 71), 0)
    face_perm = touch_ends(jax.random.randint(seeds[8], (PEERS, GROUPS, 4 * E_DEV), 0, 6), jax.random.fold_in(seeds[8], 1), 0, 5).astype(jnp.int32)
    send_cycle = touch_ends(jax.random.randint(seeds[9], (PEERS, GROUPS, 2 * HOPS * SLOTS), 0, 4 * E_DEV), jax.random.fold_in(seeds[9], 1), 0, (4 * E_DEV) - 1).astype(jnp.int32)
    send_layer = touch_ends(jax.random.randint(seeds[10], (PEERS, GROUPS, 2 * SLOTS), 0, 4 * E_DEV), jax.random.fold_in(seeds[10], 1), 0, (4 * E_DEV) - 1).astype(jnp.int32)
    surface_faces = touch_ends(jax.random.randint(seeds[11], (PEERS, GROUPS, HMAX), 0, 4 * E_DEV), jax.random.fold_in(seeds[11], 1), 0, (4 * E_DEV) - 1).astype(jnp.int32)
    surface_count = draw_surface_count(jax.random.fold_in(seeds[16], 71), 0)
    surface_points = jnp.clip(jax.random.uniform(seeds[13], (PEERS, GROUPS, 3, NFP * HMAX), jnp.float32, -2.0, 2.0) * shard_levels(seeds[13], (PEERS, GROUPS, 3, NFP * HMAX), ((0, 64), (1, 4)), -0.4, 0.0), -2.0, 2.0)
    surface_weights = jnp.clip(jnp.exp(math.log(0.004) - 1.3862944 * jax.random.uniform(seeds[14], (PEERS, GROUPS, NFP * HMAX), jnp.float32) ** shard_levels(seeds[14], (PEERS, GROUPS, NFP * HMAX), ((0, 64), (1, 4)), -0.2, 0.2)), 0.001, 0.004)
    angles = jnp.clip(jax.random.uniform(seeds[15], (2, ANGLES), jnp.float32, -3.140625, 3.140625), -3.140625, 3.140625)
    return {"fields": fields, "residual": residual, "geometry": geometry, "normals": normals, "face_scale": face_scale, "derivatives": derivatives, "lift_matrix": lift_matrix, "face_source": face_source, "face_perm": face_perm, "send_cycle": send_cycle, "send_layer": send_layer, "surface_faces": surface_faces, "surface_count": surface_count, "surface_points": surface_points, "surface_weights": surface_weights, "angles": angles}


HIGHEST_PRECISION = lax.Precision.HIGHEST
SECTION_A = (-0.4178904745, -1.192151694643)
SECTION_B = (0.3792103129999, 0.8229550293869)
SECTION_C = (0.1496590219993, 0.3704009573644)
TIME_STEP = 0.2
ANGULAR_FREQUENCY = 2.0 * math.pi
WAVENUMBER = 2.0 * math.pi


def static_tables():
    node_list = []
    for i in range(5):
        for j in range(5 - i):
            for k in range(5 - i - j):
                node_list.append((i, j, k, 4 - i - j - k))
    face_nodes = []
    for which_face in range(4):
        face_nodes.append([n for n, barycentric in enumerate(node_list) if barycentric[which_face] == 0])
    reduced = [tuple(b for q, b in enumerate(node_list[n]) if q != 0) for n in face_nodes[0]]
    orderings = [(0, 1, 2), (1, 2, 0), (2, 0, 1), (0, 2, 1), (2, 1, 0), (1, 0, 2)]
    permutation = [[reduced.index(tuple(triple[s] for s in ordering)) for triple in reduced] for ordering in orderings]
    return np.array(face_nodes, np.int32), np.array(permutation, np.int32)


def cross_product(a, b):
    return [a[1] * b[2] - a[2] * b[1], a[2] * b[0] - a[0] * b[2], a[0] * b[1] - a[1] * b[0]]


def face_traces(fields, face_nodes):
    element_count = fields.shape[-1]
    picked = fields[:, face_nodes.reshape(-1), :]
    return picked.reshape(6, 4, 15, element_count).transpose(0, 2, 1, 3).reshape(6, 15, 4 * element_count)


def tendency(fields, inner_trace, outer_trace, factors, normals, face_scale, derivatives, lift_matrix):
    element_count = fields.shape[-1]
    e_jump = inner_trace[:3] - outer_trace[:3]
    h_jump = inner_trace[3:] - outer_trace[3:]
    normal = normals.reshape(3, 1, 4 * element_count)
    e_dot = jnp.sum(normal * e_jump, axis=0)
    h_dot = jnp.sum(normal * h_jump, axis=0)
    flux_e = jnp.stack(cross_product(normal, h_jump)) + e_jump - normal * e_dot
    flux_h = -jnp.stack(cross_product(normal, e_jump)) + h_jump - normal * h_dot
    face_factor = 0.5 * face_scale.reshape(1, 1, 4 * element_count)
    flux_all = jnp.concatenate([flux_e, flux_h]) * face_factor
    flux_all = flux_all.reshape(6, 15, 4, element_count).transpose(0, 2, 1, 3).reshape(6, 60, element_count)
    lifted = jnp.einsum('ij,cjx->cix', lift_matrix, flux_all, precision=HIGHEST_PRECISION)
    slopes = jnp.einsum('rij,cjx->rcix', derivatives, fields, precision=HIGHEST_PRECISION)
    gradients = [factors[m] * slopes[0] + factors[3 + m] * slopes[1] + factors[6 + m] * slopes[2] for m in range(3)]
    curl_h = [gradients[1][5] - gradients[2][4], gradients[2][3] - gradients[0][5], gradients[0][4] - gradients[1][3]]
    curl_e = [gradients[1][2] - gradients[2][1], gradients[2][0] - gradients[0][2], gradients[0][1] - gradients[1][0]]
    return jnp.concatenate([jnp.stack(curl_h) + lifted[:3], -jnp.stack(curl_e) + lifted[3:]])


def surface_currents(inner_trace, normals, surface_faces):
    face_count = surface_faces.shape[0]
    surface_trace = jnp.take(inner_trace, surface_faces, axis=2).reshape(6, 15 * face_count)
    normal = jnp.take(normals.reshape(3, -1), surface_faces, axis=1)
    normal = jnp.broadcast_to(normal[:, None, :], (3, 15, face_count)).reshape(3, 15 * face_count)
    electric = [surface_trace[0], surface_trace[1], surface_trace[2]]
    magnetic = [surface_trace[3], surface_trace[4], surface_trace[5]]
    return jnp.stack(cross_product(normal, magnetic) + [-x for x in cross_product(normal, electric)])


def far_projection(real_part, imag_part, points, weights, count_live, angles):
    face_count = weights.shape[0] // 15
    live_mask = (jnp.arange(15 * face_count, dtype=jnp.int32) % face_count < count_live).astype(jnp.float32)
    weighted = jnp.concatenate([real_part, imag_part]) * (weights * live_mask)
    polar = angles[0]
    azimuth = angles[1]
    direction = jnp.stack([jnp.sin(polar) * jnp.cos(azimuth), jnp.sin(polar) * jnp.sin(azimuth), jnp.cos(polar)])
    phase_arg = WAVENUMBER * jnp.dot(points.T, direction, precision=HIGHEST_PRECISION)
    trig_table = jnp.concatenate([jnp.cos(phase_arg), jnp.sin(phase_arg)], axis=1)
    projected = jnp.dot(weighted, trig_table, precision=HIGHEST_PRECISION)
    angle_count = angles.shape[1]
    real_far = projected[:6, :angle_count] - projected[6:, angle_count:]
    imag_far = projected[:6, angle_count:] + projected[6:, :angle_count]
    return jnp.concatenate([real_far, imag_far])


def reference(fields, residual, geometry, normals, face_scale, derivatives, lift_matrix, face_source, face_perm, send_cycle, send_layer, surface_faces, surface_count, surface_points, surface_weights, angles):
    face_nodes, node_table = static_tables()
    orientations = jnp.asarray(node_table)
    offsets = list(range(-HOPS, 0)) + list(range(1, HOPS + 1))

    def flatten_parts(array):
        return array.reshape((PEERS * GROUPS,) + array.shape[2:])

    field_now = flatten_parts(fields)
    residual_now = flatten_parts(residual)
    real_sum = jnp.zeros((PEERS * GROUPS, 6, 15 * HMAX), jnp.float32)
    imag_sum = jnp.zeros((PEERS * GROUPS, 6, 15 * HMAX), jnp.float32)
    for step_index in range(2):
        def outgoing(packed):
            field_part, cycle_part, layer_part = packed
            traces = face_traces(field_part, face_nodes)
            return jnp.take(traces, cycle_part, axis=2), jnp.take(traces, layer_part, axis=2)

        cycle_out, layer_out = lax.map(outgoing, (field_now, flatten_parts(send_cycle), flatten_parts(send_layer)))
        cycle_out = cycle_out.reshape(PEERS, GROUPS, 6, 15, 2 * HOPS, SLOTS)
        cycle_in = jnp.stack([jnp.roll(cycle_out[:, :, :, :, 2 * HOPS - 1 - k], -offset, axis=0) for k, offset in enumerate(offsets)], axis=4)
        cycle_in = cycle_in.reshape(PEERS, GROUPS, 6, 15, 2 * HOPS * SLOTS)
        layer_out = layer_out.reshape(PEERS, GROUPS, 6, 15, 2 * SLOTS)
        zero_rim = jnp.zeros((PEERS, 1, 6, 15, SLOTS), jnp.float32)
        below = jnp.concatenate([zero_rim, layer_out[:, :-1, :, :, SLOTS:]], axis=1)
        above = jnp.concatenate([layer_out[:, 1:, :, :, :SLOTS], zero_rim], axis=1)
        received = flatten_parts(jnp.concatenate([cycle_in, below, above], axis=4))

        def advance(packed):
            field_part, residual_part, received_part, factor_part, normal_part, scale_part, source_part, perm_part, surface_part = packed
            inner_trace = face_traces(field_part, face_nodes)
            combined = jnp.concatenate([inner_trace, received_part], axis=2)
            outer_trace = combined[:, orientations[perm_part].T, source_part[None, :]]
            rate = tendency(field_part, inner_trace, outer_trace, factor_part, normal_part, scale_part, derivatives, lift_matrix)
            residual_next = SECTION_A[step_index] * residual_part + TIME_STEP * rate
            field_next = field_part + SECTION_B[step_index] * residual_next
            return field_next, residual_next, surface_currents(inner_trace, normal_part, surface_part)

        field_now, residual_now, currents = lax.map(advance, (field_now, residual_now, received, flatten_parts(geometry), flatten_parts(normals), flatten_parts(face_scale), flatten_parts(face_source), flatten_parts(face_perm), flatten_parts(surface_faces)))
        phase_now = ANGULAR_FREQUENCY * TIME_STEP * SECTION_C[step_index]
        real_sum = real_sum + math.cos(phase_now) * currents
        imag_sum = imag_sum - math.sin(phase_now) * currents

    def project(packed):
        real_part, imag_part, point_part, weight_part, count_part = packed
        return far_projection(real_part, imag_part, point_part, weight_part, count_part, angles)

    partials = lax.map(project, (real_sum, imag_sum, flatten_parts(surface_points), flatten_parts(surface_weights), surface_count.reshape(-1)))
    far_field = jnp.sum(partials, axis=0)
    return field_now.reshape(fields.shape), residual_now.reshape(residual.shape), far_field
```

```python
import functools
import math

import jax
import jax.numpy as jnp
import numpy as np
from jax import lax
from jax.experimental import pallas as pl
from jax.experimental.pallas import tpu as pltpu
from jax.sharding import PartitionSpec as P

SECTION_A = (-0.4178904745, -1.192151694643)
SECTION_B = (0.3792103129999, 0.8229550293869)
SECTION_C = (0.1496590219993, 0.3704009573644)
TIME_STEP = 0.2
ANGULAR_FREQUENCY = 2.0 * math.pi
HOPS = 3
MESH = pl.DeviceIdType.MESH
F32 = jnp.float32
BF16 = jnp.bfloat16

NODES = 35
NODE_PAD = 40
SPLIT_PAD = 48
FACE = 15
FACE_PAD = 16
ELEMS = 256
FACES = 4 * ELEMS
SLOTS = 128
ANGLES = 1024

SIN_POLY = (4.442883014678955, -7.308245658874512, 3.6063544750213623, -0.8461129069328308, 0.10982698947191238)
COS_POLY = (1.4142135381698608, -6.978850841522217, 5.7394609451293945, -1.8835630416870117, 0.31069818139076233)
ROUNDER = 12582912.0


def static_tables():
    node_list = []
    for i in range(5):
        for j in range(5 - i):
            for k in range(5 - i - j):
                node_list.append((i, j, k, 4 - i - j - k))
    face_nodes = []
    for which_face in range(4):
        face_nodes.append(
            [n for n, barycentric in enumerate(node_list) if barycentric[which_face] == 0]
        )
    reduced = [tuple((b for q, b in enumerate(node_list[n]) if q != 0)) for n in face_nodes[0]]
    orderings = [(0, 1, 2), (1, 2, 0), (2, 0, 1), (0, 2, 1), (2, 1, 0), (1, 0, 2)]
    permutation = [
        [reduced.index(tuple((triple[s] for s in ordering))) for triple in reduced]
        for ordering in orderings
    ]
    return (np.array(face_nodes, np.int32), np.array(permutation, np.int32))


def constant_matrices():
    face_nodes, node_table = static_tables()
    pick = np.zeros((64, 5 * SPLIT_PAD), np.float32)
    for k in range(4):
        for n in range(FACE):
            for part in range(3):
                pick[k * FACE_PAD + n, part * SPLIT_PAD + face_nodes[k][n]] = 1
    place = np.zeros((2, 128, 5 * SPLIT_PAD), np.float32)
    for i in range(NODES):
        for part in range(3):
            place[0, i, part * SPLIT_PAD + i] = 1
        for part in range(3, 5):
            place[1, i, part * SPLIT_PAD + i] = 1
    lift = np.zeros((2, 128, 192), np.float32)
    for k in range(4):
        for n in range(FACE):
            for part in range(3):
                lift[part // 2, k * FACE + n, part * 64 + k * FACE_PAD + n] = 1
    table = np.zeros((FACE_PAD, 8), np.int32)
    table[:FACE, :6] = node_table.T
    table[FACE, :] = FACE
    return (
        pick.astype(jnp.bfloat16),
        place.reshape(256, -1).astype(jnp.bfloat16),
        lift.reshape(256, -1).astype(jnp.bfloat16),
        table,
    )


def dot(a, b, dims=((1,), (0,))):
    return lax.dot_general(a, b, (dims, ((), ())), preferred_element_type=F32)


def split2(x):
    high = x.astype(BF16)
    return high, (x - high.astype(F32)).astype(BF16)


def split3(x):
    high = x.astype(BF16)
    rest = x - high.astype(F32)
    middle = rest.astype(BF16)
    return high, middle, (rest - middle.astype(F32)).astype(BF16)


def cross(a, b):
    return [a[1] * b[2] - a[2] * b[1], a[2] * b[0] - a[0] * b[2], a[0] * b[1] - a[1] * b[0]]


def kernel(
    fields,
    residual,
    geometry,
    normals,
    face_scale,
    derivatives,
    lift_matrix,
    face_source,
    face_perm,
    send_list,
    surface_count,
    surface_points,
    surface_weights,
    angles,
    pick,
    place,
    place_lift,
    node_table,
    fields_out,
    residual_out,
    far_out,
    q_now,
    w_now,
    q_parts,
    small,
    volume_matrix,
    lift_stack,
    trace,
    trace_parts,
    received_parts,
    pick_out,
    pick_in,
    node_index,
    send,
    recv,
    phase,
    trig,
    point_parts,
    weighted,
    far_part,
    far_a,
    far_b,
    far_c,
    send_sem,
    recv_sem,
    far_send_sem,
    far_recv_sem,
):
    d = lax.axis_index("dom")
    g = lax.axis_index("sect")
    block, place_in = d // 8, d % 8

    def dom_shift(by):
        return lax.rem(d + 64 + by, 64)

    def sect_shift(by):
        return lax.rem(g + 4 + by, 4)

    offsets = list(range(-HOPS, 0)) + list(range(1, HOPS + 1))
    near = [(dom_shift(o), g) for o in offsets] + [(d, sect_shift(-1)), (d, sect_shift(1))]
    sect_peers = [(d, sect_shift(i)) for i in range(1, 4)]
    in_peers = [(block * 8 + lax.rem(place_in + i, 8), g) for i in range(1, 8)]
    block_peers = [(lax.rem(block + i, 8) * 8 + place_in, g) for i in range(1, 8)]
    everyone = near + sect_peers + in_peers + block_peers
    barrier = pltpu.get_barrier_semaphore()
    for peer in everyone:
        pl.semaphore_signal(barrier, inc=1, device_id=peer, device_id_type=MESH)

    q_now[...] = jnp.zeros_like(q_now)
    w_now[...] = jnp.zeros_like(w_now)
    small[...] = jnp.zeros_like(small)
    for c in range(6):
        q_now[c, 0:NODES, :] = fields[c]
        w_now[c, 0:NODES, :] = residual[c]

    def make_parts():
        for c in range(6):
            p1, p2, p3 = split3(q_now[c])
            for at, part in enumerate((p1, p2, p3, p1, p2)):
                q_parts[at * SPLIT_PAD : (at + 1) * SPLIT_PAD, c * ELEMS : (c + 1) * ELEMS] = part

    def make_trace():
        picked = dot(pick[...], q_parts[...])
        for c in range(6):
            for k in range(4):
                trace[c * FACE_PAD : (c + 1) * FACE_PAD, k * ELEMS : (k + 1) * ELEMS] = picked[
                    k * FACE_PAD : (k + 1) * FACE_PAD, c * ELEMS : (c + 1) * ELEMS
                ]
        high, low = split2(trace[...])
        trace_parts[0:96, :] = high
        trace_parts[96:192, :] = low

    def one_hot(target, index_row, rows, step):
        width = index_row.shape[1]

        def body(i, carry):
            at = pl.multiple_of(i * step, step)
            rows_at = lax.broadcasted_iota(jnp.int32, (step, width), 0) + i * step
            target[pl.ds(at, step), :] = jnp.where(rows_at == index_row, 1.0, 0.0).astype(BF16)
            return carry

        lax.fori_loop(0, rows // step, body, 0)

    make_parts()
    make_trace()
    one_hot(pick_out, send_list[...], FACES, 32)

    def copies(step):
        made = []
        for j, peer in enumerate(near):
            landing = 5 - j if j < 6 else 13 - j
            made.append(
                pltpu.make_async_remote_copy(
                    src_ref=send.at[step, j],
                    dst_ref=recv.at[step, landing],
                    send_sem=send_sem.at[step, j],
                    recv_sem=recv_sem.at[step, landing],
                    device_id=peer,
                    device_id_type=MESH,
                )
            )
        return made

    def gather_out(step):
        both = dot(trace_parts[...], pick_out[...])
        gathered = both[0:96] + both[96:192]
        for j in range(8):
            send[step, j] = gathered[:, j * SLOTS : (j + 1) * SLOTS]
        return gathered[:, 8 * SLOTS :]

    surface_0 = gather_out(0)
    pl.semaphore_wait(barrier, len(everyone))
    transfers_0 = copies(0)
    for copy in transfers_0:
        copy.start()

    for r in range(3):
        small[r * NODE_PAD : r * NODE_PAD + NODES, 0:NODES] = derivatives[r]
    main, rest = split2(small[0:128, :])
    volume_matrix[...] = (dot(main, place[0:128, :]) + dot(rest, place[128:256, :])).astype(BF16)
    small[0:128, :] = jnp.zeros((128, 128), F32)
    small[0:NODES, 0:60] = lift_matrix[...]
    main, rest = split2(small[0:SPLIT_PAD, :])
    lift_stack[...] = (dot(main, place_lift[0:128, :]) + dot(rest, place_lift[128:256, :])).astype(BF16)
    small[0:SPLIT_PAD, :] = jnp.zeros((SPLIT_PAD, 128), F32)

    one_hot(pick_in, face_source[...], 2 * FACES, 32)
    orient = jnp.broadcast_to(face_perm[...], (FACE_PAD, FACES))
    index = jnp.broadcast_to(node_table[:, 0:1], (FACE_PAD, FACES))
    for which in range(1, 6):
        index = jnp.where(orient == which, node_table[:, which : which + 1], index)
    node_index[...] = index

    normal_rows = jnp.concatenate(
        [jnp.concatenate([normals[m, k : k + 1, :] for k in range(4)], axis=1) for m in range(3)]
        + [jnp.zeros((5, FACES), F32)],
        axis=0,
    )
    high, low = split2(jnp.concatenate([normal_rows, normal_rows - normal_rows.astype(BF16).astype(F32)], axis=0))
    picked = dot(high, pick_out[:, 8 * SLOTS :])
    surface_normal = picked[0:8] + picked[8:16]

    def currents(gathered):
        e = [gathered[c * FACE_PAD : (c + 1) * FACE_PAD, :] for c in range(3)]
        h = [gathered[c * FACE_PAD : (c + 1) * FACE_PAD, :] for c in range(3, 6)]
        v = [surface_normal[m : m + 1, :] for m in range(3)]
        return cross(v, h) + [-x for x in cross(v, e)]

    currents_0 = currents(surface_0)

    polar, azimuth = angles[0:1, :], angles[1:2, :]
    direction = jnp.concatenate(
        [
            jnp.sin(polar) * jnp.cos(azimuth),
            jnp.sin(polar) * jnp.sin(azimuth),
            jnp.cos(polar),
            jnp.zeros((5, ANGLES), F32),
        ],
        axis=0,
    )
    d1, d2, d3 = [x.astype(F32) for x in split3(direction)]
    direction_parts = jnp.concatenate([d1, d2, d1, d3, d2, d1], axis=0).astype(BF16)
    points = jnp.concatenate([surface_points[...], jnp.zeros((5, FACE * SLOTS), F32)], axis=0)
    p1, p2, p3 = [x.astype(F32) for x in split3(points)]
    stacked = jnp.concatenate([p1, p1, p2, p1, p2, p3], axis=0)
    point_parts[...] = stacked.T.astype(BF16)

    def table_block(n, carry):
        rows = pl.multiple_of(n * SLOTS, SLOTS)
        phase[...] = dot(point_parts[pl.ds(rows, SLOTS), :], direction_parts)

        def table_rows(i, inner):
            at = pl.multiple_of(i * 16, 16)
            turns = phase[pl.ds(at, 16), :]
            r = turns - ((turns + ROUNDER) - ROUNDER)
            u = r * r
            s = SIN_POLY[4]
            c = COS_POLY[4]
            for order in range(3, -1, -1):
                s = s * u + SIN_POLY[order]
                c = c * u + COS_POLY[order]
            s = s * r
            sine = s * c
            cosine = 1.0 - s * s
            out = pl.multiple_of(rows + at, 16)
            high_c, low_c = split2(cosine)
            high_s, low_s = split2(sine)
            trig[pl.ds(out, 16), 0:ANGLES] = high_c
            trig[pl.ds(out, 16), ANGLES : 2 * ANGLES] = high_s
            trig[pl.ds(out, 16), 2 * ANGLES : 3 * ANGLES] = low_c
            trig[pl.ds(out, 16), 3 * ANGLES :] = low_s
            return inner

        return lax.fori_loop(0, SLOTS // 16, table_rows, carry)

    lax.fori_loop(0, FACE, table_block, 0)

    def advance(step):
        slopes = dot(volume_matrix[...], q_parts[...])
        for slot in range(8):
            arrived = recv[step, slot]
            if slot == 6:
                arrived = jnp.where(g > 0, arrived, 0.0)
            if slot == 7:
                arrived = jnp.where(g < 3, arrived, 0.0)
            high, low = split2(arrived)
            received_parts[0:96, slot * SLOTS : (slot + 1) * SLOTS] = high
            received_parts[96:192, slot * SLOTS : (slot + 1) * SLOTS] = low
        both = dot(trace_parts[...], pick_in[0:FACES, :]) + dot(received_parts[...], pick_in[FACES:, :])
        column = both[0:96] + both[96:192]
        index = node_index[...]
        in_first = index < 8
        index = index & 7

        def by_node(x):
            halves = []
            for half in (slice(0, 8), slice(8, 16)):
                first = jnp.take_along_axis(x[0:8], index[half], axis=0, mode="promise_in_bounds")
                second = jnp.take_along_axis(x[8:16], index[half], axis=0, mode="promise_in_bounds")
                halves.append(jnp.where(in_first[half], first, second))
            return jnp.concatenate(halves, axis=0)

        jump = []
        for c in range(6):
            rows = slice(c * FACE_PAD, (c + 1) * FACE_PAD)
            jump.append(trace[rows, :] - by_node(column[rows, :]))
        flux = [[] for _ in range(6)]
        for k in range(4):
            part = [x[:, k * ELEMS : (k + 1) * ELEMS] for x in jump]
            v = [normals[m, k : k + 1, :] for m in range(3)]
            half = 0.5 * face_scale[k : k + 1, :]
            e, h = part[:3], part[3:]
            e_dot = v[0] * e[0] + v[1] * e[1] + v[2] * e[2]
            h_dot = v[0] * h[0] + v[1] * h[1] + v[2] * h[2]
            ve, vh = cross(v, e), cross(v, h)
            for m in range(3):
                flux[m].append((vh[m] + e[m] - v[m] * e_dot) * half)
                flux[3 + m].append((h[m] - ve[m] - v[m] * h_dot) * half)
        flux_rows = jnp.concatenate([jnp.concatenate(x, axis=0) for x in flux], axis=1)
        f1, f2 = split2(flux_rows)
        lifted = dot(lift_stack[...], jnp.concatenate([f1, f2, f1], axis=0))

        def slope(r, c):
            return slopes[r * NODE_PAD : (r + 1) * NODE_PAD, c * ELEMS : (c + 1) * ELEMS]

        factors = [geometry[i : i + 1, :] for i in range(9)]

        def gradient(m, c):
            return factors[m] * slope(0, c) + factors[3 + m] * slope(1, c) + factors[6 + m] * slope(2, c)

        for c in range(6):
            other = 3 if c < 3 else 0
            a, b = (c + 1) % 3, (c + 2) % 3
            curl = gradient(a, other + b) - gradient(b, other + a)
            if c >= 3:
                curl = -curl
            rate = curl + lifted[0:NODE_PAD, c * ELEMS : (c + 1) * ELEMS]
            w_next = SECTION_A[step] * w_now[c] + TIME_STEP * rate
            q_next = q_now[c, 0:NODE_PAD, :] + SECTION_B[step] * w_next
            if step == 0:
                w_now[c] = w_next
                q_now[c, 0:NODE_PAD, :] = q_next
            else:
                fields_out[c] = q_next[0:NODES]
                residual_out[c] = w_next[0:NODES]

    for copy in transfers_0:
        copy.wait()
    advance(0)

    make_parts()
    make_trace()
    surface_1 = gather_out(1)
    transfers_1 = copies(1)
    for copy in transfers_1:
        copy.start()
    currents_1 = currents(surface_1)

    turn = [ANGULAR_FREQUENCY * TIME_STEP * x for x in SECTION_C]
    weighted[...] = jnp.zeros_like(weighted)
    live = lax.broadcasted_iota(jnp.int32, (1, SLOTS), 1) < surface_count[...]
    node_weight = [
        jnp.where(live, surface_weights[:, n * SLOTS : (n + 1) * SLOTS], 0.0) for n in range(FACE)
    ]
    node_weight = jnp.concatenate(node_weight + [jnp.zeros((1, SLOTS), F32)], axis=0)
    for c in range(6):
        real = (math.cos(turn[0]) * currents_0[c] + math.cos(turn[1]) * currents_1[c]) * node_weight
        imag = (math.sin(turn[0]) * currents_0[c] + math.sin(turn[1]) * currents_1[c]) * -node_weight
        for n in range(FACE):
            weighted[c : c + 1, n * SLOTS : (n + 1) * SLOTS] = real[n : n + 1, :]
            weighted[8 + c : 9 + c, n * SLOTS : (n + 1) * SLOTS] = imag[n : n + 1, :]
    high, low = split2(weighted[...])
    weighted_parts = jnp.concatenate([high, low], axis=0)
    for j in range(4):
        at = j * ELEMS
        sums = []
        for first in (0, ANGLES):
            fine = dot(weighted_parts, trig[:, first + at : first + at + ELEMS])
            rest = dot(high, trig[:, 2 * ANGLES + first + at : 2 * ANGLES + first + at + ELEMS])
            sums.append(fine[0:16] + fine[16:32] + rest)
        by_cos, by_sin = sums
        far_part[j, 0:8] = by_cos[0:8] - by_sin[8:16]
        far_part[j, 8:16] = by_sin[0:8] + by_cos[8:16]

    def far_copies(stage, peers, source, landing):
        made = []
        for i, peer in enumerate(peers):
            made.append(
                pltpu.make_async_remote_copy(
                    src_ref=source(i),
                    dst_ref=landing(i),
                    send_sem=far_send_sem.at[stage, i],
                    recv_sem=far_recv_sem.at[stage, i],
                    device_id=peer,
                    device_id_type=MESH,
                )
            )
        for copy in made:
            copy.start()
        return made

    stage_a = far_copies(
        0, sect_peers, lambda i: far_part.at[sect_shift(i + 1)], lambda i: far_a.at[i]
    )
    for copy in stage_a:
        copy.wait()
    far_b[place_in] = far_part[g] + far_a[0] + far_a[1] + far_a[2]
    stage_b = far_copies(1, in_peers, lambda i: far_b.at[place_in], lambda i: far_b.at[place_in])
    for copy in stage_b:
        copy.wait()
    total = far_b[0]
    for i in range(1, 8):
        total = total + far_b[i]
    far_c[block] = total
    stage_c = far_copies(2, block_peers, lambda i: far_c.at[block], lambda i: far_c.at[block])

    for copy in transfers_1:
        copy.wait()
    advance(1)

    for copy in stage_c:
        copy.wait()
    total = far_c[0]
    for i in range(1, 8):
        total = total + far_c[i]
    far_out[0:6, :] = total[0:6]
    far_out[6:12, :] = total[8:14]


def on_device(
    fields,
    residual,
    geometry,
    normals,
    face_scale,
    derivatives,
    lift_matrix,
    face_source,
    face_perm,
    send_cycle,
    send_layer,
    surface_faces,
    surface_count,
    surface_points,
    surface_weights,
    angles,
):
    pick, place, place_lift, node_table = constant_matrices()
    send_list = jnp.concatenate([send_cycle[0], send_layer[0], surface_faces[0]], axis=1)
    vmem = pl.BlockSpec(memory_space=pltpu.VMEM)
    fields_out, residual_out, far = pl.pallas_call(
        kernel,
        out_shape=(
            jax.ShapeDtypeStruct((6, NODES, ELEMS), F32),
            jax.ShapeDtypeStruct((6, NODES, ELEMS), F32),
            jax.ShapeDtypeStruct((12, ELEMS), F32),
        ),
        in_specs=[vmem] * 18,
        out_specs=(vmem, vmem, vmem),
        scratch_shapes=[
            pltpu.VMEM((6, SPLIT_PAD, ELEMS), F32),
            pltpu.VMEM((6, NODE_PAD, ELEMS), F32),
            pltpu.VMEM((5 * SPLIT_PAD, 6 * ELEMS), BF16),
            pltpu.VMEM((128, 128), F32),
            pltpu.VMEM((128, 5 * SPLIT_PAD), BF16),
            pltpu.VMEM((SPLIT_PAD, 192), BF16),
            pltpu.VMEM((96, FACES), F32),
            pltpu.VMEM((192, FACES), BF16),
            pltpu.VMEM((192, 8 * SLOTS), BF16),
            pltpu.VMEM((FACES, 9 * SLOTS), BF16),
            pltpu.VMEM((2 * FACES, FACES), BF16),
            pltpu.VMEM((FACE_PAD, FACES), jnp.int32),
            pltpu.VMEM((2, 8, 96, SLOTS), F32),
            pltpu.VMEM((2, 8, 96, SLOTS), F32),
            pltpu.VMEM((SLOTS, ANGLES), F32),
            pltpu.VMEM((FACE * SLOTS, 4 * ANGLES), BF16),
            pltpu.VMEM((FACE * SLOTS, 48), BF16),
            pltpu.VMEM((16, FACE * SLOTS), F32),
            pltpu.VMEM((4, 16, ELEMS), F32),
            pltpu.VMEM((3, 16, ELEMS), F32),
            pltpu.VMEM((8, 16, ELEMS), F32),
            pltpu.VMEM((8, 16, ELEMS), F32),
            pltpu.SemaphoreType.DMA((2, 8)),
            pltpu.SemaphoreType.DMA((2, 8)),
            pltpu.SemaphoreType.DMA((3, 7)),
            pltpu.SemaphoreType.DMA((3, 7)),
        ],
        compiler_params=pltpu.CompilerParams(
            collective_id=0, has_side_effects=True, vmem_limit_bytes=48 * 1024 * 1024
        ),
    )(
        fields[0, 0],
        residual[0, 0],
        geometry[0, 0],
        normals[0, 0],
        face_scale[0, 0],
        derivatives,
        lift_matrix,
        face_source[0],
        face_perm[0],
        send_list,
        surface_count,
        surface_points[0, 0],
        surface_weights[0],
        angles,
        pick,
        place,
        place_lift,
        node_table,
    )
    return (fields_out[None, None], residual_out[None, None], far)


def solution(mesh):
    in_specs = (
        P("dom", "sect", None, None, None),
        P("dom", "sect", None, None, None),
        P("dom", "sect", None, None),
        P("dom", "sect", None, None, None),
        P("dom", "sect", None, None),
        P(),
        P(),
        P("dom", "sect", None),
        P("dom", "sect", None),
        P("dom", "sect", None),
        P("dom", "sect", None),
        P("dom", "sect", None),
        P("dom", "sect"),
        P("dom", "sect", None, None),
        P("dom", "sect", None),
        P(),
    )
    out_specs = (
        P("dom", "sect", None, None, None),
        P("dom", "sect", None, None, None),
        P(None, "sect"),
    )
    return jax.shard_map(
        on_device, mesh=mesh, in_specs=in_specs, out_specs=out_specs, check_vma=False
    )
```

```python
import functools
import math

import jax
import jax.numpy as jnp
import numpy as np
from jax import lax
from jax.experimental import pallas as pl
from jax.experimental.pallas import tpu as pltpu
from jax.sharding import PartitionSpec as P

SECTION_A = (-0.4178904745, -1.192151694643)
SECTION_B = (0.3792103129999, 0.8229550293869)
SECTION_C = (0.1496590219993, 0.3704009573644)
TIME_STEP = 0.2
ANGULAR_FREQUENCY = 2.0 * math.pi
HOPS = 3
MESH = pl.DeviceIdType.MESH
F32 = jnp.float32
BF16 = jnp.bfloat16

NODES = 35
NODE_PAD = 40
SPLIT_PAD = 48
FACE = 15
FACE_PAD = 16
ELEMS = 256
FACES = 4 * ELEMS
SLOTS = 128
ANGLES = 1024
POINTS = FACE * SLOTS

SIN_POLY = (4.442879676818848, -7.3078179359436035, 3.5977888107299805, -0.7912381887435913)
COS_POLY = (1.4142135381698608, -6.978850841522217, 5.7394609451293945, -1.8835630416870117, 0.31069818139076233)
SIN_MONIC = tuple(x / SIN_POLY[-1] for x in SIN_POLY[:-1])
COS_MONIC = tuple(x / COS_POLY[-1] for x in COS_POLY[:-1])
COS_GAIN = SIN_POLY[-1] * SIN_POLY[-1]
SIN_GAIN = SIN_POLY[-1] * COS_POLY[-1]


def static_tables():
    node_list = []
    for i in range(5):
        for j in range(5 - i):
            for k in range(5 - i - j):
                node_list.append((i, j, k, 4 - i - j - k))
    face_nodes = []
    for which_face in range(4):
        face_nodes.append(
            [n for n, barycentric in enumerate(node_list) if barycentric[which_face] == 0]
        )
    reduced = [tuple((b for q, b in enumerate(node_list[n]) if q != 0)) for n in face_nodes[0]]
    orderings = [(0, 1, 2), (1, 2, 0), (2, 0, 1), (0, 2, 1), (2, 1, 0), (1, 0, 2)]
    permutation = [
        [reduced.index(tuple((triple[s] for s in ordering))) for triple in reduced]
        for ordering in orderings
    ]
    return (np.array(face_nodes, np.int32), np.array(permutation, np.int32))


def constant_matrices():
    face_nodes, node_table = static_tables()
    pick = np.zeros((64, 5 * SPLIT_PAD), np.float32)
    for k in range(4):
        for n in range(FACE):
            for part in range(3):
                pick[k * FACE_PAD + n, part * SPLIT_PAD + face_nodes[k][n]] = 1
    place = np.zeros((2, 128, 5 * SPLIT_PAD), np.float32)
    for i in range(NODES):
        for part in range(3):
            place[0, i, part * SPLIT_PAD + i] = 1
        for part in range(3, 5):
            place[1, i, part * SPLIT_PAD + i] = 1
    lift = np.zeros((2, 128, 192), np.float32)
    for k in range(4):
        for n in range(FACE):
            for part in range(3):
                lift[part // 2, k * FACE + n, part * 64 + k * FACE_PAD + n] = 1
    table = np.zeros((FACE_PAD, 8), np.int32)
    table[:FACE, :6] = node_table.T
    table[FACE, :] = FACE
    return (
        pick.astype(jnp.bfloat16),
        place.reshape(256, -1).astype(jnp.bfloat16),
        lift.reshape(256, -1).astype(jnp.bfloat16),
        table,
    )


def dot(a, b, dims=((1,), (0,))):
    return lax.dot_general(a, b, (dims, ((), ())), preferred_element_type=F32)


def split2(x):
    high = x.astype(BF16)
    return high, (x - high.astype(F32)).astype(BF16)


def split3(x):
    high = x.astype(BF16)
    rest = x - high.astype(F32)
    middle = rest.astype(BF16)
    return high, middle, (rest - middle.astype(F32)).astype(BF16)


def cross(a, b):
    return [a[1] * b[2] - a[2] * b[1], a[2] * b[0] - a[0] * b[2], a[0] * b[1] - a[1] * b[0]]


def kernel(
    fields,
    residual,
    geometry,
    normals,
    face_scale,
    derivatives,
    lift_matrix,
    face_source,
    face_perm,
    send_list,
    surface_count,
    surface_points,
    surface_weights,
    angles,
    pick,
    place,
    place_lift,
    node_table,
    fields_out,
    residual_out,
    far_out,
    q_now,
    w_now,
    q_parts,
    small,
    volume_matrix,
    lift_stack,
    trace,
    trace_parts,
    received_parts,
    pick_out,
    pick_in,
    node_index,
    send,
    recv,
    phase,
    trig,
    point_parts,
    by_node,
    weighted,
    slopes,
    column,
    far_part,
    far_a,
    far_b,
    far_c,
    send_sem,
    recv_sem,
    far_send_sem,
    far_recv_sem,
):
    d = lax.axis_index("dom")
    g = lax.axis_index("sect")
    block, place_in = d // 8, d % 8

    def dom_shift(by):
        return lax.rem(d + 64 + by, 64)

    def sect_shift(by):
        return lax.rem(g + 4 + by, 4)

    offsets = list(range(-HOPS, 0)) + list(range(1, HOPS + 1))
    near = [(dom_shift(o), g) for o in offsets] + [(d, sect_shift(-1)), (d, sect_shift(1))]
    sect_peers = [(d, sect_shift(i)) for i in range(1, 4)]
    in_peers = [(block * 8 + lax.rem(place_in + i, 8), g) for i in range(1, 8)]
    block_peers = [(lax.rem(block + i, 8) * 8 + place_in, g) for i in range(1, 8)]
    everyone = near + sect_peers + in_peers + block_peers
    barrier = pltpu.get_barrier_semaphore()
    for peer in everyone:
        pl.semaphore_signal(barrier, inc=1, device_id=peer, device_id_type=MESH)

    q_now[...] = jnp.zeros_like(q_now)
    w_now[...] = jnp.zeros_like(w_now)
    small[...] = jnp.zeros_like(small)
    for c in range(6):
        q_now[c, 0:NODES, :] = fields[c]
        w_now[c, 0:NODES, :] = residual[c]

    def make_parts():
        for c in range(6):
            p1, p2, p3 = split3(q_now[c])
            for at, part in enumerate((p1, p2, p3, p1, p2)):
                q_parts[at * SPLIT_PAD : (at + 1) * SPLIT_PAD, c * ELEMS : (c + 1) * ELEMS] = part

    def make_trace():
        picked = dot(pick[...], q_parts[...])
        for c in range(6):
            for k in range(4):
                trace[c * FACE_PAD : (c + 1) * FACE_PAD, k * ELEMS : (k + 1) * ELEMS] = picked[
                    k * FACE_PAD : (k + 1) * FACE_PAD, c * ELEMS : (c + 1) * ELEMS
                ]
        high, low = split2(trace[...])
        trace_parts[0:96, :] = high
        trace_parts[96:192, :] = low

    def one_hot(target, index_row, rows, step):
        width = index_row.shape[1]

        def body(i, carry):
            at = pl.multiple_of(i * step, step)
            rows_at = lax.broadcasted_iota(jnp.int32, (step, width), 0) + i * step
            target[pl.ds(at, step), :] = jnp.where(rows_at == index_row, 1.0, 0.0).astype(BF16)
            return carry

        lax.fori_loop(0, rows // step, body, 0)

    make_parts()
    make_trace()
    one_hot(pick_out, send_list[...], FACES, 32)

    def copies(step):
        made = []
        for j, peer in enumerate(near):
            landing = 5 - j if j < 6 else 13 - j
            made.append(
                pltpu.make_async_remote_copy(
                    src_ref=send.at[step, j],
                    dst_ref=recv.at[step, landing],
                    send_sem=send_sem.at[step, j],
                    recv_sem=recv_sem.at[step, landing],
                    device_id=peer,
                    device_id_type=MESH,
                )
            )
        return made

    def gather_out(step):
        both = dot(trace_parts[...], pick_out[...])
        gathered = both[0:96] + both[96:192]
        for j in range(8):
            send[step, j] = gathered[:, j * SLOTS : (j + 1) * SLOTS]
        return gathered[:, 8 * SLOTS :]

    surface_0 = gather_out(0)
    pl.semaphore_wait(barrier, len(everyone))
    transfers_0 = copies(0)
    for copy in transfers_0:
        copy.start()

    for r in range(3):
        small[r * NODE_PAD : r * NODE_PAD + NODES, 0:NODES] = derivatives[r]
    main, rest = split2(small[0:128, :])
    volume_matrix[...] = (dot(main, place[0:128, :]) + dot(rest, place[128:256, :])).astype(BF16)
    small[0:128, :] = jnp.zeros((128, 128), F32)
    small[0:NODES, 0:60] = lift_matrix[...]
    main, rest = split2(small[0:SPLIT_PAD, :])
    lift_stack[...] = (dot(main, place_lift[0:128, :]) + dot(rest, place_lift[128:256, :])).astype(BF16)
    small[0:SPLIT_PAD, :] = jnp.zeros((SPLIT_PAD, 128), F32)

    one_hot(pick_in, face_source[...], 2 * FACES, 32)
    orient = jnp.broadcast_to(face_perm[...], (FACE_PAD, FACES))
    index = jnp.broadcast_to(node_table[:, 0:1], (FACE_PAD, FACES))
    for which in range(1, 6):
        index = jnp.where(orient == which, node_table[:, which : which + 1], index)
    node_index[...] = index

    normal_rows = jnp.concatenate(
        [jnp.concatenate([normals[m, k : k + 1, :] for k in range(4)], axis=1) for m in range(3)]
        + [jnp.zeros((5, FACES), F32)],
        axis=0,
    )
    high, low = split2(jnp.concatenate([normal_rows, normal_rows - normal_rows.astype(BF16).astype(F32)], axis=0))
    picked = dot(high, pick_out[:, 8 * SLOTS :])
    surface_normal = picked[0:8] + picked[8:16]

    def currents(gathered):
        e = [gathered[c * FACE_PAD : (c + 1) * FACE_PAD, :] for c in range(3)]
        h = [gathered[c * FACE_PAD : (c + 1) * FACE_PAD, :] for c in range(3, 6)]
        v = [surface_normal[m : m + 1, :] for m in range(3)]
        return cross(v, h) + [-x for x in cross(v, e)]

    currents_0 = currents(surface_0)

    polar, azimuth = angles[0:1, :], angles[1:2, :]
    direction = jnp.concatenate(
        [
            jnp.sin(polar) * jnp.cos(azimuth),
            jnp.sin(polar) * jnp.sin(azimuth),
            jnp.cos(polar),
            jnp.zeros((5, ANGLES), F32),
        ],
        axis=0,
    )
    d1, d2, d3 = [x.astype(F32) for x in split3(direction)]
    direction_parts = jnp.concatenate([d1, d2, d1, d3, d2, d1], axis=0).astype(BF16)
    points = jnp.concatenate([surface_points[...], jnp.zeros((5, POINTS), F32)], axis=0)
    p1, p2, p3 = [x.astype(F32) for x in split3(points)]
    point_parts[...] = jnp.concatenate([p1, p1, p2, p1, p2, p3], axis=0).T.astype(BF16)

    def table_block(n, carry):
        rows = pl.multiple_of(n * SLOTS, SLOTS)
        phase[...] = dot(point_parts[pl.ds(rows, SLOTS), :], direction_parts)

        def table_rows(i, inner):
            at = pl.multiple_of(i * 32, 32)
            turns = phase[pl.ds(at, 32), :]
            r = turns - jnp.round(turns)
            u = r * r
            s = u + SIN_MONIC[2]
            for order in range(1, -1, -1):
                s = s * u + SIN_MONIC[order]
            c = u + COS_MONIC[3]
            for order in range(2, -1, -1):
                c = c * u + COS_MONIC[order]
            s = s * r
            sine = s * c
            cosine = 1.0 / COS_GAIN - s * s
            out = pl.ds(pl.multiple_of(rows + at, 32), 32)
            high, low = split2(cosine)
            trig[0, out, :] = high
            trig[2, out, :] = low
            high, low = split2(sine)
            trig[1, out, :] = high
            trig[3, out, :] = low
            return inner

        return lax.fori_loop(0, SLOTS // 32, table_rows, carry)

    lax.fori_loop(0, FACE, table_block, 0)

    def local_part(step):
        slopes[...] = dot(volume_matrix[...], q_parts[...])
        both = dot(trace_parts[...], pick_in[0:FACES, :])
        column[...] = both[0:96] + both[96:192]

    local_part(0)

    def advance(step):
        for slot in range(8):
            arrived = recv[step, slot]
            if slot == 6:
                arrived = jnp.where(g > 0, arrived, 0.0)
            if slot == 7:
                arrived = jnp.where(g < 3, arrived, 0.0)
            high, low = split2(arrived)
            received_parts[0:96, slot * SLOTS : (slot + 1) * SLOTS] = high
            received_parts[96:192, slot * SLOTS : (slot + 1) * SLOTS] = low
        both = dot(received_parts[...], pick_in[FACES:, :])
        outer = column[...] + (both[0:96] + both[96:192])
        index = node_index[...]
        in_first = index < 8
        index = index & 7

        def turned(x):
            halves = []
            for half in (slice(0, 8), slice(8, 16)):
                first = jnp.take_along_axis(x[0:8], index[half], axis=0, mode="promise_in_bounds")
                second = jnp.take_along_axis(x[8:16], index[half], axis=0, mode="promise_in_bounds")
                halves.append(jnp.where(in_first[half], first, second))
            return jnp.concatenate(halves, axis=0)

        jump = []
        for c in range(6):
            rows = slice(c * FACE_PAD, (c + 1) * FACE_PAD)
            jump.append(trace[rows, :] - turned(outer[rows, :]))
        flux = [[] for _ in range(6)]
        for k in range(4):
            part = [x[:, k * ELEMS : (k + 1) * ELEMS] for x in jump]
            v = [normals[m, k : k + 1, :] for m in range(3)]
            half = 0.5 * face_scale[k : k + 1, :]
            e, h = part[:3], part[3:]
            e_dot = v[0] * e[0] + v[1] * e[1] + v[2] * e[2]
            h_dot = v[0] * h[0] + v[1] * h[1] + v[2] * h[2]
            ve, vh = cross(v, e), cross(v, h)
            for m in range(3):
                flux[m].append((vh[m] + e[m] - v[m] * e_dot) * half)
                flux[3 + m].append((h[m] - ve[m] - v[m] * h_dot) * half)
        flux_rows = jnp.concatenate([jnp.concatenate(x, axis=0) for x in flux], axis=1)
        f1, f2 = split2(flux_rows)
        lifted = dot(lift_stack[...], jnp.concatenate([f1, f2, f1], axis=0))

        def slope(r, c):
            return slopes[r * NODE_PAD : (r + 1) * NODE_PAD, c * ELEMS : (c + 1) * ELEMS]

        factors = [geometry[i : i + 1, :] for i in range(9)]

        def gradient(m, c):
            return factors[m] * slope(0, c) + factors[3 + m] * slope(1, c) + factors[6 + m] * slope(2, c)

        for c in range(6):
            other = 3 if c < 3 else 0
            a, b = (c + 1) % 3, (c + 2) % 3
            curl = gradient(a, other + b) - gradient(b, other + a)
            if c >= 3:
                curl = -curl
            rate = curl + lifted[0:NODE_PAD, c * ELEMS : (c + 1) * ELEMS]
            w_next = SECTION_A[step] * w_now[c] + TIME_STEP * rate
            q_next = q_now[c, 0:NODE_PAD, :] + SECTION_B[step] * w_next
            if step == 0:
                w_now[c] = w_next
                q_now[c, 0:NODE_PAD, :] = q_next
            else:
                fields_out[c] = q_next[0:NODES]
                residual_out[c] = w_next[0:NODES]

    for copy in transfers_0:
        copy.wait_recv()
    advance(0)

    make_parts()
    make_trace()
    surface_1 = gather_out(1)
    transfers_1 = copies(1)
    for copy in transfers_1:
        copy.start()
    currents_1 = currents(surface_1)

    turn = [ANGULAR_FREQUENCY * TIME_STEP * x for x in SECTION_C]
    weighted[...] = jnp.zeros_like(weighted)
    live = lax.broadcasted_iota(jnp.int32, (1, SLOTS), 1) < surface_count[...]
    node_weight = [
        jnp.where(live, surface_weights[:, n * SLOTS : (n + 1) * SLOTS], 0.0) for n in range(FACE)
    ]
    node_weight = jnp.concatenate(node_weight + [jnp.zeros((1, SLOTS), F32)], axis=0)
    for c in range(6):
        rows = slice(c * FACE_PAD, (c + 1) * FACE_PAD)
        real = math.cos(turn[0]) * currents_0[c] + math.cos(turn[1]) * currents_1[c]
        imag = math.sin(turn[0]) * currents_0[c] + math.sin(turn[1]) * currents_1[c]
        by_node[0, rows] = real * node_weight
        by_node[1, rows] = imag * -node_weight
    for n in range(FACE):
        at = slice(n * SLOTS, (n + 1) * SLOTS)
        real = by_node[0, pl.ds(n, 6, stride=FACE_PAD), :]
        imag = by_node[1, pl.ds(n, 6, stride=FACE_PAD), :]
        weighted[0, 0:6, at] = real * COS_GAIN
        weighted[0, 8:14, at] = imag * COS_GAIN
        weighted[1, 0:6, at] = imag * -SIN_GAIN
        weighted[1, 8:14, at] = real * SIN_GAIN
    far_rows = jnp.zeros((16, ANGLES), F32)
    for which in range(2):
        high, low = split2(weighted[which])
        fine = dot(jnp.concatenate([high, low], axis=0), trig[which])
        far_rows += fine[0:16] + fine[16:32] + dot(high, trig[2 + which])
    for j in range(4):
        for half in range(2):
            at = slice((2 * j + half) * SLOTS, (2 * j + half + 1) * SLOTS)
            far_part[j, half * 12 : half * 12 + 6] = far_rows[0:6, at]
            far_part[j, half * 12 + 6 : half * 12 + 12] = far_rows[8:14, at]

    def far_copies(stage, peers, source, landing):
        made = []
        for i, peer in enumerate(peers):
            made.append(
                pltpu.make_async_remote_copy(
                    src_ref=source(i),
                    dst_ref=landing(i),
                    send_sem=far_send_sem.at[stage, i],
                    recv_sem=far_recv_sem.at[stage, i],
                    device_id=peer,
                    device_id_type=MESH,
                )
            )
        for copy in made:
            copy.start()
        return made

    stage_a = far_copies(
        0, sect_peers, lambda i: far_part.at[sect_shift(i + 1)], lambda i: far_a.at[i]
    )
    local_part(1)
    for copy in stage_a:
        copy.wait_recv()
    far_b[place_in] = far_part[g] + far_a[0] + far_a[1] + far_a[2]
    stage_b = far_copies(1, in_peers, lambda i: far_b.at[place_in], lambda i: far_b.at[place_in])
    for copy in transfers_1:
        copy.wait_recv()
    advance(1)
    for copy in stage_b:
        copy.wait_recv()
    total = far_b[0]
    for i in range(1, 8):
        total = total + far_b[i]
    far_c[block] = total
    stage_c = far_copies(2, block_peers, lambda i: far_c.at[block], lambda i: far_c.at[block])
    for copy in transfers_0 + transfers_1 + stage_a + stage_b:
        copy.wait_send()
    for copy in stage_c:
        copy.wait()
    total = far_c[0]
    for i in range(1, 8):
        total = total + far_c[i]
    far_out[:, 0:SLOTS] = total[0:12]
    far_out[:, SLOTS:] = total[12:24]


def on_device(
    fields,
    residual,
    geometry,
    normals,
    face_scale,
    derivatives,
    lift_matrix,
    face_source,
    face_perm,
    send_cycle,
    send_layer,
    surface_faces,
    surface_count,
    surface_points,
    surface_weights,
    angles,
):
    pick, place, place_lift, node_table = constant_matrices()
    send_list = jnp.concatenate([send_cycle[0], send_layer[0], surface_faces[0]], axis=1)
    vmem = pl.BlockSpec(memory_space=pltpu.VMEM)
    fields_out, residual_out, far = pl.pallas_call(
        kernel,
        out_shape=(
            jax.ShapeDtypeStruct((6, NODES, ELEMS), F32),
            jax.ShapeDtypeStruct((6, NODES, ELEMS), F32),
            jax.ShapeDtypeStruct((12, ELEMS), F32),
        ),
        in_specs=[vmem] * 18,
        out_specs=(vmem, vmem, vmem),
        scratch_shapes=[
            pltpu.VMEM((6, SPLIT_PAD, ELEMS), F32),
            pltpu.VMEM((6, NODE_PAD, ELEMS), F32),
            pltpu.VMEM((5 * SPLIT_PAD, 6 * ELEMS), BF16),
            pltpu.VMEM((128, 128), F32),
            pltpu.VMEM((128, 5 * SPLIT_PAD), BF16),
            pltpu.VMEM((SPLIT_PAD, 192), BF16),
            pltpu.VMEM((96, FACES), F32),
            pltpu.VMEM((192, FACES), BF16),
            pltpu.VMEM((192, 8 * SLOTS), BF16),
            pltpu.VMEM((FACES, 9 * SLOTS), BF16),
            pltpu.VMEM((2 * FACES, FACES), BF16),
            pltpu.VMEM((FACE_PAD, FACES), jnp.int32),
            pltpu.VMEM((2, 8, 96, SLOTS), F32),
            pltpu.VMEM((2, 8, 96, SLOTS), F32),
            pltpu.VMEM((SLOTS, ANGLES), F32),
            pltpu.VMEM((4, POINTS, ANGLES), BF16),
            pltpu.VMEM((POINTS, 48), BF16),
            pltpu.VMEM((2, 96, SLOTS), F32),
            pltpu.VMEM((2, 16, POINTS), F32),
            pltpu.VMEM((128, 6 * ELEMS), F32),
            pltpu.VMEM((96, FACES), F32),
            pltpu.VMEM((4, 24, SLOTS), F32),
            pltpu.VMEM((3, 24, SLOTS), F32),
            pltpu.VMEM((8, 24, SLOTS), F32),
            pltpu.VMEM((8, 24, SLOTS), F32),
            pltpu.SemaphoreType.DMA((2, 8)),
            pltpu.SemaphoreType.DMA((2, 8)),
            pltpu.SemaphoreType.DMA((3, 7)),
            pltpu.SemaphoreType.DMA((3, 7)),
        ],
        compiler_params=pltpu.CompilerParams(
            collective_id=0, has_side_effects=True, vmem_limit_bytes=48 * 1024 * 1024
        ),
    )(
        fields[0, 0],
        residual[0, 0],
        geometry[0, 0],
        normals[0, 0],
        face_scale[0, 0],
        derivatives,
        lift_matrix,
        face_source[0],
        face_perm[0],
        send_list,
        surface_count,
        surface_points[0, 0],
        surface_weights[0],
        angles,
        pick,
        place,
        place_lift,
        node_table,
    )
    return (fields_out[None, None], residual_out[None, None], far)


def solution(mesh):
    in_specs = (
        P("dom", "sect", None, None, None),
        P("dom", "sect", None, None, None),
        P("dom", "sect", None, None),
        P("dom", "sect", None, None, None),
        P("dom", "sect", None, None),
        P(),
        P(),
        P("dom", "sect", None),
        P("dom", "sect", None),
        P("dom", "sect", None),
        P("dom", "sect", None),
        P("dom", "sect", None),
        P("dom", "sect"),
        P("dom", "sect", None, None),
        P("dom", "sect", None),
        P(),
    )
    out_specs = (
        P("dom", "sect", None, None, None),
        P("dom", "sect", None, None, None),
        P(None, "sect"),
    )
    return jax.shard_map(
        on_device, mesh=mesh, in_specs=in_specs, out_specs=out_specs, check_vma=False
    )
```

```python
import functools
import math

import jax
import jax.numpy as jnp
import numpy as np
from jax import lax
from jax.experimental import pallas as pl
from jax.experimental.pallas import tpu as pltpu
from jax.sharding import PartitionSpec as P

SECTION_A = (-0.4178904745, -1.192151694643)
SECTION_B = (0.3792103129999, 0.8229550293869)
SECTION_C = (0.1496590219993, 0.3704009573644)
TIME_STEP = 0.2
ANGULAR_FREQUENCY = 2.0 * math.pi
HOPS = 3
MESH = pl.DeviceIdType.MESH
FAR_FIRST = (0, 5, 1, 4, 6, 7, 2, 3)
F32 = jnp.float32
BF16 = jnp.bfloat16

NODES = 35
NODE_PAD = 40
SPLIT_PAD = 48
FACE = 15
FACE_PAD = 16
ELEMS = 256
FACES = 4 * ELEMS
SLOTS = 128
ANGLES = 1024
POINTS = FACE * SLOTS
TABLE_ROWS = 160

SIN_POLY = (4.442879676818848, -7.3078179359436035, 3.5977888107299805, -0.7912381887435913)
COS_POLY = (1.4142041206359863, -6.977642059326172, 5.715238571166992, -1.7283486127853394)
SIN_MONIC = tuple(x / SIN_POLY[-1] for x in SIN_POLY[:-1])
COS_MONIC = tuple(x / COS_POLY[-1] for x in COS_POLY[:-1])
COS_GAIN = SIN_POLY[-1] * SIN_POLY[-1]
SIN_GAIN = SIN_POLY[-1] * COS_POLY[-1]


def static_tables():
    node_list = []
    for i in range(5):
        for j in range(5 - i):
            for k in range(5 - i - j):
                node_list.append((i, j, k, 4 - i - j - k))
    face_nodes = []
    for which_face in range(4):
        face_nodes.append(
            [n for n, barycentric in enumerate(node_list) if barycentric[which_face] == 0]
        )
    reduced = [tuple((b for q, b in enumerate(node_list[n]) if q != 0)) for n in face_nodes[0]]
    orderings = [(0, 1, 2), (1, 2, 0), (2, 0, 1), (0, 2, 1), (2, 1, 0), (1, 0, 2)]
    permutation = [
        [reduced.index(tuple((triple[s] for s in ordering))) for triple in reduced]
        for ordering in orderings
    ]
    return (np.array(face_nodes, np.int32), np.array(permutation, np.int32))


def constant_matrices():
    face_nodes, node_table = static_tables()
    pick = np.zeros((64, 5 * SPLIT_PAD), np.float32)
    for k in range(4):
        for n in range(FACE):
            for part in range(3):
                pick[k * FACE_PAD + n, part * SPLIT_PAD + face_nodes[k][n]] = 1
    place = np.zeros((2, 128, 5 * SPLIT_PAD), np.float32)
    for i in range(NODES):
        for part in range(3):
            place[0, i, part * SPLIT_PAD + i] = 1
        for part in range(3, 5):
            place[1, i, part * SPLIT_PAD + i] = 1
    lift = np.zeros((2, 128, 192), np.float32)
    for k in range(4):
        for n in range(FACE):
            for part in range(3):
                lift[part // 2, k * FACE + n, part * 64 + k * FACE_PAD + n] = 1
    table = np.zeros((FACE_PAD, 8), np.int32)
    table[:FACE, :6] = node_table.T
    table[FACE, :] = FACE
    return (
        pick,
        place.reshape(256, -1),
        lift.reshape(256, -1),
        table,
    )


def dot(a, b, dims=((1,), (0,))):
    return lax.dot_general(a, b, (dims, ((), ())), preferred_element_type=F32)


def split2(x):
    high = x.astype(BF16)
    return high, (x - high.astype(F32)).astype(BF16)


def split3(x):
    high = x.astype(BF16)
    rest = x - high.astype(F32)
    middle = rest.astype(BF16)
    return high, middle, (rest - middle.astype(F32)).astype(BF16)


def cross(a, b):
    return [a[1] * b[2] - a[2] * b[1], a[2] * b[0] - a[0] * b[2], a[0] * b[1] - a[1] * b[0]]


def kernel(
    fields_in,
    residual_in,
    geometry_in,
    normals_in,
    face_scale_in,
    derivatives_in,
    lift_matrix_in,
    face_source_in,
    face_perm_in,
    send_cycle_in,
    send_layer_in,
    surface_faces_in,
    surface_count_in,
    surface_points_in,
    surface_weights_in,
    angles_in,
    pick_in_,
    place_in_,
    place_lift_in,
    node_table_in,
    fields_out,
    residual_out,
    far_out,
    q_now,
    w_now,
    fields,
    residual,
    geometry,
    normals,
    face_scale,
    derivatives,
    lift_matrix,
    face_source,
    face_perm,
    send_list,
    surface_count,
    surface_points,
    surface_weights,
    angles,
    pick,
    place,
    place_lift,
    node_table,
    q_parts,
    small,
    volume_matrix,
    lift_stack,
    trace,
    trace_parts,
    received_parts,
    pick_out,
    pick_in,
    node_index,
    send,
    recv,
    phase_even,
    phase_odd,
    trig,
    point_parts,
    by_node,
    weighted,
    slopes,
    column,
    far_part,
    far_a,
    far_b,
    far_c,
    load_sem,
    send_sem,
    recv_sem,
    far_send_sem,
    far_recv_sem,
):
    d = lax.axis_index("dom")
    g = lax.axis_index("sect")
    block, place_at = d // 8, d % 8

    def dom_shift(by):
        return lax.rem(d + 64 + by, 64)

    def sect_shift(by):
        return lax.rem(g + 4 + by, 4)

    offsets = list(range(-HOPS, 0)) + list(range(1, HOPS + 1))
    near = [(dom_shift(o), g) for o in offsets] + [(d, sect_shift(-1)), (d, sect_shift(1))]
    sect_peers = [(d, sect_shift(i)) for i in range(1, 4)]
    in_peers = [(block * 8 + lax.rem(place_at + i, 8), g) for i in range(1, 8)]
    block_peers = [(lax.rem(block + i, 8) * 8 + place_at, g) for i in range(1, 8)]
    everyone = near + sect_peers + in_peers + block_peers

    barrier = pltpu.get_barrier_semaphore()
    for peer in everyone:
        pl.semaphore_signal(barrier, inc=1, device_id=peer, device_id_type=MESH)

    def load(at, source, target):
        copy = pltpu.make_async_copy(source, target, load_sem.at[at])
        copy.start()
        return copy

    first = [
        load(0, fields_in.at[:, :, 0, :], fields),
        load(6, pick_in_, pick),
        load(7, send_cycle_in, send_list.at[:, 0 : 6 * SLOTS]),
        load(8, send_layer_in, send_list.at[:, 6 * SLOTS : 8 * SLOTS]),
        load(9, surface_faces_in, send_list.at[:, 8 * SLOTS :]),
    ]
    rest = [
        (residual_in.at[:, :, 0, :], residual),
        (geometry_in.at[:, 0, :], geometry),
        (normals_in, normals),
        (face_scale_in, face_scale),
        (derivatives_in, derivatives),
        (lift_matrix_in, lift_matrix),
        (face_source_in, face_source),
        (face_perm_in, face_perm),
        (surface_count_in, surface_count),
        (surface_points_in.at[:, 0, :], surface_points),
        (surface_weights_in, surface_weights),
        (angles_in, angles),
        (place_in_, place),
        (place_lift_in, place_lift),
        (node_table_in, node_table),
    ]
    q_now[:, 32:SPLIT_PAD, :] = jnp.zeros((6, SPLIT_PAD - 32, ELEMS), F32)
    w_now[:, 32:NODE_PAD, :] = jnp.zeros((6, NODE_PAD - 32, ELEMS), F32)

    def make_parts():
        for c in range(6):
            p1, p2, p3 = split3(q_now[c])
            for at, part in enumerate((p1, p2, p3, p1, p2)):
                q_parts[at * SPLIT_PAD : (at + 1) * SPLIT_PAD, c * ELEMS : (c + 1) * ELEMS] = part

    def make_trace():
        picked = dot(pick[...].astype(BF16), q_parts[...])
        for c in range(6):
            for k in range(4):
                trace[c * FACE_PAD : (c + 1) * FACE_PAD, k * ELEMS : (k + 1) * ELEMS] = picked[
                    k * FACE_PAD : (k + 1) * FACE_PAD, c * ELEMS : (c + 1) * ELEMS
                ]
        high, low = split2(trace[...])
        trace_parts[0:96, :] = high
        trace_parts[96:192, :] = low

    def one_hot(target, index_row, rows):
        width = index_row.shape[1]
        row_of = lax.broadcasted_iota(jnp.int32, (SLOTS, width), 0).astype(F32).astype(BF16)

        def body(i, carry):
            at = pl.multiple_of(i * SLOTS, SLOTS)
            wanted = (index_row - i * SLOTS).astype(F32).astype(BF16)
            target[pl.ds(at, SLOTS), :] = jnp.where(row_of == wanted, BF16(1), BF16(0))
            return carry

        lax.fori_loop(0, rows // SLOTS, body, 0)

    later = [load(10 + i, *pair) for i, pair in enumerate(rest)]
    for copy in first[1:]:
        copy.wait()
    one_hot(pick_out, send_list[...], FACES)
    first[0].wait()
    for c in range(6):
        q_now[c, 0:NODES, :] = fields[c]
    make_parts()
    make_trace()

    def copies(step):
        made = []
        for j, peer in enumerate(near):
            landing = 5 - j if j < 6 else 13 - j
            made.append(
                pltpu.make_async_remote_copy(
                    src_ref=send.at[step, j],
                    dst_ref=recv.at[step, landing],
                    send_sem=send_sem.at[step, j],
                    recv_sem=recv_sem.at[step, landing],
                    device_id=peer,
                    device_id_type=MESH,
                )
            )
        return made

    def gather_out(step):
        both = dot(trace_parts[...], pick_out[...])
        gathered = both[0:96] + both[96:192]
        for j in range(8):
            send[step, j] = gathered[:, j * SLOTS : (j + 1) * SLOTS]
        return gathered[:, 8 * SLOTS :]

    surface_0 = gather_out(0)
    pl.semaphore_wait(barrier, len(everyone))
    transfers_0 = copies(0)
    for j in FAR_FIRST:
        transfers_0[j].start()

    small[...] = jnp.zeros_like(small)
    for copy in later:
        copy.wait()
    for c in range(6):
        w_now[c, 0:NODES, :] = residual[c]
    for r in range(3):
        small[r * NODE_PAD : r * NODE_PAD + NODES, 0:NODES] = derivatives[r]
    main, rest = split2(small[0:128, :])
    volume_matrix[...] = (
        dot(main, place[0:128, :].astype(BF16)) + dot(rest, place[128:256, :].astype(BF16))
    ).astype(BF16)
    small[0:128, :] = jnp.zeros((128, 128), F32)
    small[0:NODES, 0:60] = lift_matrix[...]
    main, rest = split2(small[0:SPLIT_PAD, :])
    lift_stack[...] = (
        dot(main, place_lift[0:128, :].astype(BF16)) + dot(rest, place_lift[128:256, :].astype(BF16))
    ).astype(BF16)
    small[0:SPLIT_PAD, :] = jnp.zeros((SPLIT_PAD, 128), F32)

    one_hot(pick_in, face_source[...], 2 * FACES)
    orient = jnp.broadcast_to(face_perm[...], (FACE_PAD, FACES))
    index = jnp.broadcast_to(node_table[:, 0:1], (FACE_PAD, FACES))
    for which in range(1, 6):
        index = jnp.where(orient == which, node_table[:, which : which + 1], index)
    node_index[...] = index

    normal_rows = jnp.concatenate(
        [jnp.concatenate([normals[m, k : k + 1, :] for k in range(4)], axis=1) for m in range(3)]
        + [jnp.zeros((5, FACES), F32)],
        axis=0,
    )
    high, low = split2(jnp.concatenate([normal_rows, normal_rows - normal_rows.astype(BF16).astype(F32)], axis=0))
    picked = dot(high, pick_out[:, 8 * SLOTS :])
    surface_normal = picked[0:8] + picked[8:16]

    def currents(gathered):
        e = [gathered[c * FACE_PAD : (c + 1) * FACE_PAD, :] for c in range(3)]
        h = [gathered[c * FACE_PAD : (c + 1) * FACE_PAD, :] for c in range(3, 6)]
        v = [surface_normal[m : m + 1, :] for m in range(3)]
        return cross(v, h) + [-x for x in cross(v, e)]

    currents_0 = currents(surface_0)

    polar, azimuth = angles[0:1, :], angles[1:2, :]
    direction = jnp.concatenate(
        [
            jnp.sin(polar) * jnp.cos(azimuth),
            jnp.sin(polar) * jnp.sin(azimuth),
            jnp.cos(polar),
            jnp.zeros((5, ANGLES), F32),
        ],
        axis=0,
    )
    d1, d2, d3 = [x.astype(F32) for x in split3(direction)]
    direction_parts = jnp.concatenate([d1, d2, d1, d3, d2, d1], axis=0).astype(BF16)
    points = jnp.concatenate([surface_points[...], jnp.zeros((5, POINTS), F32)], axis=0)
    p1, p2, p3 = [x.astype(F32) for x in split3(points)]
    point_parts[...] = jnp.concatenate([p1, p1, p2, p1, p2, p3], axis=0).T.astype(BF16)

    def find_phases(target, chunk):
        at = pl.multiple_of(chunk * TABLE_ROWS, TABLE_ROWS)
        target[...] = dot(point_parts[pl.ds(at, TABLE_ROWS), :], direction_parts)

    def fill_table(phases, chunk):
        for first_row in range(0, TABLE_ROWS, 32):
            turns = phases[first_row : first_row + 32, :]
            r = turns - jnp.round(turns)
            u = r * r
            s = u + SIN_MONIC[2]
            c = u + COS_MONIC[2]
            for order in range(1, -1, -1):
                s = s * u + SIN_MONIC[order]
                c = c * u + COS_MONIC[order]
            s = s * r
            sine = s * c
            cosine = 1.0 / COS_GAIN - s * s
            out = pl.ds(pl.multiple_of(chunk * TABLE_ROWS + first_row, 32), 32)
            high, low = split2(cosine)
            trig[0, out, :] = high
            trig[2, out, :] = low
            high, low = split2(sine)
            trig[1, out, :] = high
            trig[3, out, :] = low

    find_phases(phase_even, 0)

    def table_pair(i, carry):
        find_phases(phase_odd, 2 * i + 1)
        fill_table(phase_even, 2 * i)
        find_phases(phase_even, lax.rem(2 * i + 2, POINTS // TABLE_ROWS))
        fill_table(phase_odd, 2 * i + 1)
        return carry

    lax.fori_loop(0, POINTS // TABLE_ROWS // 2, table_pair, 0)

    def local_part(step):
        slopes[...] = dot(volume_matrix[...], q_parts[...])
        both = dot(trace_parts[...], pick_in[0:FACES, :])
        column[...] = both[0:96] + both[96:192]

    local_part(0)

    def advance(step):
        for slot in range(8):
            arrived = recv[step, slot]
            if slot == 6:
                arrived = jnp.where(g > 0, arrived, 0.0)
            if slot == 7:
                arrived = jnp.where(g < 3, arrived, 0.0)
            high, low = split2(arrived)
            received_parts[0:96, slot * SLOTS : (slot + 1) * SLOTS] = high
            received_parts[96:192, slot * SLOTS : (slot + 1) * SLOTS] = low
        both = dot(received_parts[...], pick_in[FACES:, :])
        outer = column[...] + (both[0:96] + both[96:192])
        index = node_index[...]
        in_first = index < 8
        index = index & 7

        def turned(x):
            halves = []
            for half in (slice(0, 8), slice(8, 16)):
                first = jnp.take_along_axis(x[0:8], index[half], axis=0, mode="promise_in_bounds")
                second = jnp.take_along_axis(x[8:16], index[half], axis=0, mode="promise_in_bounds")
                halves.append(jnp.where(in_first[half], first, second))
            return jnp.concatenate(halves, axis=0)

        jump = []
        for c in range(6):
            rows = slice(c * FACE_PAD, (c + 1) * FACE_PAD)
            jump.append(trace[rows, :] - turned(outer[rows, :]))
        flux = [[] for _ in range(6)]
        for k in range(4):
            part = [x[:, k * ELEMS : (k + 1) * ELEMS] for x in jump]
            v = [normals[m, k : k + 1, :] for m in range(3)]
            half = 0.5 * face_scale[k : k + 1, :]
            e, h = part[:3], part[3:]
            e_dot = v[0] * e[0] + v[1] * e[1] + v[2] * e[2]
            h_dot = v[0] * h[0] + v[1] * h[1] + v[2] * h[2]
            ve, vh = cross(v, e), cross(v, h)
            for m in range(3):
                flux[m].append((vh[m] + e[m] - v[m] * e_dot) * half)
                flux[3 + m].append((h[m] - ve[m] - v[m] * h_dot) * half)
        flux_rows = jnp.concatenate([jnp.concatenate(x, axis=0) for x in flux], axis=1)
        f1, f2 = split2(flux_rows)
        lifted = dot(lift_stack[...], jnp.concatenate([f1, f2, f1], axis=0))

        def slope(r, c):
            return slopes[r * NODE_PAD : (r + 1) * NODE_PAD, c * ELEMS : (c + 1) * ELEMS]

        factors = [geometry[i : i + 1, :] for i in range(9)]

        def gradient(m, c):
            return factors[m] * slope(0, c) + factors[3 + m] * slope(1, c) + factors[6 + m] * slope(2, c)

        for c in range(6):
            other = 3 if c < 3 else 0
            a, b = (c + 1) % 3, (c + 2) % 3
            curl = gradient(a, other + b) - gradient(b, other + a)
            if c >= 3:
                curl = -curl
            rate = curl + lifted[0:NODE_PAD, c * ELEMS : (c + 1) * ELEMS]
            w_next = SECTION_A[step] * w_now[c] + TIME_STEP * rate
            q_next = q_now[c, 0:NODE_PAD, :] + SECTION_B[step] * w_next
            if step == 0:
                w_now[c] = w_next
                q_now[c, 0:NODE_PAD, :] = q_next
            else:
                fields[c] = q_next[0:NODES]
                residual[c] = w_next[0:NODES]

    for copy in transfers_0:
        copy.wait_recv()
    advance(0)

    make_parts()
    make_trace()
    surface_1 = gather_out(1)
    transfers_1 = copies(1)
    for j in FAR_FIRST:
        transfers_1[j].start()
    currents_1 = currents(surface_1)

    turn = [ANGULAR_FREQUENCY * TIME_STEP * x for x in SECTION_C]
    weighted[...] = jnp.zeros_like(weighted)
    live = lax.broadcasted_iota(jnp.int32, (1, SLOTS), 1) < surface_count[...]
    node_weight = [
        jnp.where(live, surface_weights[:, n * SLOTS : (n + 1) * SLOTS], 0.0) for n in range(FACE)
    ]
    node_weight = jnp.concatenate(node_weight + [jnp.zeros((1, SLOTS), F32)], axis=0)
    for c in range(6):
        rows = slice(c * FACE_PAD, (c + 1) * FACE_PAD)
        real = math.cos(turn[0]) * currents_0[c] + math.cos(turn[1]) * currents_1[c]
        imag = math.sin(turn[0]) * currents_0[c] + math.sin(turn[1]) * currents_1[c]
        by_node[0, rows] = real * node_weight
        by_node[1, rows] = imag * -node_weight
    for n in range(FACE):
        at = slice(n * SLOTS, (n + 1) * SLOTS)
        real = by_node[0, pl.ds(n, 6, stride=FACE_PAD), :]
        imag = by_node[1, pl.ds(n, 6, stride=FACE_PAD), :]
        weighted[0, 0:6, at] = real * COS_GAIN
        weighted[0, 8:14, at] = imag * COS_GAIN
        weighted[1, 0:6, at] = imag * -SIN_GAIN
        weighted[1, 8:14, at] = real * SIN_GAIN
    far_rows = jnp.zeros((16, ANGLES), F32)
    for which in range(2):
        high, low = split2(weighted[which])
        fine = dot(jnp.concatenate([high, low], axis=0), trig[which])
        far_rows += fine[0:16] + fine[16:32] + dot(high, trig[2 + which])
    for j in range(4):
        for half in range(2):
            at = slice((2 * j + half) * SLOTS, (2 * j + half + 1) * SLOTS)
            far_part[j, half * 12 : half * 12 + 6] = far_rows[0:6, at]
            far_part[j, half * 12 + 6 : half * 12 + 12] = far_rows[8:14, at]

    def far_copies(stage, peers, source, landing):
        made = []
        for i, peer in enumerate(peers):
            made.append(
                pltpu.make_async_remote_copy(
                    src_ref=source(i),
                    dst_ref=landing(i),
                    send_sem=far_send_sem.at[stage, i],
                    recv_sem=far_recv_sem.at[stage, i],
                    device_id=peer,
                    device_id_type=MESH,
                )
            )
        for copy in made:
            copy.start()
        return made

    stage_a = far_copies(
        0, sect_peers, lambda i: far_part.at[sect_shift(i + 1)], lambda i: far_a.at[i]
    )
    local_part(1)
    for copy in stage_a:
        copy.wait_recv()
    far_b[place_at] = far_part[g] + far_a[0] + far_a[1] + far_a[2]
    stage_b = far_copies(1, in_peers, lambda i: far_b.at[place_at], lambda i: far_b.at[place_at])
    for copy in transfers_1:
        copy.wait_recv()
    advance(1)
    stores = [load(0, fields, fields_out), load(10, residual, residual_out)]
    for copy in stage_b:
        copy.wait_recv()
    total = far_b[0]
    for i in range(1, 8):
        total = total + far_b[i]
    far_c[block] = total
    stage_c = far_copies(2, block_peers, lambda i: far_c.at[block], lambda i: far_c.at[block])
    for copy in transfers_0 + transfers_1 + stage_a + stage_b:
        copy.wait_send()
    for copy in stores:
        copy.wait()
    for copy in stage_c:
        copy.wait()
    total = far_c[0]
    for i in range(1, 8):
        total = total + far_c[i]
    far_out[:, 0:SLOTS] = total[0:12]
    far_out[:, SLOTS:] = total[12:24]


def hand_over(fields, residual, far, fields_out, residual_out, far_out, sem):
    pairs = [
        (fields, fields_out.at[:, :, 0, :]),
        (residual, residual_out.at[:, :, 0, :]),
        (far, far_out),
    ]
    copies = [pltpu.make_async_copy(a, b, sem.at[i]) for i, (a, b) in enumerate(pairs)]
    for copy in copies:
        copy.start()
    for copy in copies:
        copy.wait()


def on_device(
    fields,
    residual,
    geometry,
    normals,
    face_scale,
    derivatives,
    lift_matrix,
    face_source,
    face_perm,
    send_cycle,
    send_layer,
    surface_faces,
    surface_count,
    surface_points,
    surface_weights,
    angles,
):
    pick, place, place_lift, node_table = constant_matrices()
    hbm = pl.BlockSpec(memory_space=pltpu.HBM)
    vmem = pl.BlockSpec(memory_space=pltpu.VMEM)
    fields_out, residual_out, far = pl.pallas_call(
        kernel,
        out_shape=(
            jax.ShapeDtypeStruct((6, NODES, ELEMS), F32),
            jax.ShapeDtypeStruct((6, NODES, ELEMS), F32),
            jax.ShapeDtypeStruct((12, ELEMS), F32),
        ),
        in_specs=[hbm] * 20,
        out_specs=(hbm, hbm, vmem),
        scratch_shapes=[
            pltpu.VMEM((6, SPLIT_PAD, ELEMS), F32),
            pltpu.VMEM((6, NODE_PAD, ELEMS), F32),
            pltpu.VMEM((6, NODES, ELEMS), F32),
            pltpu.VMEM((6, NODES, ELEMS), F32),
            pltpu.VMEM((9, ELEMS), F32),
            pltpu.VMEM((3, 4, ELEMS), F32),
            pltpu.VMEM((4, ELEMS), F32),
            pltpu.VMEM((3, NODES, NODES), F32),
            pltpu.VMEM((NODES, 60), F32),
            pltpu.VMEM((1, FACES), jnp.int32),
            pltpu.VMEM((1, FACES), jnp.int32),
            pltpu.VMEM((1, 9 * SLOTS), jnp.int32),
            pltpu.VMEM((1, 1), jnp.int32),
            pltpu.VMEM((3, POINTS), F32),
            pltpu.VMEM((1, POINTS), F32),
            pltpu.VMEM((2, ANGLES), F32),
            pltpu.VMEM((64, 5 * SPLIT_PAD), F32),
            pltpu.VMEM((256, 5 * SPLIT_PAD), F32),
            pltpu.VMEM((256, 192), F32),
            pltpu.VMEM((FACE_PAD, 8), jnp.int32),
            pltpu.VMEM((5 * SPLIT_PAD, 6 * ELEMS), BF16),
            pltpu.VMEM((128, 128), F32),
            pltpu.VMEM((128, 5 * SPLIT_PAD), BF16),
            pltpu.VMEM((SPLIT_PAD, 192), BF16),
            pltpu.VMEM((96, FACES), F32),
            pltpu.VMEM((192, FACES), BF16),
            pltpu.VMEM((192, 8 * SLOTS), BF16),
            pltpu.VMEM((FACES, 9 * SLOTS), BF16),
            pltpu.VMEM((2 * FACES, FACES), BF16),
            pltpu.VMEM((FACE_PAD, FACES), jnp.int32),
            pltpu.VMEM((2, 8, 96, SLOTS), F32),
            pltpu.VMEM((2, 8, 96, SLOTS), F32),
            pltpu.VMEM((TABLE_ROWS, ANGLES), F32),
            pltpu.VMEM((TABLE_ROWS, ANGLES), F32),
            pltpu.VMEM((4, POINTS, ANGLES), BF16),
            pltpu.VMEM((POINTS, 48), BF16),
            pltpu.VMEM((2, 96, SLOTS), F32),
            pltpu.VMEM((2, 16, POINTS), F32),
            pltpu.VMEM((128, 6 * ELEMS), F32),
            pltpu.VMEM((96, FACES), F32),
            pltpu.VMEM((4, 24, SLOTS), F32),
            pltpu.VMEM((3, 24, SLOTS), F32),
            pltpu.VMEM((8, 24, SLOTS), F32),
            pltpu.VMEM((8, 24, SLOTS), F32),
            pltpu.SemaphoreType.DMA((30,)),
            pltpu.SemaphoreType.DMA((2, 8)),
            pltpu.SemaphoreType.DMA((2, 8)),
            pltpu.SemaphoreType.DMA((3, 7)),
            pltpu.SemaphoreType.DMA((3, 7)),
        ],
        compiler_params=pltpu.CompilerParams(
            collective_id=0, has_side_effects=True, vmem_limit_bytes=63 * 1024 * 1024
        ),
    )(
        fields[0].transpose(1, 2, 0, 3),
        residual[0].transpose(1, 2, 0, 3),
        geometry[0].transpose(1, 0, 2),
        normals[0, 0],
        face_scale[0, 0],
        derivatives,
        lift_matrix,
        face_source[0],
        face_perm[0],
        send_cycle[0],
        send_layer[0],
        surface_faces[0],
        surface_count,
        surface_points[0].transpose(1, 0, 2),
        surface_weights[0],
        angles,
        pick,
        place,
        place_lift,
        node_table,
    )
    fields_out, residual_out, far = pl.pallas_call(
        hand_over,
        out_shape=(
            jax.ShapeDtypeStruct((6, NODES, 1, ELEMS), F32),
            jax.ShapeDtypeStruct((6, NODES, 1, ELEMS), F32),
            jax.ShapeDtypeStruct((12, ELEMS), F32),
        ),
        in_specs=[vmem] * 3,
        out_specs=(hbm, hbm, hbm),
        scratch_shapes=[pltpu.SemaphoreType.DMA((3,))],
    )(fields_out, residual_out, far)
    return (fields_out.transpose(2, 0, 1, 3)[None], residual_out.transpose(2, 0, 1, 3)[None], far)


def solution(mesh):
    in_specs = (
        P("dom", "sect", None, None, None),
        P("dom", "sect", None, None, None),
        P("dom", "sect", None, None),
        P("dom", "sect", None, None, None),
        P("dom", "sect", None, None),
        P(),
        P(),
        P("dom", "sect", None),
        P("dom", "sect", None),
        P("dom", "sect", None),
        P("dom", "sect", None),
        P("dom", "sect", None),
        P("dom", "sect"),
        P("dom", "sect", None, None),
        P("dom", "sect", None),
        P(),
    )
    out_specs = (
        P("dom", "sect", None, None, None),
        P("dom", "sect", None, None, None),
        P(None, "sect"),
    )
    return jax.shard_map(
        on_device, mesh=mesh, in_specs=in_specs, out_specs=out_specs, check_vma=False
    )
```

```python
import functools
import math

import jax
import jax.numpy as jnp
import numpy as np
from jax import lax
from jax.experimental import pallas as pl
from jax.experimental.pallas import tpu as pltpu
from jax.sharding import PartitionSpec as P

SECTION_A = (-0.4178904745, -1.192151694643)
SECTION_B = (0.3792103129999, 0.8229550293869)
SECTION_C = (0.1496590219993, 0.3704009573644)
TIME_STEP = 0.2
ANGULAR_FREQUENCY = 2.0 * math.pi
HOPS = 3
MESH = pl.DeviceIdType.MESH
FAR_FIRST = (0, 5, 1, 4, 6, 7, 2, 3)
F32 = jnp.float32
BF16 = jnp.bfloat16

NODES = 35
NODE_PAD = 40
SPLIT_PAD = 48
FACE = 15
FACE_PAD = 16
ELEMS = 256
FACES = 4 * ELEMS
SLOTS = 128
ANGLES = 1024
POINTS = FACE * SLOTS
TABLE_ROWS = 320
PAIR_ROWS = 2 * TABLE_ROWS
SECTOR = 256

SIN_POLY = (4.442879676818848, -7.3078179359436035, 3.5977888107299805, -0.7912381887435913)
COS_POLY = (1.4142041206359863, -6.977642059326172, 5.715238571166992, -1.7283486127853394)
SIN_MONIC = tuple(x / SIN_POLY[-1] for x in SIN_POLY[:-1])
COS_MONIC = tuple(x / COS_POLY[-1] for x in COS_POLY[:-1])
COS_GAIN = SIN_POLY[-1] * SIN_POLY[-1]
SIN_GAIN = SIN_POLY[-1] * COS_POLY[-1]


def static_tables():
    node_list = []
    for i in range(5):
        for j in range(5 - i):
            for k in range(5 - i - j):
                node_list.append((i, j, k, 4 - i - j - k))
    face_nodes = []
    for which_face in range(4):
        face_nodes.append(
            [n for n, barycentric in enumerate(node_list) if barycentric[which_face] == 0]
        )
    reduced = [tuple((b for q, b in enumerate(node_list[n]) if q != 0)) for n in face_nodes[0]]
    orderings = [(0, 1, 2), (1, 2, 0), (2, 0, 1), (0, 2, 1), (2, 1, 0), (1, 0, 2)]
    permutation = [
        [reduced.index(tuple((triple[s] for s in ordering))) for triple in reduced]
        for ordering in orderings
    ]
    return (np.array(face_nodes, np.int32), np.array(permutation, np.int32))


def constant_matrices():
    face_nodes, node_table = static_tables()
    pick = np.zeros((64, 5 * SPLIT_PAD), np.float32)
    for k in range(4):
        for n in range(FACE):
            for part in range(3):
                pick[k * FACE_PAD + n, part * SPLIT_PAD + face_nodes[k][n]] = 1
    place = np.zeros((2, 128, 5 * SPLIT_PAD), np.float32)
    for i in range(NODES):
        for part in range(3):
            place[0, i, part * SPLIT_PAD + i] = 1
        for part in range(3, 5):
            place[1, i, part * SPLIT_PAD + i] = 1
    lift = np.zeros((2, 128, 192), np.float32)
    for k in range(4):
        for n in range(FACE):
            for part in range(3):
                lift[part // 2, k * FACE + n, part * 64 + k * FACE_PAD + n] = 1
    table = np.zeros((FACE_PAD, 8), np.int32)
    table[:FACE, :6] = node_table.T
    table[FACE, :] = FACE
    return (
        pick,
        place.reshape(256, -1),
        lift.reshape(256, -1),
        table,
    )


def dot(a, b, dims=((1,), (0,))):
    return lax.dot_general(a, b, (dims, ((), ())), preferred_element_type=F32)


def split2(x):
    high = x.astype(BF16)
    return high, (x - high.astype(F32)).astype(BF16)


def split3(x):
    high = x.astype(BF16)
    rest = x - high.astype(F32)
    middle = rest.astype(BF16)
    return high, middle, (rest - middle.astype(F32)).astype(BF16)


def cross(a, b):
    return [a[1] * b[2] - a[2] * b[1], a[2] * b[0] - a[0] * b[2], a[0] * b[1] - a[1] * b[0]]


def kernel(
    fields_in,
    residual_in,
    geometry_in,
    normals_in,
    face_scale_in,
    derivatives_in,
    lift_matrix_in,
    face_source_in,
    face_perm_in,
    send_cycle_in,
    send_layer_in,
    surface_faces_in,
    surface_count_in,
    surface_points_in,
    surface_weights_in,
    angles_in,
    pick_in_,
    place_in_,
    place_lift_in,
    node_table_in,
    fields_out,
    residual_out,
    far_out,
    q_now,
    w_now,
    fields,
    residual,
    geometry,
    normals,
    face_scale,
    derivatives,
    lift_matrix,
    face_source,
    face_perm,
    send_list,
    surface_count,
    surface_points,
    surface_weights,
    angles,
    pick,
    place,
    place_lift,
    node_table,
    q_parts,
    small,
    volume_matrix,
    lift_stack,
    trace,
    trace_parts,
    received_parts,
    pick_out,
    pick_in,
    node_index,
    send,
    recv,
    phase_even,
    phase_odd,
    table_0,
    table_1,
    table_2,
    table_3,
    point_parts,
    direction_parts,
    by_node,
    weighted,
    weighted_parts,
    far_rows,
    slopes,
    column,
    far_part,
    far_a,
    far_b,
    far_c,
    load_sem,
    send_sem,
    recv_sem,
    far_send_sem,
    far_recv_sem,
):
    d = lax.axis_index("dom")
    g = lax.axis_index("sect")
    block, place_at = d // 8, d % 8

    def dom_shift(by):
        return lax.rem(d + 64 + by, 64)

    def sect_shift(by):
        return lax.rem(g + 4 + by, 4)

    offsets = list(range(-HOPS, 0)) + list(range(1, HOPS + 1))
    near = [(dom_shift(o), g) for o in offsets] + [(d, sect_shift(-1)), (d, sect_shift(1))]
    sect_peers = [(d, sect_shift(i)) for i in range(1, 4)]
    in_peers = [(block * 8 + lax.rem(place_at + i, 8), g) for i in range(1, 8)]
    block_peers = [(lax.rem(block + i, 8) * 8 + place_at, g) for i in range(1, 8)]
    everyone = near + sect_peers + in_peers + block_peers

    barrier = pltpu.get_barrier_semaphore()
    for peer in everyone:
        pl.semaphore_signal(barrier, inc=1, device_id=peer, device_id_type=MESH)

    def load(at, source, target):
        copy = pltpu.make_async_copy(source, target, load_sem.at[at])
        copy.start()
        return copy

    first = [
        load(0, fields_in.at[:, :, 0, :], fields),
        load(6, pick_in_, pick),
        load(7, send_cycle_in, send_list.at[:, 0 : 6 * SLOTS]),
        load(8, send_layer_in, send_list.at[:, 6 * SLOTS : 8 * SLOTS]),
        load(9, surface_faces_in, send_list.at[:, 8 * SLOTS :]),
    ]
    rest = [
        (residual_in.at[:, :, 0, :], residual),
        (geometry_in.at[:, 0, :], geometry),
        (normals_in, normals),
        (face_scale_in, face_scale),
        (derivatives_in, derivatives),
        (lift_matrix_in, lift_matrix),
        (face_source_in, face_source),
        (face_perm_in, face_perm),
        (surface_count_in, surface_count),
        (surface_points_in.at[:, 0, :], surface_points),
        (surface_weights_in, surface_weights),
        (angles_in, angles),
        (place_in_, place),
        (place_lift_in, place_lift),
        (node_table_in, node_table),
    ]
    q_now[:, 32:SPLIT_PAD, :] = jnp.zeros((6, SPLIT_PAD - 32, ELEMS), F32)
    w_now[:, 32:NODE_PAD, :] = jnp.zeros((6, NODE_PAD - 32, ELEMS), F32)

    def make_parts():
        for c in range(6):
            p1, p2, p3 = split3(q_now[c])
            for at, part in enumerate((p1, p2, p3, p1, p2)):
                q_parts[at * SPLIT_PAD : (at + 1) * SPLIT_PAD, c * ELEMS : (c + 1) * ELEMS] = part

    def make_trace():
        picked = dot(pick[...].astype(BF16), q_parts[...])
        for c in range(6):
            for k in range(4):
                trace[c * FACE_PAD : (c + 1) * FACE_PAD, k * ELEMS : (k + 1) * ELEMS] = picked[
                    k * FACE_PAD : (k + 1) * FACE_PAD, c * ELEMS : (c + 1) * ELEMS
                ]
        high, low = split2(trace[...])
        trace_parts[0:96, :] = high
        trace_parts[96:192, :] = low

    def one_hot(target, index_row, rows):
        width = index_row.shape[1]
        row_of = lax.broadcasted_iota(jnp.int32, (SLOTS, width), 0).astype(F32).astype(BF16)

        def body(i, carry):
            at = pl.multiple_of(i * SLOTS, SLOTS)
            wanted = (index_row - i * SLOTS).astype(F32).astype(BF16)
            target[pl.ds(at, SLOTS), :] = jnp.where(row_of == wanted, BF16(1), BF16(0))
            return carry

        lax.fori_loop(0, rows // SLOTS, body, 0)

    later = [load(10 + i, *pair) for i, pair in enumerate(rest)]
    for copy in first[1:]:
        copy.wait()
    one_hot(pick_out, send_list[...], FACES)
    first[0].wait()
    for c in range(6):
        q_now[c, 0:NODES, :] = fields[c]
    make_parts()
    make_trace()

    def copies(step):
        made = []
        for j, peer in enumerate(near):
            landing = 5 - j if j < 6 else 13 - j
            made.append(
                pltpu.make_async_remote_copy(
                    src_ref=send.at[step, j],
                    dst_ref=recv.at[step, landing],
                    send_sem=send_sem.at[step, j],
                    recv_sem=recv_sem.at[step, landing],
                    device_id=peer,
                    device_id_type=MESH,
                )
            )
        return made

    def gather_out(step):
        both = dot(trace_parts[...], pick_out[...])
        gathered = both[0:96] + both[96:192]
        for j in range(8):
            send[step, j] = gathered[:, j * SLOTS : (j + 1) * SLOTS]
        return gathered[:, 8 * SLOTS :]

    surface_0 = gather_out(0)
    pl.semaphore_wait(barrier, len(everyone))
    transfers_0 = copies(0)
    for j in FAR_FIRST:
        transfers_0[j].start()

    small[...] = jnp.zeros_like(small)
    for copy in later:
        copy.wait()
    for c in range(6):
        w_now[c, 0:NODES, :] = residual[c]
    for r in range(3):
        small[r * NODE_PAD : r * NODE_PAD + NODES, 0:NODES] = derivatives[r]
    main, rest = split2(small[0:128, :])
    volume_matrix[...] = (
        dot(main, place[0:128, :].astype(BF16)) + dot(rest, place[128:256, :].astype(BF16))
    ).astype(BF16)
    small[0:128, :] = jnp.zeros((128, 128), F32)
    small[0:NODES, 0:60] = lift_matrix[...]
    main, rest = split2(small[0:SPLIT_PAD, :])
    lift_stack[...] = (
        dot(main, place_lift[0:128, :].astype(BF16)) + dot(rest, place_lift[128:256, :].astype(BF16))
    ).astype(BF16)
    small[0:SPLIT_PAD, :] = jnp.zeros((SPLIT_PAD, 128), F32)

    one_hot(pick_in, face_source[...], 2 * FACES)
    orient = jnp.broadcast_to(face_perm[...], (FACE_PAD, FACES))
    index = jnp.broadcast_to(node_table[:, 0:1], (FACE_PAD, FACES))
    for which in range(1, 6):
        index = jnp.where(orient == which, node_table[:, which : which + 1], index)
    node_index[...] = index

    normal_rows = jnp.concatenate(
        [jnp.concatenate([normals[m, k : k + 1, :] for k in range(4)], axis=1) for m in range(3)]
        + [jnp.zeros((5, FACES), F32)],
        axis=0,
    )
    high, low = split2(jnp.concatenate([normal_rows, normal_rows - normal_rows.astype(BF16).astype(F32)], axis=0))
    picked = dot(high, pick_out[:, 8 * SLOTS :])
    surface_normal = picked[0:8] + picked[8:16]

    def currents(gathered):
        e = [gathered[c * FACE_PAD : (c + 1) * FACE_PAD, :] for c in range(3)]
        h = [gathered[c * FACE_PAD : (c + 1) * FACE_PAD, :] for c in range(3, 6)]
        v = [surface_normal[m : m + 1, :] for m in range(3)]
        return cross(v, h) + [-x for x in cross(v, e)]

    currents_0 = currents(surface_0)

    polar, azimuth = angles[0:1, :], angles[1:2, :]
    direction = jnp.concatenate(
        [
            jnp.sin(polar) * jnp.cos(azimuth),
            jnp.sin(polar) * jnp.sin(azimuth),
            jnp.cos(polar),
            jnp.zeros((5, ANGLES), F32),
        ],
        axis=0,
    )
    d1, d2, d3 = [x.astype(F32) for x in split3(direction)]
    direction_parts[...] = jnp.concatenate([d1, d2, d1, d3, d2, d1], axis=0).astype(BF16)
    points = jnp.concatenate([surface_points[...], jnp.zeros((5, POINTS), F32)], axis=0)
    p1, p2, p3 = [x.astype(F32) for x in split3(points)]
    point_parts[...] = jnp.concatenate([p1, p1, p2, p1, p2, p3], axis=0).T.astype(BF16)

    tables = (table_0, table_1, table_2, table_3)

    def fill_table(nth, beside=None):
        table = tables[nth]
        sector = pl.ds(pl.multiple_of(sect_shift(nth + 1) * SECTOR, SECTOR), SECTOR)

        def find_phases(target, chunk):
            at = pl.multiple_of(chunk * TABLE_ROWS, TABLE_ROWS)
            target[...] = dot(point_parts[pl.ds(at, TABLE_ROWS), :], direction_parts[:, sector])

        def fill(phases, chunk):
            for first_row in range(0, TABLE_ROWS, 80):
                turns = phases[first_row : first_row + 80, :]
                r = turns - jnp.round(turns)
                u = r * r
                s = u + SIN_MONIC[2]
                c = u + COS_MONIC[2]
                for order in range(1, -1, -1):
                    s = s * u + SIN_MONIC[order]
                    c = c * u + COS_MONIC[order]
                s = s * r
                sine = s * c
                cosine = 1.0 / COS_GAIN - s * s
                out = pl.ds(pl.multiple_of(chunk * TABLE_ROWS + first_row, 80), 80)
                high, low = split2(cosine)
                table[0, out, :] = high
                table[2, out, :] = low
                high, low = split2(sine)
                table[1, out, :] = high
                table[3, out, :] = low

        find_phases(phase_even, 0)

        def pair(i, carry):
            find_phases(phase_odd, 2 * i + 1)
            fill(phase_even, 2 * i)
            find_phases(phase_even, lax.rem(2 * i + 2, POINTS // TABLE_ROWS))
            fill(phase_odd, 2 * i + 1)
            if beside is not None:
                beside(i)
            return carry

        lax.fori_loop(0, POINTS // PAIR_ROWS, pair, 0)

    fill_table(0)
    fill_table(1)

    def local_part(step):
        slopes[...] = dot(volume_matrix[...], q_parts[...])
        both = dot(trace_parts[...], pick_in[0:FACES, :])
        column[...] = both[0:96] + both[96:192]

    local_part(0)

    def advance(step):
        for slot in range(8):
            arrived = recv[step, slot]
            if slot == 6:
                arrived = jnp.where(g > 0, arrived, 0.0)
            if slot == 7:
                arrived = jnp.where(g < 3, arrived, 0.0)
            high, low = split2(arrived)
            received_parts[0:96, slot * SLOTS : (slot + 1) * SLOTS] = high
            received_parts[96:192, slot * SLOTS : (slot + 1) * SLOTS] = low
        both = dot(received_parts[...], pick_in[FACES:, :])
        outer = column[...] + (both[0:96] + both[96:192])
        index = node_index[...]
        in_first = index < 8
        index = index & 7

        def turned(x):
            halves = []
            for half in (slice(0, 8), slice(8, 16)):
                first = jnp.take_along_axis(x[0:8], index[half], axis=0, mode="promise_in_bounds")
                second = jnp.take_along_axis(x[8:16], index[half], axis=0, mode="promise_in_bounds")
                halves.append(jnp.where(in_first[half], first, second))
            return jnp.concatenate(halves, axis=0)

        jump = []
        for c in range(6):
            rows = slice(c * FACE_PAD, (c + 1) * FACE_PAD)
            jump.append(trace[rows, :] - turned(outer[rows, :]))
        flux = [[] for _ in range(6)]
        for k in range(4):
            part = [x[:, k * ELEMS : (k + 1) * ELEMS] for x in jump]
            v = [normals[m, k : k + 1, :] for m in range(3)]
            half = 0.5 * face_scale[k : k + 1, :]
            e, h = part[:3], part[3:]
            e_dot = v[0] * e[0] + v[1] * e[1] + v[2] * e[2]
            h_dot = v[0] * h[0] + v[1] * h[1] + v[2] * h[2]
            ve, vh = cross(v, e), cross(v, h)
            for m in range(3):
                flux[m].append((vh[m] + e[m] - v[m] * e_dot) * half)
                flux[3 + m].append((h[m] - ve[m] - v[m] * h_dot) * half)
        flux_rows = jnp.concatenate([jnp.concatenate(x, axis=0) for x in flux], axis=1)
        f1, f2 = split2(flux_rows)
        lifted = dot(lift_stack[...], jnp.concatenate([f1, f2, f1], axis=0))

        def slope(r, c):
            return slopes[r * NODE_PAD : (r + 1) * NODE_PAD, c * ELEMS : (c + 1) * ELEMS]

        factors = [geometry[i : i + 1, :] for i in range(9)]

        def gradient(m, c):
            return factors[m] * slope(0, c) + factors[3 + m] * slope(1, c) + factors[6 + m] * slope(2, c)

        for c in range(6):
            other = 3 if c < 3 else 0
            a, b = (c + 1) % 3, (c + 2) % 3
            curl = gradient(a, other + b) - gradient(b, other + a)
            if c >= 3:
                curl = -curl
            rate = curl + lifted[0:NODE_PAD, c * ELEMS : (c + 1) * ELEMS]
            w_next = SECTION_A[step] * w_now[c] + TIME_STEP * rate
            q_next = q_now[c, 0:NODE_PAD, :] + SECTION_B[step] * w_next
            if step == 0:
                w_now[c] = w_next
                q_now[c, 0:NODE_PAD, :] = q_next
            else:
                fields[c] = q_next[0:NODES]
                residual[c] = w_next[0:NODES]

    for copy in transfers_0:
        copy.wait_recv()
    advance(0)

    make_parts()
    make_trace()
    surface_1 = gather_out(1)
    transfers_1 = copies(1)
    for j in FAR_FIRST:
        transfers_1[j].start()
    currents_1 = currents(surface_1)

    turn = [ANGULAR_FREQUENCY * TIME_STEP * x for x in SECTION_C]
    weighted[...] = jnp.zeros_like(weighted)
    live = lax.broadcasted_iota(jnp.int32, (1, SLOTS), 1) < surface_count[...]
    node_weight = [
        jnp.where(live, surface_weights[:, n * SLOTS : (n + 1) * SLOTS], 0.0) for n in range(FACE)
    ]
    node_weight = jnp.concatenate(node_weight + [jnp.zeros((1, SLOTS), F32)], axis=0)
    for c in range(6):
        rows = slice(c * FACE_PAD, (c + 1) * FACE_PAD)
        real = math.cos(turn[0]) * currents_0[c] + math.cos(turn[1]) * currents_1[c]
        imag = math.sin(turn[0]) * currents_0[c] + math.sin(turn[1]) * currents_1[c]
        by_node[0, rows] = real * node_weight
        by_node[1, rows] = imag * -node_weight
    for n in range(FACE):
        at = slice(n * SLOTS, (n + 1) * SLOTS)
        real = by_node[0, pl.ds(n, 6, stride=FACE_PAD), :]
        imag = by_node[1, pl.ds(n, 6, stride=FACE_PAD), :]
        weighted[0, 0:6, at] = real * COS_GAIN
        weighted[0, 8:14, at] = imag * COS_GAIN
        weighted[1, 0:6, at] = imag * -SIN_GAIN
        weighted[1, 8:14, at] = real * SIN_GAIN
    for which in range(2):
        high, low = split2(weighted[which])
        weighted_parts[which, 0:16, :] = high
        weighted_parts[which, 16:32, :] = low
    far_rows[...] = jnp.zeros_like(far_rows)

    def project(nth, first_row, rows):
        table = tables[nth]
        total = far_rows[nth]
        for which in range(2):
            weights = weighted_parts[which, :, pl.ds(first_row, rows)]
            fine = dot(weights, table[which, pl.ds(first_row, rows), :])
            rest = dot(weights[0:16], table[2 + which, pl.ds(first_row, rows), :])
            total += fine[0:16] + fine[16:32] + rest
        far_rows[nth] = total

    def pack(nth):
        for half in range(2):
            at = slice(half * SLOTS, (half + 1) * SLOTS)
            far_part[nth, half * 12 : half * 12 + 6] = far_rows[nth, 0:6, at]
            far_part[nth, half * 12 + 6 : half * 12 + 12] = far_rows[nth, 8:14, at]

    def far_copy(stage, i, peer, source, target):
        copy = pltpu.make_async_remote_copy(
            src_ref=source,
            dst_ref=target,
            send_sem=far_send_sem.at[stage, i],
            recv_sem=far_recv_sem.at[stage, i],
            device_id=peer,
            device_id_type=MESH,
        )
        copy.start()
        return copy

    def project_two(i):
        at = pl.multiple_of(i * PAIR_ROWS, PAIR_ROWS)
        project(0, at, PAIR_ROWS)
        project(1, at, PAIR_ROWS)

    fill_table(2, project_two)
    stage_a = []
    for nth in range(3):
        if nth == 2:
            project(2, 0, POINTS)
        pack(nth)
        stage_a.append(far_copy(0, nth, sect_peers[nth], far_part.at[nth], far_a.at[nth]))
    fill_table(3)
    project(3, 0, POINTS)
    pack(3)

    local_part(1)
    for copy in stage_a:
        copy.wait_recv()
    far_b[place_at] = far_part[3] + far_a[0] + far_a[1] + far_a[2]
    stage_b = [
        far_copy(1, i, peer, far_b.at[place_at], far_b.at[place_at])
        for i, peer in enumerate(in_peers)
    ]
    for copy in transfers_1:
        copy.wait_recv()
    advance(1)
    stores = [load(0, fields, fields_out), load(10, residual, residual_out)]
    for copy in stage_b:
        copy.wait_recv()
    total = far_b[0]
    for i in range(1, 8):
        total = total + far_b[i]
    far_c[block] = total
    stage_c = [
        far_copy(2, i, peer, far_c.at[block], far_c.at[block]) for i, peer in enumerate(block_peers)
    ]
    for copy in transfers_0 + transfers_1 + stage_a + stage_b:
        copy.wait_send()
    for copy in stores:
        copy.wait()
    for copy in stage_c:
        copy.wait()
    total = far_c[0]
    for i in range(1, 8):
        total = total + far_c[i]
    far_out[:, 0:SLOTS] = total[0:12]
    far_out[:, SLOTS:] = total[12:24]


def hand_over(fields, residual, far, fields_out, residual_out, far_out, sem):
    pairs = [
        (fields, fields_out.at[:, :, 0, :]),
        (residual, residual_out.at[:, :, 0, :]),
        (far, far_out),
    ]
    copies = [pltpu.make_async_copy(a, b, sem.at[i]) for i, (a, b) in enumerate(pairs)]
    for copy in copies:
        copy.start()
    for copy in copies:
        copy.wait()


def on_device(
    fields,
    residual,
    geometry,
    normals,
    face_scale,
    derivatives,
    lift_matrix,
    face_source,
    face_perm,
    send_cycle,
    send_layer,
    surface_faces,
    surface_count,
    surface_points,
    surface_weights,
    angles,
):
    pick, place, place_lift, node_table = constant_matrices()
    hbm = pl.BlockSpec(memory_space=pltpu.HBM)
    vmem = pl.BlockSpec(memory_space=pltpu.VMEM)
    fields_out, residual_out, far = pl.pallas_call(
        kernel,
        out_shape=(
            jax.ShapeDtypeStruct((6, NODES, ELEMS), F32),
            jax.ShapeDtypeStruct((6, NODES, ELEMS), F32),
            jax.ShapeDtypeStruct((12, ELEMS), F32),
        ),
        in_specs=[hbm] * 20,
        out_specs=(hbm, hbm, vmem),
        scratch_shapes=[
            pltpu.VMEM((6, SPLIT_PAD, ELEMS), F32),
            pltpu.VMEM((6, NODE_PAD, ELEMS), F32),
            pltpu.VMEM((6, NODES, ELEMS), F32),
            pltpu.VMEM((6, NODES, ELEMS), F32),
            pltpu.VMEM((9, ELEMS), F32),
            pltpu.VMEM((3, 4, ELEMS), F32),
            pltpu.VMEM((4, ELEMS), F32),
            pltpu.VMEM((3, NODES, NODES), F32),
            pltpu.VMEM((NODES, 60), F32),
            pltpu.VMEM((1, FACES), jnp.int32),
            pltpu.VMEM((1, FACES), jnp.int32),
            pltpu.VMEM((1, 9 * SLOTS), jnp.int32),
            pltpu.VMEM((1, 1), jnp.int32),
            pltpu.VMEM((3, POINTS), F32),
            pltpu.VMEM((1, POINTS), F32),
            pltpu.VMEM((2, ANGLES), F32),
            pltpu.VMEM((64, 5 * SPLIT_PAD), F32),
            pltpu.VMEM((256, 5 * SPLIT_PAD), F32),
            pltpu.VMEM((256, 192), F32),
            pltpu.VMEM((FACE_PAD, 8), jnp.int32),
            pltpu.VMEM((5 * SPLIT_PAD, 6 * ELEMS), BF16),
            pltpu.VMEM((128, 128), F32),
            pltpu.VMEM((128, 5 * SPLIT_PAD), BF16),
            pltpu.VMEM((SPLIT_PAD, 192), BF16),
            pltpu.VMEM((96, FACES), F32),
            pltpu.VMEM((192, FACES), BF16),
            pltpu.VMEM((192, 8 * SLOTS), BF16),
            pltpu.VMEM((FACES, 9 * SLOTS), BF16),
            pltpu.VMEM((2 * FACES, FACES), BF16),
            pltpu.VMEM((FACE_PAD, FACES), jnp.int32),
            pltpu.VMEM((2, 8, 96, SLOTS), F32),
            pltpu.VMEM((2, 8, 96, SLOTS), F32),
            pltpu.VMEM((TABLE_ROWS, SECTOR), F32),
            pltpu.VMEM((TABLE_ROWS, SECTOR), F32),
            pltpu.VMEM((4, POINTS, SECTOR), BF16),
            pltpu.VMEM((4, POINTS, SECTOR), BF16),
            pltpu.VMEM((4, POINTS, SECTOR), BF16),
            pltpu.VMEM((4, POINTS, SECTOR), BF16),
            pltpu.VMEM((POINTS, 48), BF16),
            pltpu.VMEM((48, ANGLES), BF16),
            pltpu.VMEM((2, 96, SLOTS), F32),
            pltpu.VMEM((2, 16, POINTS), F32),
            pltpu.VMEM((2, 32, POINTS), BF16),
            pltpu.VMEM((4, 16, SECTOR), F32),
            pltpu.VMEM((128, 6 * ELEMS), F32),
            pltpu.VMEM((96, FACES), F32),
            pltpu.VMEM((4, 24, SLOTS), F32),
            pltpu.VMEM((3, 24, SLOTS), F32),
            pltpu.VMEM((8, 24, SLOTS), F32),
            pltpu.VMEM((8, 24, SLOTS), F32),
            pltpu.SemaphoreType.DMA((30,)),
            pltpu.SemaphoreType.DMA((2, 8)),
            pltpu.SemaphoreType.DMA((2, 8)),
            pltpu.SemaphoreType.DMA((3, 7)),
            pltpu.SemaphoreType.DMA((3, 7)),
        ],
        compiler_params=pltpu.CompilerParams(
            collective_id=0, has_side_effects=True, vmem_limit_bytes=63 * 1024 * 1024
        ),
    )(
        fields[0].transpose(1, 2, 0, 3),
        residual[0].transpose(1, 2, 0, 3),
        geometry[0].transpose(1, 0, 2),
        normals[0, 0],
        face_scale[0, 0],
        derivatives,
        lift_matrix,
        face_source[0],
        face_perm[0],
        send_cycle[0],
        send_layer[0],
        surface_faces[0],
        surface_count,
        surface_points[0].transpose(1, 0, 2),
        surface_weights[0],
        angles,
        pick,
        place,
        place_lift,
        node_table,
    )
    fields_out, residual_out, far = pl.pallas_call(
        hand_over,
        out_shape=(
            jax.ShapeDtypeStruct((6, NODES, 1, ELEMS), F32),
            jax.ShapeDtypeStruct((6, NODES, 1, ELEMS), F32),
            jax.ShapeDtypeStruct((12, ELEMS), F32),
        ),
        in_specs=[vmem] * 3,
        out_specs=(hbm, hbm, hbm),
        scratch_shapes=[pltpu.SemaphoreType.DMA((3,))],
    )(fields_out, residual_out, far)
    return (fields_out.transpose(2, 0, 1, 3)[None], residual_out.transpose(2, 0, 1, 3)[None], far)


def solution(mesh):
    in_specs = (
        P("dom", "sect", None, None, None),
        P("dom", "sect", None, None, None),
        P("dom", "sect", None, None),
        P("dom", "sect", None, None, None),
        P("dom", "sect", None, None),
        P(),
        P(),
        P("dom", "sect", None),
        P("dom", "sect", None),
        P("dom", "sect", None),
        P("dom", "sect", None),
        P("dom", "sect", None),
        P("dom", "sect"),
        P("dom", "sect", None, None),
        P("dom", "sect", None),
        P(),
    )
    out_specs = (
        P("dom", "sect", None, None, None),
        P("dom", "sect", None, None, None),
        P(None, "sect"),
    )
    return jax.shard_map(
        on_device, mesh=mesh, in_specs=in_specs, out_specs=out_specs, check_vma=False
    )
```

```python
import functools
import math

import jax
import jax.numpy as jnp
import numpy as np
from jax import lax
from jax.experimental import pallas as pl
from jax.experimental.pallas import tpu as pltpu
from jax.sharding import PartitionSpec as P

SECTION_A = (-0.4178904745, -1.192151694643)
SECTION_B = (0.3792103129999, 0.8229550293869)
SECTION_C = (0.1496590219993, 0.3704009573644)
TIME_STEP = 0.2
ANGULAR_FREQUENCY = 2.0 * math.pi
HOPS = 3
MESH = pl.DeviceIdType.MESH
FAR_FIRST = (0, 5, 1, 4, 6, 7, 2, 3)
F32 = jnp.float32
BF16 = jnp.bfloat16

NODES = 35
NODE_PAD = 40
SPLIT_PAD = 48
FACE = 15
FACE_PAD = 16
ELEMS = 256
FACES = 4 * ELEMS
SLOTS = 128
ANGLES = 1024
POINTS = FACE * SLOTS
TABLE_ROWS = 320
PAIR_ROWS = 2 * TABLE_ROWS
SECTOR = 256

SIN_POLY = (4.442879676818848, -7.3078179359436035, 3.5977888107299805, -0.7912381887435913)
COS_POLY = (1.4142041206359863, -6.977642059326172, 5.715238571166992, -1.7283486127853394)
SIN_MONIC = tuple(x / SIN_POLY[-1] for x in SIN_POLY[:-1])
COS_MONIC = tuple(x / COS_POLY[-1] for x in COS_POLY[:-1])
COS_GAIN = SIN_POLY[-1] * SIN_POLY[-1]
SIN_GAIN = SIN_POLY[-1] * COS_POLY[-1]


def static_tables():
    node_list = []
    for i in range(5):
        for j in range(5 - i):
            for k in range(5 - i - j):
                node_list.append((i, j, k, 4 - i - j - k))
    face_nodes = []
    for which_face in range(4):
        face_nodes.append(
            [n for n, barycentric in enumerate(node_list) if barycentric[which_face] == 0]
        )
    reduced = [tuple((b for q, b in enumerate(node_list[n]) if q != 0)) for n in face_nodes[0]]
    orderings = [(0, 1, 2), (1, 2, 0), (2, 0, 1), (0, 2, 1), (2, 1, 0), (1, 0, 2)]
    permutation = [
        [reduced.index(tuple((triple[s] for s in ordering))) for triple in reduced]
        for ordering in orderings
    ]
    return (np.array(face_nodes, np.int32), np.array(permutation, np.int32))


def constant_matrices():
    face_nodes, node_table = static_tables()
    pick = np.zeros((64, 5 * SPLIT_PAD), np.float32)
    for k in range(4):
        for n in range(FACE):
            for part in range(3):
                pick[k * FACE_PAD + n, part * SPLIT_PAD + face_nodes[k][n]] = 1
    place = np.zeros((2, 128, 5 * SPLIT_PAD), np.float32)
    for i in range(NODES):
        for part in range(3):
            place[0, i, part * SPLIT_PAD + i] = 1
        for part in range(3, 5):
            place[1, i, part * SPLIT_PAD + i] = 1
    lift = np.zeros((2, 128, 192), np.float32)
    for k in range(4):
        for n in range(FACE):
            for part in range(3):
                lift[part // 2, k * FACE + n, part * 64 + k * FACE_PAD + n] = 1
    table = np.zeros((FACE_PAD, 8), np.int32)
    table[:FACE, :6] = node_table.T
    table[FACE, :] = FACE
    return (
        pick,
        place.reshape(256, -1),
        lift.reshape(256, -1),
        table,
    )


def dot(a, b, dims=((1,), (0,))):
    return lax.dot_general(a, b, (dims, ((), ())), preferred_element_type=F32)


def split2(x):
    high = x.astype(BF16)
    return high, (x - high.astype(F32)).astype(BF16)


def split3(x):
    high = x.astype(BF16)
    rest = x - high.astype(F32)
    middle = rest.astype(BF16)
    return high, middle, (rest - middle.astype(F32)).astype(BF16)


def cross(a, b):
    return [a[1] * b[2] - a[2] * b[1], a[2] * b[0] - a[0] * b[2], a[0] * b[1] - a[1] * b[0]]


def kernel(
    fields_in,
    residual_in,
    geometry_in,
    normals_in,
    face_scale_in,
    derivatives_in,
    lift_matrix_in,
    face_source_in,
    face_perm_in,
    send_cycle_in,
    send_layer_in,
    surface_faces_in,
    surface_count_in,
    surface_points_in,
    surface_weights_in,
    angles_in,
    pick_in_,
    place_in_,
    place_lift_in,
    node_table_in,
    fields_out,
    residual_out,
    far_out,
    q_now,
    w_now,
    fields,
    residual,
    geometry,
    normals,
    face_scale,
    derivatives,
    lift_matrix,
    face_source,
    face_perm,
    send_list,
    surface_count,
    surface_points,
    surface_weights,
    angles,
    pick,
    place,
    place_lift,
    node_table,
    q_parts,
    small,
    volume_matrix,
    lift_stack,
    trace,
    trace_parts,
    received_parts,
    pick_out,
    pick_in,
    node_index,
    send,
    recv,
    phase_even,
    phase_odd,
    table_0,
    table_1,
    table_2,
    table_3,
    point_parts,
    direction_parts,
    by_node,
    weighted,
    weighted_parts,
    far_rows,
    slopes,
    column,
    far_part,
    far_a,
    far_b,
    far_c,
    load_sem,
    send_sem,
    recv_sem,
    far_send_sem,
    far_recv_sem,
):
    d = lax.axis_index("dom")
    g = lax.axis_index("sect")
    block, place_at = d // 8, d % 8

    def dom_shift(by):
        return lax.rem(d + 64 + by, 64)

    def sect_shift(by):
        return lax.rem(g + 4 + by, 4)

    offsets = list(range(-HOPS, 0)) + list(range(1, HOPS + 1))
    near = [(dom_shift(o), g) for o in offsets] + [(d, sect_shift(-1)), (d, sect_shift(1))]
    sect_peers = [(d, sect_shift(i)) for i in range(1, 4)]
    in_peers = [(block * 8 + lax.rem(place_at + i, 8), g) for i in range(1, 8)]
    block_peers = [(lax.rem(block + i, 8) * 8 + place_at, g) for i in range(1, 8)]
    everyone = near + sect_peers + in_peers + block_peers

    barrier = pltpu.get_barrier_semaphore()
    for peer in everyone:
        pl.semaphore_signal(barrier, inc=1, device_id=peer, device_id_type=MESH)

    def load(at, source, target):
        copy = pltpu.make_async_copy(source, target, load_sem.at[at])
        copy.start()
        return copy

    first = [
        load(0, fields_in.at[:, :, 0, :], fields),
        load(6, pick_in_, pick),
        load(7, send_cycle_in, send_list.at[:, 0 : 6 * SLOTS]),
        load(8, send_layer_in, send_list.at[:, 6 * SLOTS : 8 * SLOTS]),
        load(9, surface_faces_in, send_list.at[:, 8 * SLOTS :]),
    ]
    rest = [
        (residual_in.at[:, :, 0, :], residual),
        (geometry_in.at[:, 0, :], geometry),
        (normals_in, normals),
        (face_scale_in, face_scale),
        (derivatives_in, derivatives),
        (lift_matrix_in, lift_matrix),
        (face_source_in, face_source),
        (face_perm_in, face_perm),
        (surface_count_in, surface_count),
        (surface_points_in.at[:, 0, :], surface_points),
        (surface_weights_in, surface_weights),
        (angles_in, angles),
        (place_in_, place),
        (place_lift_in, place_lift),
        (node_table_in, node_table),
    ]
    q_now[:, 32:SPLIT_PAD, :] = jnp.zeros((6, SPLIT_PAD - 32, ELEMS), F32)
    w_now[:, 32:NODE_PAD, :] = jnp.zeros((6, NODE_PAD - 32, ELEMS), F32)

    def make_parts():
        for c in range(6):
            p1, p2, p3 = split3(q_now[c])
            for at, part in enumerate((p1, p2, p3, p1, p2)):
                q_parts[at * SPLIT_PAD : (at + 1) * SPLIT_PAD, c * ELEMS : (c + 1) * ELEMS] = part

    def make_trace():
        picked = dot(pick[...].astype(BF16), q_parts[...])
        for c in range(6):
            for k in range(4):
                trace[c * FACE_PAD : (c + 1) * FACE_PAD, k * ELEMS : (k + 1) * ELEMS] = picked[
                    k * FACE_PAD : (k + 1) * FACE_PAD, c * ELEMS : (c + 1) * ELEMS
                ]
        high, low = split2(trace[...])
        trace_parts[0:96, :] = high
        trace_parts[96:192, :] = low

    def one_hot(target, index_row, rows):
        width = index_row.shape[1]
        row_of = lax.broadcasted_iota(jnp.int32, (SLOTS, width), 0).astype(F32).astype(BF16)

        def body(i, carry):
            at = pl.multiple_of(i * SLOTS, SLOTS)
            wanted = (index_row - i * SLOTS).astype(F32).astype(BF16)
            target[pl.ds(at, SLOTS), :] = jnp.where(row_of == wanted, BF16(1), BF16(0))
            return carry

        lax.fori_loop(0, rows // SLOTS, body, 0)

    later = [load(10 + i, *pair) for i, pair in enumerate(rest)]
    for copy in first[1:]:
        copy.wait()
    one_hot(pick_out, send_list[...], FACES)
    first[0].wait()
    for c in range(6):
        q_now[c, 0:NODES, :] = fields[c]
    make_parts()
    make_trace()

    def copies(step):
        made = []
        for j, peer in enumerate(near):
            landing = 5 - j if j < 6 else 13 - j
            made.append(
                pltpu.make_async_remote_copy(
                    src_ref=send.at[step, j],
                    dst_ref=recv.at[step, landing],
                    send_sem=send_sem.at[step, j],
                    recv_sem=recv_sem.at[step, landing],
                    device_id=peer,
                    device_id_type=MESH,
                )
            )
        return made

    def gather_out(step):
        both = dot(trace_parts[...], pick_out[...])
        gathered = both[0:96] + both[96:192]
        for j in range(8):
            send[step, j] = gathered[:, j * SLOTS : (j + 1) * SLOTS]
        return gathered[:, 8 * SLOTS :]

    surface_0 = gather_out(0)
    pl.semaphore_wait(barrier, len(everyone))
    transfers_0 = copies(0)
    for j in FAR_FIRST:
        transfers_0[j].start()

    small[...] = jnp.zeros_like(small)
    for copy in later:
        copy.wait()
    for c in range(6):
        w_now[c, 0:NODES, :] = residual[c]
    for r in range(3):
        small[r * NODE_PAD : r * NODE_PAD + NODES, 0:NODES] = derivatives[r]
    main, rest = split2(small[0:128, :])
    volume_matrix[...] = (
        dot(main, place[0:128, :].astype(BF16)) + dot(rest, place[128:256, :].astype(BF16))
    ).astype(BF16)
    small[0:128, :] = jnp.zeros((128, 128), F32)
    small[0:NODES, 0:60] = lift_matrix[...]
    main, rest = split2(small[0:SPLIT_PAD, :])
    lift_stack[...] = (
        dot(main, place_lift[0:128, :].astype(BF16)) + dot(rest, place_lift[128:256, :].astype(BF16))
    ).astype(BF16)
    small[0:SPLIT_PAD, :] = jnp.zeros((SPLIT_PAD, 128), F32)

    one_hot(pick_in, face_source[...], 2 * FACES)
    orient = jnp.broadcast_to(face_perm[...], (FACE_PAD, FACES))
    index = jnp.broadcast_to(node_table[:, 0:1], (FACE_PAD, FACES))
    for which in range(1, 6):
        index = jnp.where(orient == which, node_table[:, which : which + 1], index)
    node_index[...] = index

    normal_rows = jnp.concatenate(
        [jnp.concatenate([normals[m, k : k + 1, :] for k in range(4)], axis=1) for m in range(3)]
        + [jnp.zeros((5, FACES), F32)],
        axis=0,
    )
    high, low = split2(jnp.concatenate([normal_rows, normal_rows - normal_rows.astype(BF16).astype(F32)], axis=0))
    picked = dot(high, pick_out[:, 8 * SLOTS :])
    surface_normal = picked[0:8] + picked[8:16]

    def currents(gathered):
        e = [gathered[c * FACE_PAD : (c + 1) * FACE_PAD, :] for c in range(3)]
        h = [gathered[c * FACE_PAD : (c + 1) * FACE_PAD, :] for c in range(3, 6)]
        v = [surface_normal[m : m + 1, :] for m in range(3)]
        return cross(v, h) + [-x for x in cross(v, e)]

    currents_0 = currents(surface_0)

    polar, azimuth = angles[0:1, :], angles[1:2, :]
    direction = jnp.concatenate(
        [
            jnp.sin(polar) * jnp.cos(azimuth),
            jnp.sin(polar) * jnp.sin(azimuth),
            jnp.cos(polar),
            jnp.zeros((5, ANGLES), F32),
        ],
        axis=0,
    )
    d1, d2, d3 = [x.astype(F32) for x in split3(direction)]
    direction_parts[...] = jnp.concatenate([d1, d2, d1, d3, d2, d1], axis=0).astype(BF16)
    points = jnp.concatenate([surface_points[...], jnp.zeros((5, POINTS), F32)], axis=0)
    p1, p2, p3 = [x.astype(F32) for x in split3(points)]
    point_parts[...] = jnp.concatenate([p1, p1, p2, p1, p2, p3], axis=0).T.astype(BF16)

    tables = (table_0, table_1, table_2, table_3)

    def fill_table(nth, beside=None):
        table = tables[nth]
        sector = pl.ds(pl.multiple_of(sect_shift(nth + 1) * SECTOR, SECTOR), SECTOR)

        def find_phases(target, chunk):
            at = pl.multiple_of(chunk * TABLE_ROWS, TABLE_ROWS)
            target[...] = dot(point_parts[pl.ds(at, TABLE_ROWS), :], direction_parts[:, sector])

        def fill(phases, chunk):
            for first_row in range(0, TABLE_ROWS, 80):
                turns = phases[first_row : first_row + 80, :]
                r = turns - jnp.round(turns)
                u = r * r
                s = u + SIN_MONIC[2]
                c = u + COS_MONIC[2]
                for order in range(1, -1, -1):
                    s = s * u + SIN_MONIC[order]
                    c = c * u + COS_MONIC[order]
                s = s * r
                sine = s * c
                cosine = 1.0 / COS_GAIN - s * s
                out = pl.ds(pl.multiple_of(chunk * TABLE_ROWS + first_row, 80), 80)
                high, low = split2(cosine)
                table[0, out, :] = high
                table[2, out, :] = low
                high, low = split2(sine)
                table[1, out, :] = high
                table[3, out, :] = low

        find_phases(phase_even, 0)

        def pair(i, carry):
            find_phases(phase_odd, 2 * i + 1)
            fill(phase_even, 2 * i)
            find_phases(phase_even, lax.rem(2 * i + 2, POINTS // TABLE_ROWS))
            fill(phase_odd, 2 * i + 1)
            if beside is not None:
                beside(i)
            return carry

        lax.fori_loop(0, POINTS // PAIR_ROWS, pair, 0)

    fill_table(0)
    fill_table(1)

    def local_part(step):
        slopes[...] = dot(volume_matrix[...], q_parts[...])
        both = dot(trace_parts[...], pick_in[0:FACES, :])
        column[...] = both[0:96] + both[96:192]

    local_part(0)

    def advance(step):
        for slot in range(8):
            arrived = recv[step, slot]
            if slot == 6:
                arrived = jnp.where(g > 0, arrived, 0.0)
            if slot == 7:
                arrived = jnp.where(g < 3, arrived, 0.0)
            high, low = split2(arrived)
            received_parts[0:96, slot * SLOTS : (slot + 1) * SLOTS] = high
            received_parts[96:192, slot * SLOTS : (slot + 1) * SLOTS] = low
        both = dot(received_parts[...], pick_in[FACES:, :])
        outer = column[...] + (both[0:96] + both[96:192])
        index = node_index[...]
        in_first = index < 8
        index = index & 7

        def turned(x):
            halves = []
            for half in (slice(0, 8), slice(8, 16)):
                first = jnp.take_along_axis(x[0:8], index[half], axis=0, mode="promise_in_bounds")
                second = jnp.take_along_axis(x[8:16], index[half], axis=0, mode="promise_in_bounds")
                halves.append(jnp.where(in_first[half], first, second))
            return jnp.concatenate(halves, axis=0)

        jump = []
        for c in range(6):
            rows = slice(c * FACE_PAD, (c + 1) * FACE_PAD)
            jump.append(trace[rows, :] - turned(outer[rows, :]))
        flux = [[] for _ in range(6)]
        for k in range(4):
            part = [x[:, k * ELEMS : (k + 1) * ELEMS] for x in jump]
            v = [normals[m, k : k + 1, :] for m in range(3)]
            half = 0.5 * face_scale[k : k + 1, :]
            e, h = part[:3], part[3:]
            e_dot = v[0] * e[0] + v[1] * e[1] + v[2] * e[2]
            h_dot = v[0] * h[0] + v[1] * h[1] + v[2] * h[2]
            ve, vh = cross(v, e), cross(v, h)
            for m in range(3):
                flux[m].append((vh[m] + e[m] - v[m] * e_dot) * half)
                flux[3 + m].append((h[m] - ve[m] - v[m] * h_dot) * half)
        flux_rows = jnp.concatenate([jnp.concatenate(x, axis=0) for x in flux], axis=1)
        f1, f2 = split2(flux_rows)
        lifted = dot(lift_stack[...], jnp.concatenate([f1, f2, f1], axis=0))

        def slope(r, c):
            return slopes[r * NODE_PAD : (r + 1) * NODE_PAD, c * ELEMS : (c + 1) * ELEMS]

        factors = [geometry[i : i + 1, :] for i in range(9)]

        def gradient(m, c):
            return factors[m] * slope(0, c) + factors[3 + m] * slope(1, c) + factors[6 + m] * slope(2, c)

        for c in range(6):
            other = 3 if c < 3 else 0
            a, b = (c + 1) % 3, (c + 2) % 3
            curl = gradient(a, other + b) - gradient(b, other + a)
            if c >= 3:
                curl = -curl
            rate = curl + lifted[0:NODE_PAD, c * ELEMS : (c + 1) * ELEMS]
            w_next = SECTION_A[step] * w_now[c] + TIME_STEP * rate
            q_next = q_now[c, 0:NODE_PAD, :] + SECTION_B[step] * w_next
            if step == 0:
                w_now[c] = w_next
                q_now[c, 0:NODE_PAD, :] = q_next
            else:
                fields_out[c] = q_next[0:NODES]
                residual_out[c] = w_next[0:NODES]

    for copy in transfers_0:
        copy.wait_recv()
    advance(0)

    make_parts()
    make_trace()
    surface_1 = gather_out(1)
    transfers_1 = copies(1)
    for j in FAR_FIRST:
        transfers_1[j].start()
    currents_1 = currents(surface_1)

    turn = [ANGULAR_FREQUENCY * TIME_STEP * x for x in SECTION_C]
    weighted[...] = jnp.zeros_like(weighted)
    live = lax.broadcasted_iota(jnp.int32, (1, SLOTS), 1) < surface_count[...]
    node_weight = [
        jnp.where(live, surface_weights[:, n * SLOTS : (n + 1) * SLOTS], 0.0) for n in range(FACE)
    ]
    node_weight = jnp.concatenate(node_weight + [jnp.zeros((1, SLOTS), F32)], axis=0)
    for c in range(6):
        rows = slice(c * FACE_PAD, (c + 1) * FACE_PAD)
        real = math.cos(turn[0]) * currents_0[c] + math.cos(turn[1]) * currents_1[c]
        imag = math.sin(turn[0]) * currents_0[c] + math.sin(turn[1]) * currents_1[c]
        by_node[0, rows] = real * node_weight
        by_node[1, rows] = imag * -node_weight
    for n in range(FACE):
        at = slice(n * SLOTS, (n + 1) * SLOTS)
        real = by_node[0, pl.ds(n, 6, stride=FACE_PAD), :]
        imag = by_node[1, pl.ds(n, 6, stride=FACE_PAD), :]
        weighted[0, 0:6, at] = real * COS_GAIN
        weighted[0, 8:14, at] = imag * COS_GAIN
        weighted[1, 0:6, at] = imag * -SIN_GAIN
        weighted[1, 8:14, at] = real * SIN_GAIN
    for which in range(2):
        high, low = split2(weighted[which])
        weighted_parts[which, 0:16, :] = high
        weighted_parts[which, 16:32, :] = low
    far_rows[...] = jnp.zeros_like(far_rows)

    def project(nth, first_row, rows):
        table = tables[nth]
        total = far_rows[nth]
        for which in range(2):
            weights = weighted_parts[which, :, pl.ds(first_row, rows)]
            fine = dot(weights, table[which, pl.ds(first_row, rows), :])
            rest = dot(weights[0:16], table[2 + which, pl.ds(first_row, rows), :])
            total += fine[0:16] + fine[16:32] + rest
        far_rows[nth] = total

    def pack(nth):
        for half in range(2):
            at = slice(half * SLOTS, (half + 1) * SLOTS)
            far_part[nth, half * 12 : half * 12 + 6] = far_rows[nth, 0:6, at]
            far_part[nth, half * 12 + 6 : half * 12 + 12] = far_rows[nth, 8:14, at]

    def far_copy(stage, i, peer, source, target):
        copy = pltpu.make_async_remote_copy(
            src_ref=source,
            dst_ref=target,
            send_sem=far_send_sem.at[stage, i],
            recv_sem=far_recv_sem.at[stage, i],
            device_id=peer,
            device_id_type=MESH,
        )
        copy.start()
        return copy

    def project_two(i):
        at = pl.multiple_of(i * PAIR_ROWS, PAIR_ROWS)
        project(0, at, PAIR_ROWS)
        project(1, at, PAIR_ROWS)

    fill_table(2, project_two)
    stage_a = []
    for nth in range(3):
        if nth == 2:
            project(2, 0, POINTS)
        pack(nth)
        stage_a.append(far_copy(0, nth, sect_peers[nth], far_part.at[nth], far_a.at[nth]))
    fill_table(3)
    project(3, 0, POINTS)
    pack(3)

    local_part(1)
    for copy in stage_a:
        copy.wait_recv()
    far_b[place_at] = far_part[3] + far_a[0] + far_a[1] + far_a[2]
    stage_b = [
        far_copy(1, i, peer, far_b.at[place_at], far_b.at[place_at])
        for i, peer in enumerate(in_peers)
    ]
    for copy in transfers_1:
        copy.wait_recv()
    advance(1)
    for copy in stage_b:
        copy.wait_recv()
    total = far_b[0]
    for i in range(1, 8):
        total = total + far_b[i]
    far_c[block] = total
    stage_c = [
        far_copy(2, i, peer, far_c.at[block], far_c.at[block]) for i, peer in enumerate(block_peers)
    ]
    for copy in transfers_0 + transfers_1 + stage_a + stage_b:
        copy.wait_send()
    for copy in stage_c:
        copy.wait()
    total = far_c[0]
    for i in range(1, 8):
        total = total + far_c[i]
    far_out[:, 0:SLOTS] = total[0:12]
    far_out[:, SLOTS:] = total[12:24]


def hand_over(fields, residual, far, fields_out, residual_out, far_out, sem):
    pairs = [
        (fields, fields_out.at[:, :, 0, :]),
        (residual, residual_out.at[:, :, 0, :]),
        (far, far_out),
    ]
    copies = [pltpu.make_async_copy(a, b, sem.at[i]) for i, (a, b) in enumerate(pairs)]
    for copy in copies:
        copy.start()
    for copy in copies:
        copy.wait()


def on_device(
    fields,
    residual,
    geometry,
    normals,
    face_scale,
    derivatives,
    lift_matrix,
    face_source,
    face_perm,
    send_cycle,
    send_layer,
    surface_faces,
    surface_count,
    surface_points,
    surface_weights,
    angles,
):
    pick, place, place_lift, node_table = constant_matrices()
    hbm = pl.BlockSpec(memory_space=pltpu.HBM)
    vmem = pl.BlockSpec(memory_space=pltpu.VMEM)
    fields_out, residual_out, far = pl.pallas_call(
        kernel,
        out_shape=(
            pltpu.VMEM((6, NODES, ELEMS), F32),
            pltpu.VMEM((6, NODES, ELEMS), F32),
            pltpu.VMEM((12, ELEMS), F32),
        ),
        in_specs=[hbm] * 20,
        out_specs=(vmem, vmem, vmem),
        scratch_shapes=[
            pltpu.VMEM((6, SPLIT_PAD, ELEMS), F32),
            pltpu.VMEM((6, NODE_PAD, ELEMS), F32),
            pltpu.VMEM((6, NODES, ELEMS), F32),
            pltpu.VMEM((6, NODES, ELEMS), F32),
            pltpu.VMEM((9, ELEMS), F32),
            pltpu.VMEM((3, 4, ELEMS), F32),
            pltpu.VMEM((4, ELEMS), F32),
            pltpu.VMEM((3, NODES, NODES), F32),
            pltpu.VMEM((NODES, 60), F32),
            pltpu.VMEM((1, FACES), jnp.int32),
            pltpu.VMEM((1, FACES), jnp.int32),
            pltpu.VMEM((1, 9 * SLOTS), jnp.int32),
            pltpu.VMEM((1, 1), jnp.int32),
            pltpu.VMEM((3, POINTS), F32),
            pltpu.VMEM((1, POINTS), F32),
            pltpu.VMEM((2, ANGLES), F32),
            pltpu.VMEM((64, 5 * SPLIT_PAD), F32),
            pltpu.VMEM((256, 5 * SPLIT_PAD), F32),
            pltpu.VMEM((256, 192), F32),
            pltpu.VMEM((FACE_PAD, 8), jnp.int32),
            pltpu.VMEM((5 * SPLIT_PAD, 6 * ELEMS), BF16),
            pltpu.VMEM((128, 128), F32),
            pltpu.VMEM((128, 5 * SPLIT_PAD), BF16),
            pltpu.VMEM((SPLIT_PAD, 192), BF16),
            pltpu.VMEM((96, FACES), F32),
            pltpu.VMEM((192, FACES), BF16),
            pltpu.VMEM((192, 8 * SLOTS), BF16),
            pltpu.VMEM((FACES, 9 * SLOTS), BF16),
            pltpu.VMEM((2 * FACES, FACES), BF16),
            pltpu.VMEM((FACE_PAD, FACES), jnp.int32),
            pltpu.VMEM((2, 8, 96, SLOTS), F32),
            pltpu.VMEM((2, 8, 96, SLOTS), F32),
            pltpu.VMEM((TABLE_ROWS, SECTOR), F32),
            pltpu.VMEM((TABLE_ROWS, SECTOR), F32),
            pltpu.VMEM((4, POINTS, SECTOR), BF16),
            pltpu.VMEM((4, POINTS, SECTOR), BF16),
            pltpu.VMEM((4, POINTS, SECTOR), BF16),
            pltpu.VMEM((4, POINTS, SECTOR), BF16),
            pltpu.VMEM((POINTS, 48), BF16),
            pltpu.VMEM((48, ANGLES), BF16),
            pltpu.VMEM((2, 96, SLOTS), F32),
            pltpu.VMEM((2, 16, POINTS), F32),
            pltpu.VMEM((2, 32, POINTS), BF16),
            pltpu.VMEM((4, 16, SECTOR), F32),
            pltpu.VMEM((128, 6 * ELEMS), F32),
            pltpu.VMEM((96, FACES), F32),
            pltpu.VMEM((4, 24, SLOTS), F32),
            pltpu.VMEM((3, 24, SLOTS), F32),
            pltpu.VMEM((8, 24, SLOTS), F32),
            pltpu.VMEM((8, 24, SLOTS), F32),
            pltpu.SemaphoreType.DMA((30,)),
            pltpu.SemaphoreType.DMA((2, 8)),
            pltpu.SemaphoreType.DMA((2, 8)),
            pltpu.SemaphoreType.DMA((3, 7)),
            pltpu.SemaphoreType.DMA((3, 7)),
        ],
        compiler_params=pltpu.CompilerParams(
            collective_id=0, has_side_effects=True, vmem_limit_bytes=63 * 1024 * 1024
        ),
    )(
        fields[0].transpose(1, 2, 0, 3),
        residual[0].transpose(1, 2, 0, 3),
        geometry[0].transpose(1, 0, 2),
        normals[0, 0],
        face_scale[0, 0],
        derivatives,
        lift_matrix,
        face_source[0],
        face_perm[0],
        send_cycle[0],
        send_layer[0],
        surface_faces[0],
        surface_count,
        surface_points[0].transpose(1, 0, 2),
        surface_weights[0],
        angles,
        pick,
        place,
        place_lift,
        node_table,
    )
    fields_out, residual_out, far = pl.pallas_call(
        hand_over,
        out_shape=(
            jax.ShapeDtypeStruct((6, NODES, 1, ELEMS), F32),
            jax.ShapeDtypeStruct((6, NODES, 1, ELEMS), F32),
            jax.ShapeDtypeStruct((12, ELEMS), F32),
        ),
        in_specs=[vmem] * 3,
        out_specs=(hbm, hbm, hbm),
        scratch_shapes=[pltpu.SemaphoreType.DMA((3,))],
        compiler_params=pltpu.CompilerParams(vmem_limit_bytes=1024 * 1024),
    )(fields_out, residual_out, far)
    return (fields_out.transpose(2, 0, 1, 3)[None], residual_out.transpose(2, 0, 1, 3)[None], far)


def solution(mesh):
    in_specs = (
        P("dom", "sect", None, None, None),
        P("dom", "sect", None, None, None),
        P("dom", "sect", None, None),
        P("dom", "sect", None, None, None),
        P("dom", "sect", None, None),
        P(),
        P(),
        P("dom", "sect", None),
        P("dom", "sect", None),
        P("dom", "sect", None),
        P("dom", "sect", None),
        P("dom", "sect", None),
        P("dom", "sect"),
        P("dom", "sect", None, None),
        P("dom", "sect", None),
        P(),
    )
    out_specs = (
        P("dom", "sect", None, None, None),
        P("dom", "sect", None, None, None),
        P(None, "sect"),
    )
    return jax.shard_map(
        on_device, mesh=mesh, in_specs=in_specs, out_specs=out_specs, check_vma=False
    )
```

```python
import functools
import math

import jax
import jax.numpy as jnp
import numpy as np
from jax import lax
from jax.experimental import pallas as pl
from jax.experimental.pallas import tpu as pltpu
from jax.sharding import PartitionSpec as P

SECTION_A = (-0.4178904745, -1.192151694643)
SECTION_B = (0.3792103129999, 0.8229550293869)
SECTION_C = (0.1496590219993, 0.3704009573644)
TIME_STEP = 0.2
ANGULAR_FREQUENCY = 2.0 * math.pi
HOPS = 3
MESH = pl.DeviceIdType.MESH
FAR_FIRST = (0, 5, 1, 4, 6, 7, 2, 3)
F32 = jnp.float32
BF16 = jnp.bfloat16

NODES = 35
NODE_PAD = 40
SPLIT_PAD = 48
FACE = 15
FACE_PAD = 16
ELEMS = 256
FACES = 4 * ELEMS
SLOTS = 128
ANGLES = 1024
POINTS = FACE * SLOTS
TABLE_ROWS = 320
PAIR_ROWS = 2 * TABLE_ROWS
SECTOR = 256

SIN_POLY = (4.442879676818848, -7.3078179359436035, 3.5977888107299805, -0.7912381887435913)
COS_POLY = (1.4142041206359863, -6.977642059326172, 5.715238571166992, -1.7283486127853394)
SIN_MONIC = tuple(x / SIN_POLY[-1] for x in SIN_POLY[:-1])
COS_MONIC = tuple(x / COS_POLY[-1] for x in COS_POLY[:-1])
COS_GAIN = SIN_POLY[-1] * SIN_POLY[-1]
SIN_GAIN = SIN_POLY[-1] * COS_POLY[-1]


def static_tables():
    node_list = []
    for i in range(5):
        for j in range(5 - i):
            for k in range(5 - i - j):
                node_list.append((i, j, k, 4 - i - j - k))
    face_nodes = []
    for which_face in range(4):
        face_nodes.append(
            [n for n, barycentric in enumerate(node_list) if barycentric[which_face] == 0]
        )
    reduced = [tuple((b for q, b in enumerate(node_list[n]) if q != 0)) for n in face_nodes[0]]
    orderings = [(0, 1, 2), (1, 2, 0), (2, 0, 1), (0, 2, 1), (2, 1, 0), (1, 0, 2)]
    permutation = [
        [reduced.index(tuple((triple[s] for s in ordering))) for triple in reduced]
        for ordering in orderings
    ]
    return (np.array(face_nodes, np.int32), np.array(permutation, np.int32))


def constant_matrices():
    face_nodes, node_table = static_tables()
    pick = np.zeros((64, 5 * SPLIT_PAD), np.float32)
    for k in range(4):
        for n in range(FACE):
            for part in range(3):
                pick[k * FACE_PAD + n, part * SPLIT_PAD + face_nodes[k][n]] = 1
    place = np.zeros((2, 128, 5 * SPLIT_PAD), np.float32)
    for i in range(NODES):
        for part in range(3):
            place[0, i, part * SPLIT_PAD + i] = 1
        for part in range(3, 5):
            place[1, i, part * SPLIT_PAD + i] = 1
    lift = np.zeros((2, 128, 192), np.float32)
    for k in range(4):
        for n in range(FACE):
            for part in range(3):
                lift[part // 2, k * FACE + n, part * 64 + k * FACE_PAD + n] = 1
    table = np.zeros((FACE_PAD, 8), np.int32)
    table[:FACE, :6] = node_table.T
    table[FACE, :] = FACE
    return (
        pick,
        place.reshape(256, -1),
        lift.reshape(256, -1),
        table,
    )


def dot(a, b, dims=((1,), (0,))):
    return lax.dot_general(a, b, (dims, ((), ())), preferred_element_type=F32)


def split2(x):
    high = x.astype(BF16)
    return high, (x - high.astype(F32)).astype(BF16)


def split3(x):
    high = x.astype(BF16)
    rest = x - high.astype(F32)
    middle = rest.astype(BF16)
    return high, middle, (rest - middle.astype(F32)).astype(BF16)


def cross(a, b):
    return [a[1] * b[2] - a[2] * b[1], a[2] * b[0] - a[0] * b[2], a[0] * b[1] - a[1] * b[0]]


def kernel(
    fields_in,
    residual_in,
    geometry_in,
    normals_in,
    face_scale_in,
    derivatives_in,
    lift_matrix_in,
    face_source_in,
    face_perm_in,
    send_cycle_in,
    send_layer_in,
    surface_faces_in,
    surface_count_in,
    surface_points_in,
    surface_weights_in,
    angles_in,
    pick_in_,
    place_in_,
    place_lift_in,
    node_table_in,
    fields_out,
    residual_out,
    far_out,
    q_now,
    w_now,
    fields,
    residual,
    geometry,
    normals,
    face_scale,
    derivatives,
    lift_matrix,
    face_source,
    face_perm,
    send_list,
    surface_count,
    surface_points,
    surface_weights,
    angles,
    pick,
    place,
    place_lift,
    node_table,
    q_parts,
    small,
    volume_matrix,
    lift_stack,
    trace,
    trace_parts,
    received_parts,
    pick_out,
    pick_in,
    node_index,
    send,
    recv,
    phase_even,
    phase_odd,
    table_0,
    table_1,
    table_2,
    table_3,
    point_parts,
    direction_parts,
    by_node,
    weighted,
    weighted_parts,
    far_rows,
    slopes,
    column,
    far_part,
    far_a,
    far_b,
    far_c,
    load_sem,
    send_sem,
    recv_sem,
    far_send_sem,
    far_recv_sem,
):
    d = lax.axis_index("dom")
    g = lax.axis_index("sect")
    block, place_at = d // 8, d % 8

    def dom_shift(by):
        return lax.rem(d + 64 + by, 64)

    def sect_shift(by):
        return lax.rem(g + 4 + by, 4)

    offsets = list(range(-HOPS, 0)) + list(range(1, HOPS + 1))
    near = [(dom_shift(o), g) for o in offsets] + [(d, sect_shift(-1)), (d, sect_shift(1))]
    sect_peers = [(d, sect_shift(i)) for i in range(1, 4)]
    in_peers = [(block * 8 + lax.rem(place_at + i, 8), g) for i in range(1, 8)]
    block_peers = [(lax.rem(block + i, 8) * 8 + place_at, g) for i in range(1, 8)]
    everyone = near + sect_peers + in_peers + block_peers

    barrier = pltpu.get_barrier_semaphore()
    for peer in everyone:
        pl.semaphore_signal(barrier, inc=1, device_id=peer, device_id_type=MESH)

    def load(at, source, target):
        copy = pltpu.make_async_copy(source, target, load_sem.at[at])
        copy.start()
        return copy

    first = [
        load(0, fields_in.at[:, :, 0, :], fields),
        load(6, pick_in_, pick),
        load(7, send_cycle_in, send_list.at[:, 0 : 6 * SLOTS]),
        load(8, send_layer_in, send_list.at[:, 6 * SLOTS : 8 * SLOTS]),
        load(9, surface_faces_in, send_list.at[:, 8 * SLOTS :]),
    ]
    rest = [
        (residual_in.at[:, :, 0, :], residual),
        (geometry_in.at[:, 0, :], geometry),
        (normals_in, normals),
        (face_scale_in, face_scale),
        (derivatives_in, derivatives),
        (lift_matrix_in, lift_matrix),
        (face_source_in, face_source),
        (face_perm_in, face_perm),
        (surface_count_in, surface_count),
        (surface_points_in.at[:, 0, :], surface_points),
        (surface_weights_in, surface_weights),
        (angles_in, angles),
        (place_in_, place),
        (place_lift_in, place_lift),
        (node_table_in, node_table),
    ]
    q_now[:, 32:SPLIT_PAD, :] = jnp.zeros((6, SPLIT_PAD - 32, ELEMS), F32)
    w_now[:, 32:NODE_PAD, :] = jnp.zeros((6, NODE_PAD - 32, ELEMS), F32)

    def make_parts():
        for c in range(6):
            p1, p2, p3 = split3(q_now[c])
            for at, part in enumerate((p1, p2, p3, p1, p2)):
                q_parts[at * SPLIT_PAD : (at + 1) * SPLIT_PAD, c * ELEMS : (c + 1) * ELEMS] = part

    def make_trace():
        picked = dot(pick[...].astype(BF16), q_parts[...])
        for c in range(6):
            for k in range(4):
                trace[c * FACE_PAD : (c + 1) * FACE_PAD, k * ELEMS : (k + 1) * ELEMS] = picked[
                    k * FACE_PAD : (k + 1) * FACE_PAD, c * ELEMS : (c + 1) * ELEMS
                ]
        high, low = split2(trace[...])
        trace_parts[0:96, :] = high
        trace_parts[96:192, :] = low

    def one_hot(target, index_row, rows):
        width = index_row.shape[1]
        row_of = lax.broadcasted_iota(jnp.int32, (SLOTS, width), 0).astype(F32).astype(BF16)

        def body(i, carry):
            at = pl.multiple_of(i * SLOTS, SLOTS)
            wanted = (index_row - i * SLOTS).astype(F32).astype(BF16)
            target[pl.ds(at, SLOTS), :] = jnp.where(row_of == wanted, BF16(1), BF16(0))
            return carry

        lax.fori_loop(0, rows // SLOTS, body, 0)

    later = [load(10 + i, *pair) for i, pair in enumerate(rest)]
    for copy in first[1:]:
        copy.wait()
    one_hot(pick_out, send_list[...], FACES)
    first[0].wait()
    for c in range(6):
        q_now[c, 0:NODES, :] = fields[c]
    make_parts()
    make_trace()

    def copies(step):
        made = []
        for j, peer in enumerate(near):
            landing = 5 - j if j < 6 else 13 - j
            made.append(
                pltpu.make_async_remote_copy(
                    src_ref=send.at[step, j],
                    dst_ref=recv.at[step, landing],
                    send_sem=send_sem.at[step, j],
                    recv_sem=recv_sem.at[step, landing],
                    device_id=peer,
                    device_id_type=MESH,
                )
            )
        return made

    def gather_out(step):
        both = dot(trace_parts[...], pick_out[...])
        gathered = both[0:96] + both[96:192]
        for j in range(8):
            send[step, j] = gathered[:, j * SLOTS : (j + 1) * SLOTS]
        return gathered[:, 8 * SLOTS :]

    surface_0 = gather_out(0)
    pl.semaphore_wait(barrier, len(everyone))
    transfers_0 = copies(0)
    for j in FAR_FIRST:
        transfers_0[j].start()

    small[...] = jnp.zeros_like(small)
    for copy in later:
        copy.wait()
    for c in range(6):
        w_now[c, 0:NODES, :] = residual[c]
    for r in range(3):
        small[r * NODE_PAD : r * NODE_PAD + NODES, 0:NODES] = derivatives[r]
    main, rest = split2(small[0:128, :])
    volume_matrix[...] = (
        dot(main, place[0:128, :].astype(BF16)) + dot(rest, place[128:256, :].astype(BF16))
    ).astype(BF16)
    small[0:128, :] = jnp.zeros((128, 128), F32)
    small[0:NODES, 0:60] = lift_matrix[...]
    main, rest = split2(small[0:SPLIT_PAD, :])
    lift_stack[...] = (
        dot(main, place_lift[0:128, :].astype(BF16)) + dot(rest, place_lift[128:256, :].astype(BF16))
    ).astype(BF16)
    small[0:SPLIT_PAD, :] = jnp.zeros((SPLIT_PAD, 128), F32)

    one_hot(pick_in, face_source[...], 2 * FACES)
    orient = jnp.broadcast_to(face_perm[...], (FACE_PAD, FACES))
    index = jnp.broadcast_to(node_table[:, 0:1], (FACE_PAD, FACES))
    for which in range(1, 6):
        index = jnp.where(orient == which, node_table[:, which : which + 1], index)
    node_index[...] = index

    normal_rows = jnp.concatenate(
        [jnp.concatenate([normals[m, k : k + 1, :] for k in range(4)], axis=1) for m in range(3)]
        + [jnp.zeros((5, FACES), F32)],
        axis=0,
    )
    high, low = split2(jnp.concatenate([normal_rows, normal_rows - normal_rows.astype(BF16).astype(F32)], axis=0))
    picked = dot(high, pick_out[:, 8 * SLOTS :])
    surface_normal = picked[0:8] + picked[8:16]

    def currents(gathered):
        e = [gathered[c * FACE_PAD : (c + 1) * FACE_PAD, :] for c in range(3)]
        h = [gathered[c * FACE_PAD : (c + 1) * FACE_PAD, :] for c in range(3, 6)]
        v = [surface_normal[m : m + 1, :] for m in range(3)]
        return cross(v, h) + [-x for x in cross(v, e)]

    currents_0 = currents(surface_0)

    polar, azimuth = angles[0:1, :], angles[1:2, :]
    direction = jnp.concatenate(
        [
            jnp.sin(polar) * jnp.cos(azimuth),
            jnp.sin(polar) * jnp.sin(azimuth),
            jnp.cos(polar),
            jnp.zeros((5, ANGLES), F32),
        ],
        axis=0,
    )
    d1, d2, d3 = [x.astype(F32) for x in split3(direction)]
    direction_parts[...] = jnp.concatenate([d1, d2, d1, d3, d2, d1], axis=0).astype(BF16)
    points = jnp.concatenate([surface_points[...], jnp.zeros((5, POINTS), F32)], axis=0)
    p1, p2, p3 = [x.astype(F32) for x in split3(points)]
    point_parts[...] = jnp.concatenate([p1, p1, p2, p1, p2, p3], axis=0).T.astype(BF16)

    tables = (table_0, table_1, table_2, table_3)

    def fill_table(nth, besides=(lambda: None,) * 3):
        table = tables[nth]
        sector = pl.ds(pl.multiple_of(sect_shift(nth + 1) * SECTOR, SECTOR), SECTOR)

        def find_phases(target, chunk):
            at = slice(chunk * TABLE_ROWS, (chunk + 1) * TABLE_ROWS)
            target[...] = dot(point_parts[at, :], direction_parts[:, sector])

        def fill(phases, chunk):
            for first_row in range(0, TABLE_ROWS, 80):
                turns = phases[first_row : first_row + 80, :]
                r = turns - jnp.round(turns)
                u = r * r
                s = u + SIN_MONIC[2]
                c = u + COS_MONIC[2]
                for order in range(1, -1, -1):
                    s = s * u + SIN_MONIC[order]
                    c = c * u + COS_MONIC[order]
                s = s * r
                sine = s * c
                cosine = 1.0 / COS_GAIN - s * s
                out = pl.ds(chunk * TABLE_ROWS + first_row, 80)
                high, low = split2(cosine)
                table[0, out, :] = high
                table[2, out, :] = low
                high, low = split2(sine)
                table[1, out, :] = high
                table[3, out, :] = low

        phases = (phase_even, phase_odd)
        find_phases(phases[0], 0)
        for chunk in range(POINTS // TABLE_ROWS):
            if chunk + 1 < POINTS // TABLE_ROWS:
                find_phases(phases[(chunk + 1) % 2], chunk + 1)
            fill(phases[chunk % 2], chunk)
            if chunk % 2:
                besides[chunk // 2]()

    fill_table(0)
    fill_table(1)

    def local_part(step):
        slopes[...] = dot(volume_matrix[...], q_parts[...])
        both = dot(trace_parts[...], pick_in[0:FACES, :])
        column[...] = both[0:96] + both[96:192]

    local_part(0)

    def advance(step):
        for slot in range(8):
            arrived = recv[step, slot]
            if slot == 6:
                arrived = jnp.where(g > 0, arrived, 0.0)
            if slot == 7:
                arrived = jnp.where(g < 3, arrived, 0.0)
            high, low = split2(arrived)
            received_parts[0:96, slot * SLOTS : (slot + 1) * SLOTS] = high
            received_parts[96:192, slot * SLOTS : (slot + 1) * SLOTS] = low
        both = dot(received_parts[...], pick_in[FACES:, :])
        outer = column[...] + (both[0:96] + both[96:192])
        index = node_index[...]
        in_first = index < 8
        index = index & 7

        def turned(x):
            halves = []
            for half in (slice(0, 8), slice(8, 16)):
                first = jnp.take_along_axis(x[0:8], index[half], axis=0, mode="promise_in_bounds")
                second = jnp.take_along_axis(x[8:16], index[half], axis=0, mode="promise_in_bounds")
                halves.append(jnp.where(in_first[half], first, second))
            return jnp.concatenate(halves, axis=0)

        jump = []
        for c in range(6):
            rows = slice(c * FACE_PAD, (c + 1) * FACE_PAD)
            jump.append(trace[rows, :] - turned(outer[rows, :]))
        flux = [[] for _ in range(6)]
        for k in range(4):
            part = [x[:, k * ELEMS : (k + 1) * ELEMS] for x in jump]
            v = [normals[m, k : k + 1, :] for m in range(3)]
            half = 0.5 * face_scale[k : k + 1, :]
            e, h = part[:3], part[3:]
            e_dot = v[0] * e[0] + v[1] * e[1] + v[2] * e[2]
            h_dot = v[0] * h[0] + v[1] * h[1] + v[2] * h[2]
            ve, vh = cross(v, e), cross(v, h)
            for m in range(3):
                flux[m].append((vh[m] + e[m] - v[m] * e_dot) * half)
                flux[3 + m].append((h[m] - ve[m] - v[m] * h_dot) * half)
        flux_rows = jnp.concatenate([jnp.concatenate(x, axis=0) for x in flux], axis=1)
        f1, f2 = split2(flux_rows)
        lifted = dot(lift_stack[...], jnp.concatenate([f1, f2, f1], axis=0))

        def slope(r, c):
            return slopes[r * NODE_PAD : (r + 1) * NODE_PAD, c * ELEMS : (c + 1) * ELEMS]

        factors = [geometry[i : i + 1, :] for i in range(9)]

        def gradient(m, c):
            return factors[m] * slope(0, c) + factors[3 + m] * slope(1, c) + factors[6 + m] * slope(2, c)

        for c in range(6):
            other = 3 if c < 3 else 0
            a, b = (c + 1) % 3, (c + 2) % 3
            curl = gradient(a, other + b) - gradient(b, other + a)
            if c >= 3:
                curl = -curl
            rate = curl + lifted[0:NODE_PAD, c * ELEMS : (c + 1) * ELEMS]
            w_next = SECTION_A[step] * w_now[c] + TIME_STEP * rate
            q_next = q_now[c, 0:NODE_PAD, :] + SECTION_B[step] * w_next
            if step == 0:
                w_now[c] = w_next
                q_now[c, 0:NODE_PAD, :] = q_next
            else:
                fields_out[c] = q_next[0:NODES]
                residual_out[c] = w_next[0:NODES]

    for copy in transfers_0:
        copy.wait_recv()
    advance(0)

    make_parts()
    make_trace()
    surface_1 = gather_out(1)
    transfers_1 = copies(1)
    for j in FAR_FIRST:
        transfers_1[j].start()
    currents_1 = currents(surface_1)

    turn = [ANGULAR_FREQUENCY * TIME_STEP * x for x in SECTION_C]
    weighted[...] = jnp.zeros_like(weighted)
    live = lax.broadcasted_iota(jnp.int32, (1, SLOTS), 1) < surface_count[...]
    node_weight = [
        jnp.where(live, surface_weights[:, n * SLOTS : (n + 1) * SLOTS], 0.0) for n in range(FACE)
    ]
    node_weight = jnp.concatenate(node_weight + [jnp.zeros((1, SLOTS), F32)], axis=0)
    for c in range(6):
        rows = slice(c * FACE_PAD, (c + 1) * FACE_PAD)
        real = math.cos(turn[0]) * currents_0[c] + math.cos(turn[1]) * currents_1[c]
        imag = math.sin(turn[0]) * currents_0[c] + math.sin(turn[1]) * currents_1[c]
        by_node[0, rows] = real * node_weight
        by_node[1, rows] = imag * -node_weight
    for n in range(FACE):
        at = slice(n * SLOTS, (n + 1) * SLOTS)
        real = by_node[0, pl.ds(n, 6, stride=FACE_PAD), :]
        imag = by_node[1, pl.ds(n, 6, stride=FACE_PAD), :]
        weighted[0, 0:6, at] = real * COS_GAIN
        weighted[0, 8:14, at] = imag * COS_GAIN
        weighted[1, 0:6, at] = imag * -SIN_GAIN
        weighted[1, 8:14, at] = real * SIN_GAIN
    for which in range(2):
        high, low = split2(weighted[which])
        weighted_parts[which, 0:16, :] = high
        weighted_parts[which, 16:32, :] = low
    far_rows[...] = jnp.zeros_like(far_rows)

    def project(nth, first_row, rows):
        table = tables[nth]
        total = far_rows[nth]
        for which in range(2):
            weights = weighted_parts[which, :, pl.ds(first_row, rows)]
            fine = dot(weights, table[which, pl.ds(first_row, rows), :])
            rest = dot(weights[0:16], table[2 + which, pl.ds(first_row, rows), :])
            total += fine[0:16] + fine[16:32] + rest
        far_rows[nth] = total

    def pack(nth):
        for half in range(2):
            at = slice(half * SLOTS, (half + 1) * SLOTS)
            far_part[nth, half * 12 : half * 12 + 6] = far_rows[nth, 0:6, at]
            far_part[nth, half * 12 + 6 : half * 12 + 12] = far_rows[nth, 8:14, at]

    def far_copy(stage, i, peer, source, target):
        copy = pltpu.make_async_remote_copy(
            src_ref=source,
            dst_ref=target,
            send_sem=far_send_sem.at[stage, i],
            recv_sem=far_recv_sem.at[stage, i],
            device_id=peer,
            device_id_type=MESH,
        )
        copy.start()
        return copy

    def first_beside():
        project(0, 0, POINTS)

    def second_beside():
        project(1, 0, POINTS)
        project(2, 0, PAIR_ROWS)

    def third_beside():
        project(2, PAIR_ROWS, PAIR_ROWS)

    fill_table(2, (first_beside, second_beside, third_beside))
    project(2, 2 * PAIR_ROWS, PAIR_ROWS)
    stage_a = []
    for nth in range(3):
        pack(nth)
        stage_a.append(far_copy(0, nth, sect_peers[nth], far_part.at[nth], far_a.at[nth]))
    fill_table(3)
    project(3, 0, POINTS)
    pack(3)

    local_part(1)
    for copy in stage_a:
        copy.wait_recv()
    far_b[place_at] = far_part[3] + far_a[0] + far_a[1] + far_a[2]
    stage_b = [
        far_copy(1, i, peer, far_b.at[place_at], far_b.at[place_at])
        for i, peer in enumerate(in_peers)
    ]
    for copy in transfers_1:
        copy.wait_recv()
    advance(1)
    for copy in stage_b:
        copy.wait_recv()
    total = far_b[0]
    for i in range(1, 8):
        total = total + far_b[i]
    far_c[block] = total
    stage_c = [
        far_copy(2, i, peer, far_c.at[block], far_c.at[block]) for i, peer in enumerate(block_peers)
    ]
    for copy in transfers_0 + transfers_1 + stage_a + stage_b:
        copy.wait_send()
    for copy in stage_c:
        copy.wait()
    total = far_c[0]
    for i in range(1, 8):
        total = total + far_c[i]
    far_out[:, 0:SLOTS] = total[0:12]
    far_out[:, SLOTS:] = total[12:24]


def hand_over(fields, residual, far, fields_out, residual_out, far_out, sem):
    pairs = [
        (fields, fields_out.at[:, :, 0, :]),
        (residual, residual_out.at[:, :, 0, :]),
        (far, far_out),
    ]
    copies = [pltpu.make_async_copy(a, b, sem.at[i]) for i, (a, b) in enumerate(pairs)]
    for copy in copies:
        copy.start()
    for copy in copies:
        copy.wait()


def on_device(
    fields,
    residual,
    geometry,
    normals,
    face_scale,
    derivatives,
    lift_matrix,
    face_source,
    face_perm,
    send_cycle,
    send_layer,
    surface_faces,
    surface_count,
    surface_points,
    surface_weights,
    angles,
):
    pick, place, place_lift, node_table = constant_matrices()
    hbm = pl.BlockSpec(memory_space=pltpu.HBM)
    vmem = pl.BlockSpec(memory_space=pltpu.VMEM)
    fields_out, residual_out, far = pl.pallas_call(
        kernel,
        out_shape=(
            pltpu.VMEM((6, NODES, ELEMS), F32),
            pltpu.VMEM((6, NODES, ELEMS), F32),
            pltpu.VMEM((12, ELEMS), F32),
        ),
        in_specs=[hbm] * 20,
        out_specs=(vmem, vmem, vmem),
        scratch_shapes=[
            pltpu.VMEM((6, SPLIT_PAD, ELEMS), F32),
            pltpu.VMEM((6, NODE_PAD, ELEMS), F32),
            pltpu.VMEM((6, NODES, ELEMS), F32),
            pltpu.VMEM((6, NODES, ELEMS), F32),
            pltpu.VMEM((9, ELEMS), F32),
            pltpu.VMEM((3, 4, ELEMS), F32),
            pltpu.VMEM((4, ELEMS), F32),
            pltpu.VMEM((3, NODES, NODES), F32),
            pltpu.VMEM((NODES, 60), F32),
            pltpu.VMEM((1, FACES), jnp.int32),
            pltpu.VMEM((1, FACES), jnp.int32),
            pltpu.VMEM((1, 9 * SLOTS), jnp.int32),
            pltpu.VMEM((1, 1), jnp.int32),
            pltpu.VMEM((3, POINTS), F32),
            pltpu.VMEM((1, POINTS), F32),
            pltpu.VMEM((2, ANGLES), F32),
            pltpu.VMEM((64, 5 * SPLIT_PAD), F32),
            pltpu.VMEM((256, 5 * SPLIT_PAD), F32),
            pltpu.VMEM((256, 192), F32),
            pltpu.VMEM((FACE_PAD, 8), jnp.int32),
            pltpu.VMEM((5 * SPLIT_PAD, 6 * ELEMS), BF16),
            pltpu.VMEM((128, 128), F32),
            pltpu.VMEM((128, 5 * SPLIT_PAD), BF16),
            pltpu.VMEM((SPLIT_PAD, 192), BF16),
            pltpu.VMEM((96, FACES), F32),
            pltpu.VMEM((192, FACES), BF16),
            pltpu.VMEM((192, 8 * SLOTS), BF16),
            pltpu.VMEM((FACES, 9 * SLOTS), BF16),
            pltpu.VMEM((2 * FACES, FACES), BF16),
            pltpu.VMEM((FACE_PAD, FACES), jnp.int32),
            pltpu.VMEM((2, 8, 96, SLOTS), F32),
            pltpu.VMEM((2, 8, 96, SLOTS), F32),
            pltpu.VMEM((TABLE_ROWS, SECTOR), F32),
            pltpu.VMEM((TABLE_ROWS, SECTOR), F32),
            pltpu.VMEM((4, POINTS, SECTOR), BF16),
            pltpu.VMEM((4, POINTS, SECTOR), BF16),
            pltpu.VMEM((4, POINTS, SECTOR), BF16),
            pltpu.VMEM((4, POINTS, SECTOR), BF16),
            pltpu.VMEM((POINTS, 48), BF16),
            pltpu.VMEM((48, ANGLES), BF16),
            pltpu.VMEM((2, 96, SLOTS), F32),
            pltpu.VMEM((2, 16, POINTS), F32),
            pltpu.VMEM((2, 32, POINTS), BF16),
            pltpu.VMEM((4, 16, SECTOR), F32),
            pltpu.VMEM((128, 6 * ELEMS), F32),
            pltpu.VMEM((96, FACES), F32),
            pltpu.VMEM((4, 24, SLOTS), F32),
            pltpu.VMEM((3, 24, SLOTS), F32),
            pltpu.VMEM((8, 24, SLOTS), F32),
            pltpu.VMEM((8, 24, SLOTS), F32),
            pltpu.SemaphoreType.DMA((30,)),
            pltpu.SemaphoreType.DMA((2, 8)),
            pltpu.SemaphoreType.DMA((2, 8)),
            pltpu.SemaphoreType.DMA((3, 7)),
            pltpu.SemaphoreType.DMA((3, 7)),
        ],
        compiler_params=pltpu.CompilerParams(
            collective_id=0, has_side_effects=True, vmem_limit_bytes=63 * 1024 * 1024
        ),
    )(
        fields[0].transpose(1, 2, 0, 3),
        residual[0].transpose(1, 2, 0, 3),
        geometry[0].transpose(1, 0, 2),
        normals[0, 0],
        face_scale[0, 0],
        derivatives,
        lift_matrix,
        face_source[0],
        face_perm[0],
        send_cycle[0],
        send_layer[0],
        surface_faces[0],
        surface_count,
        surface_points[0].transpose(1, 0, 2),
        surface_weights[0],
        angles,
        pick,
        place,
        place_lift,
        node_table,
    )
    fields_out, residual_out, far = pl.pallas_call(
        hand_over,
        out_shape=(
            jax.ShapeDtypeStruct((6, NODES, 1, ELEMS), F32),
            jax.ShapeDtypeStruct((6, NODES, 1, ELEMS), F32),
            jax.ShapeDtypeStruct((12, ELEMS), F32),
        ),
        in_specs=[vmem] * 3,
        out_specs=(hbm, hbm, hbm),
        scratch_shapes=[pltpu.SemaphoreType.DMA((3,))],
        compiler_params=pltpu.CompilerParams(vmem_limit_bytes=1024 * 1024),
    )(fields_out, residual_out, far)
    return (fields_out.transpose(2, 0, 1, 3)[None], residual_out.transpose(2, 0, 1, 3)[None], far)


def solution(mesh):
    in_specs = (
        P("dom", "sect", None, None, None),
        P("dom", "sect", None, None, None),
        P("dom", "sect", None, None),
        P("dom", "sect", None, None, None),
        P("dom", "sect", None, None),
        P(),
        P(),
        P("dom", "sect", None),
        P("dom", "sect", None),
        P("dom", "sect", None),
        P("dom", "sect", None),
        P("dom", "sect", None),
        P("dom", "sect"),
        P("dom", "sect", None, None),
        P("dom", "sect", None),
        P(),
    )
    out_specs = (
        P("dom", "sect", None, None, None),
        P("dom", "sect", None, None, None),
        P(None, "sect"),
    )
    return jax.shard_map(
        on_device, mesh=mesh, in_specs=in_specs, out_specs=out_specs, check_vma=False
    )
```

```python
import functools
import math

import jax
import jax.numpy as jnp
import numpy as np
from jax import lax
from jax.experimental import pallas as pl
from jax.experimental.pallas import tpu as pltpu
from jax.sharding import PartitionSpec as P

SECTION_A = (-0.4178904745, -1.192151694643)
SECTION_B = (0.3792103129999, 0.8229550293869)
SECTION_C = (0.1496590219993, 0.3704009573644)
TIME_STEP = 0.2
ANGULAR_FREQUENCY = 2.0 * math.pi
HOPS = 3
MESH = pl.DeviceIdType.MESH
RING_ORDER = (4, 3, 5, 2, 6, 1, 7)
FAR_FIRST = (0, 5, 1, 4, 6, 7, 2, 3)
F32 = jnp.float32
BF16 = jnp.bfloat16

NODES = 35
NODE_PAD = 40
SPLIT_PAD = 48
FACE = 15
FACE_PAD = 16
ELEMS = 256
FACES = 4 * ELEMS
SLOTS = 128
ANGLES = 1024
POINTS = FACE * SLOTS
TABLE_ROWS = 320
PAIR_ROWS = 2 * TABLE_ROWS
SECTOR = 256

SIN_POLY = (4.442879676818848, -7.3078179359436035, 3.5977888107299805, -0.7912381887435913)
COS_POLY = (1.4142041206359863, -6.977642059326172, 5.715238571166992, -1.7283486127853394)
SIN_MONIC = tuple(x / SIN_POLY[-1] for x in SIN_POLY[:-1])
COS_MONIC = tuple(x / COS_POLY[-1] for x in COS_POLY[:-1])
COS_GAIN = SIN_POLY[-1] * SIN_POLY[-1]
SIN_GAIN = SIN_POLY[-1] * COS_POLY[-1]


def static_tables():
    node_list = []
    for i in range(5):
        for j in range(5 - i):
            for k in range(5 - i - j):
                node_list.append((i, j, k, 4 - i - j - k))
    face_nodes = []
    for which_face in range(4):
        face_nodes.append(
            [n for n, barycentric in enumerate(node_list) if barycentric[which_face] == 0]
        )
    reduced = [tuple((b for q, b in enumerate(node_list[n]) if q != 0)) for n in face_nodes[0]]
    orderings = [(0, 1, 2), (1, 2, 0), (2, 0, 1), (0, 2, 1), (2, 1, 0), (1, 0, 2)]
    permutation = [
        [reduced.index(tuple((triple[s] for s in ordering))) for triple in reduced]
        for ordering in orderings
    ]
    return (np.array(face_nodes, np.int32), np.array(permutation, np.int32))


def constant_matrices():
    face_nodes, node_table = static_tables()
    pick = np.zeros((64, 5 * SPLIT_PAD), np.float32)
    for k in range(4):
        for n in range(FACE):
            for part in range(3):
                pick[k * FACE_PAD + n, part * SPLIT_PAD + face_nodes[k][n]] = 1
    place = np.zeros((2, 128, 5 * SPLIT_PAD), np.float32)
    for i in range(NODES):
        for part in range(3):
            place[0, i, part * SPLIT_PAD + i] = 1
        for part in range(3, 5):
            place[1, i, part * SPLIT_PAD + i] = 1
    lift = np.zeros((2, 128, 192), np.float32)
    for k in range(4):
        for n in range(FACE):
            for part in range(3):
                lift[part // 2, k * FACE + n, part * 64 + k * FACE_PAD + n] = 1
    table = np.zeros((FACE_PAD, 8), np.int32)
    table[:FACE, :6] = node_table.T
    table[FACE, :] = FACE
    return (
        pick,
        place.reshape(256, -1),
        lift.reshape(256, -1),
        table,
    )


def dot(a, b, dims=((1,), (0,))):
    return lax.dot_general(a, b, (dims, ((), ())), preferred_element_type=F32)


def split2(x):
    high = x.astype(BF16)
    return high, (x - high.astype(F32)).astype(BF16)


def split3(x):
    high = x.astype(BF16)
    rest = x - high.astype(F32)
    middle = rest.astype(BF16)
    return high, middle, (rest - middle.astype(F32)).astype(BF16)


def cross(a, b):
    return [a[1] * b[2] - a[2] * b[1], a[2] * b[0] - a[0] * b[2], a[0] * b[1] - a[1] * b[0]]


def kernel(
    fields_in,
    residual_in,
    geometry_in,
    normals_in,
    face_scale_in,
    derivatives_in,
    lift_matrix_in,
    face_source_in,
    face_perm_in,
    send_cycle_in,
    send_layer_in,
    surface_faces_in,
    surface_count_in,
    surface_points_in,
    surface_weights_in,
    angles_in,
    pick_in_,
    place_in_,
    place_lift_in,
    node_table_in,
    fields_out,
    residual_out,
    far_out,
    q_now,
    w_now,
    fields,
    residual,
    geometry,
    normals,
    face_scale,
    derivatives,
    lift_matrix,
    face_source,
    face_perm,
    send_list,
    surface_count,
    surface_points,
    surface_weights,
    angles,
    pick,
    place,
    place_lift,
    node_table,
    q_parts,
    small,
    volume_matrix,
    lift_stack,
    trace,
    trace_parts,
    received_parts,
    pick_out,
    pick_in,
    node_index,
    send,
    recv,
    phase_even,
    phase_odd,
    table_0,
    table_1,
    table_2,
    table_3,
    point_parts,
    direction_parts,
    by_node,
    weighted,
    weighted_parts,
    far_rows,
    slopes,
    column,
    far_part,
    far_a,
    far_b,
    far_c,
    load_sem,
    send_sem,
    recv_sem,
    far_send_sem,
    far_recv_sem,
):
    d = lax.axis_index("dom")
    g = lax.axis_index("sect")
    block, place_at = d // 8, d % 8

    def dom_shift(by):
        return lax.rem(d + 64 + by, 64)

    def sect_shift(by):
        return lax.rem(g + 4 + by, 4)

    offsets = list(range(-HOPS, 0)) + list(range(1, HOPS + 1))
    near = [(dom_shift(o), g) for o in offsets] + [(d, sect_shift(-1)), (d, sect_shift(1))]
    sect_peers = [(d, sect_shift(i)) for i in range(1, 4)]
    in_peers = [(block * 8 + lax.rem(place_at + i, 8), g) for i in RING_ORDER]
    block_peers = [(lax.rem(block + i, 8) * 8 + place_at, g) for i in RING_ORDER]
    everyone = near + sect_peers + in_peers + block_peers

    barrier = pltpu.get_barrier_semaphore()
    for peer in everyone:
        pl.semaphore_signal(barrier, inc=1, device_id=peer, device_id_type=MESH)

    def load(at, source, target):
        copy = pltpu.make_async_copy(source, target, load_sem.at[at])
        copy.start()
        return copy

    first = [
        load(0, fields_in.at[:, :, 0, :], fields),
        load(6, pick_in_, pick),
        load(7, send_cycle_in, send_list.at[:, 0 : 6 * SLOTS]),
        load(8, send_layer_in, send_list.at[:, 6 * SLOTS : 8 * SLOTS]),
        load(9, surface_faces_in, send_list.at[:, 8 * SLOTS :]),
    ]
    rest = [
        (residual_in.at[:, :, 0, :], residual),
        (geometry_in.at[:, 0, :], geometry),
        (normals_in, normals),
        (face_scale_in, face_scale),
        (derivatives_in, derivatives),
        (lift_matrix_in, lift_matrix),
        (face_source_in, face_source),
        (face_perm_in, face_perm),
        (surface_count_in, surface_count),
        (surface_points_in.at[:, 0, :], surface_points),
        (surface_weights_in, surface_weights),
        (angles_in, angles),
        (place_in_, place),
        (place_lift_in, place_lift),
        (node_table_in, node_table),
    ]
    q_now[:, 32:SPLIT_PAD, :] = jnp.zeros((6, SPLIT_PAD - 32, ELEMS), F32)
    w_now[:, 32:NODE_PAD, :] = jnp.zeros((6, NODE_PAD - 32, ELEMS), F32)

    def make_parts():
        for c in range(6):
            p1, p2, p3 = split3(q_now[c])
            for at, part in enumerate((p1, p2, p3, p1, p2)):
                q_parts[at * SPLIT_PAD : (at + 1) * SPLIT_PAD, c * ELEMS : (c + 1) * ELEMS] = part

    def make_trace():
        picked = dot(pick[...].astype(BF16), q_parts[...])
        for c in range(6):
            for k in range(4):
                trace[c * FACE_PAD : (c + 1) * FACE_PAD, k * ELEMS : (k + 1) * ELEMS] = picked[
                    k * FACE_PAD : (k + 1) * FACE_PAD, c * ELEMS : (c + 1) * ELEMS
                ]
        high, low = split2(trace[...])
        trace_parts[0:96, :] = high
        trace_parts[96:192, :] = low

    def one_hot(target, index_row, rows):
        width = index_row.shape[1]
        row_of = lax.broadcasted_iota(jnp.int32, (SLOTS, width), 0).astype(F32).astype(BF16)

        for at in range(0, rows, SLOTS):
            wanted = (index_row - at).astype(F32).astype(BF16)
            target[at : at + SLOTS, :] = jnp.where(row_of == wanted, BF16(1), BF16(0))

    later = [load(10 + i, *pair) for i, pair in enumerate(rest)]
    for copy in first[1:]:
        copy.wait()
    one_hot(pick_out, send_list[...], FACES)
    first[0].wait()
    for c in range(6):
        q_now[c, 0:NODES, :] = fields[c]
    make_parts()
    make_trace()

    def copies(step):
        made = []
        for j, peer in enumerate(near):
            landing = 5 - j if j < 6 else 13 - j
            made.append(
                pltpu.make_async_remote_copy(
                    src_ref=send.at[step, j],
                    dst_ref=recv.at[step, landing],
                    send_sem=send_sem.at[step, j],
                    recv_sem=recv_sem.at[step, landing],
                    device_id=peer,
                    device_id_type=MESH,
                )
            )
        return made

    def gather_out(step):
        both = dot(trace_parts[...], pick_out[...])
        gathered = both[0:96] + both[96:192]
        for j in range(8):
            send[step, j] = gathered[:, j * SLOTS : (j + 1) * SLOTS]
        return gathered[:, 8 * SLOTS :]

    surface_0 = gather_out(0)
    pl.semaphore_wait(barrier, len(everyone))
    transfers_0 = copies(0)
    for j in FAR_FIRST:
        transfers_0[j].start()

    small[...] = jnp.zeros_like(small)
    for copy in later:
        copy.wait()
    for c in range(6):
        w_now[c, 0:NODES, :] = residual[c]
    for r in range(3):
        small[r * NODE_PAD : r * NODE_PAD + NODES, 0:NODES] = derivatives[r]
    main, rest = split2(small[0:128, :])
    volume_matrix[...] = (
        dot(main, place[0:128, :].astype(BF16)) + dot(rest, place[128:256, :].astype(BF16))
    ).astype(BF16)
    small[0:128, :] = jnp.zeros((128, 128), F32)
    small[0:NODES, 0:60] = lift_matrix[...]
    main, rest = split2(small[0:SPLIT_PAD, :])
    lift_stack[...] = (
        dot(main, place_lift[0:128, :].astype(BF16)) + dot(rest, place_lift[128:256, :].astype(BF16))
    ).astype(BF16)
    small[0:SPLIT_PAD, :] = jnp.zeros((SPLIT_PAD, 128), F32)

    one_hot(pick_in, face_source[...], 2 * FACES)
    orient = jnp.broadcast_to(face_perm[...], (FACE_PAD, FACES))
    index = jnp.broadcast_to(node_table[:, 0:1], (FACE_PAD, FACES))
    for which in range(1, 6):
        index = jnp.where(orient == which, node_table[:, which : which + 1], index)
    node_index[...] = index

    normal_rows = jnp.concatenate(
        [jnp.concatenate([normals[m, k : k + 1, :] for k in range(4)], axis=1) for m in range(3)]
        + [jnp.zeros((5, FACES), F32)],
        axis=0,
    )
    high, low = split2(jnp.concatenate([normal_rows, normal_rows - normal_rows.astype(BF16).astype(F32)], axis=0))
    picked = dot(high, pick_out[:, 8 * SLOTS :])
    surface_normal = picked[0:8] + picked[8:16]

    def currents(gathered):
        e = [gathered[c * FACE_PAD : (c + 1) * FACE_PAD, :] for c in range(3)]
        h = [gathered[c * FACE_PAD : (c + 1) * FACE_PAD, :] for c in range(3, 6)]
        v = [surface_normal[m : m + 1, :] for m in range(3)]
        return cross(v, h) + [-x for x in cross(v, e)]

    currents_0 = currents(surface_0)

    polar, azimuth = angles[0:1, :], angles[1:2, :]
    direction = jnp.concatenate(
        [
            jnp.sin(polar) * jnp.cos(azimuth),
            jnp.sin(polar) * jnp.sin(azimuth),
            jnp.cos(polar),
            jnp.zeros((5, ANGLES), F32),
        ],
        axis=0,
    )
    d1, d2, d3 = [x.astype(F32) for x in split3(direction)]
    direction_parts[...] = jnp.concatenate([d1, d2, d1, d3, d2, d1], axis=0).astype(BF16)
    points = jnp.concatenate([surface_points[...], jnp.zeros((5, POINTS), F32)], axis=0)
    p1, p2, p3 = [x.astype(F32) for x in split3(points)]
    point_parts[...] = jnp.concatenate([p1, p1, p2, p1, p2, p3], axis=0).T.astype(BF16)

    tables = (table_0, table_1, table_2, table_3)

    def fill_table(nth, besides=(lambda: None,) * 3):
        table = tables[nth]

        def find_phases(target, chunk, of=nth):
            sector = pl.ds(pl.multiple_of(sect_shift(of + 1) * SECTOR, SECTOR), SECTOR)
            at = slice(chunk * TABLE_ROWS, (chunk + 1) * TABLE_ROWS)
            target[...] = dot(point_parts[at, :], direction_parts[:, sector])

        def fill(phases, chunk):
            for first_row in range(0, TABLE_ROWS, 80):
                turns = phases[first_row : first_row + 80, :]
                r = turns - jnp.round(turns)
                u = r * r
                s = u + SIN_MONIC[2]
                c = u + COS_MONIC[2]
                for order in range(1, -1, -1):
                    s = s * u + SIN_MONIC[order]
                    c = c * u + COS_MONIC[order]
                s = s * r
                sine = s * c
                cosine = 1.0 / COS_GAIN - s * s
                out = pl.ds(chunk * TABLE_ROWS + first_row, 80)
                high, low = split2(cosine)
                table[0, out, :] = high
                table[2, out, :] = low
                high, low = split2(sine)
                table[1, out, :] = high
                table[3, out, :] = low

        phases = (phase_even, phase_odd)
        if nth % 2 == 0:
            find_phases(phases[0], 0)
        for chunk in range(POINTS // TABLE_ROWS):
            if chunk + 1 < POINTS // TABLE_ROWS:
                find_phases(phases[(chunk + 1) % 2], chunk + 1)
            elif nth % 2 == 0:
                find_phases(phases[0], 0, nth + 1)
            fill(phases[chunk % 2], chunk)
            if chunk % 2:
                besides[chunk // 2]()

    fill_table(0)
    fill_table(1)

    def local_part(step):
        slopes[...] = dot(volume_matrix[...], q_parts[...])
        both = dot(trace_parts[...], pick_in[0:FACES, :])
        column[...] = both[0:96] + both[96:192]

    local_part(0)

    def advance(step):
        for slot in range(8):
            arrived = recv[step, slot]
            if slot == 6:
                arrived = jnp.where(g > 0, arrived, 0.0)
            if slot == 7:
                arrived = jnp.where(g < 3, arrived, 0.0)
            high, low = split2(arrived)
            received_parts[0:96, slot * SLOTS : (slot + 1) * SLOTS] = high
            received_parts[96:192, slot * SLOTS : (slot + 1) * SLOTS] = low
        both = dot(received_parts[...], pick_in[FACES:, :])
        outer = column[...] + (both[0:96] + both[96:192])
        index = node_index[...]
        in_first = index < 8
        index = index & 7

        def turned(x):
            halves = []
            for half in (slice(0, 8), slice(8, 16)):
                first = jnp.take_along_axis(x[0:8], index[half], axis=0, mode="promise_in_bounds")
                second = jnp.take_along_axis(x[8:16], index[half], axis=0, mode="promise_in_bounds")
                halves.append(jnp.where(in_first[half], first, second))
            return jnp.concatenate(halves, axis=0)

        jump = []
        for c in range(6):
            rows = slice(c * FACE_PAD, (c + 1) * FACE_PAD)
            jump.append(trace[rows, :] - turned(outer[rows, :]))
        flux = [[] for _ in range(6)]
        for k in range(4):
            part = [x[:, k * ELEMS : (k + 1) * ELEMS] for x in jump]
            v = [normals[m, k : k + 1, :] for m in range(3)]
            half = 0.5 * face_scale[k : k + 1, :]
            e, h = part[:3], part[3:]
            e_dot = v[0] * e[0] + v[1] * e[1] + v[2] * e[2]
            h_dot = v[0] * h[0] + v[1] * h[1] + v[2] * h[2]
            ve, vh = cross(v, e), cross(v, h)
            for m in range(3):
                flux[m].append((vh[m] + e[m] - v[m] * e_dot) * half)
                flux[3 + m].append((h[m] - ve[m] - v[m] * h_dot) * half)
        flux_rows = jnp.concatenate([jnp.concatenate(x, axis=0) for x in flux], axis=1)
        f1, f2 = split2(flux_rows)
        lifted = dot(lift_stack[...], jnp.concatenate([f1, f2, f1], axis=0))

        def slope(r, c):
            return slopes[r * NODE_PAD : (r + 1) * NODE_PAD, c * ELEMS : (c + 1) * ELEMS]

        factors = [geometry[i : i + 1, :] for i in range(9)]

        def gradient(m, c):
            return factors[m] * slope(0, c) + factors[3 + m] * slope(1, c) + factors[6 + m] * slope(2, c)

        for c in range(6):
            other = 3 if c < 3 else 0
            a, b = (c + 1) % 3, (c + 2) % 3
            curl = gradient(a, other + b) - gradient(b, other + a)
            if c >= 3:
                curl = -curl
            rate = curl + lifted[0:NODE_PAD, c * ELEMS : (c + 1) * ELEMS]
            w_next = SECTION_A[step] * w_now[c] + TIME_STEP * rate
            q_next = q_now[c, 0:NODE_PAD, :] + SECTION_B[step] * w_next
            if step == 0:
                w_now[c] = w_next
                q_now[c, 0:NODE_PAD, :] = q_next
            else:
                fields_out[c] = q_next[0:NODES]
                residual_out[c] = w_next[0:NODES]

    for copy in transfers_0:
        copy.wait_recv()
    advance(0)

    make_parts()
    make_trace()
    surface_1 = gather_out(1)
    transfers_1 = copies(1)
    for j in FAR_FIRST:
        transfers_1[j].start()
    currents_1 = currents(surface_1)

    turn = [ANGULAR_FREQUENCY * TIME_STEP * x for x in SECTION_C]
    weighted[...] = jnp.zeros_like(weighted)
    live = lax.broadcasted_iota(jnp.int32, (1, SLOTS), 1) < surface_count[...]
    node_weight = [
        jnp.where(live, surface_weights[:, n * SLOTS : (n + 1) * SLOTS], 0.0) for n in range(FACE)
    ]
    node_weight = jnp.concatenate(node_weight + [jnp.zeros((1, SLOTS), F32)], axis=0)
    for c in range(6):
        rows = slice(c * FACE_PAD, (c + 1) * FACE_PAD)
        real = math.cos(turn[0]) * currents_0[c] + math.cos(turn[1]) * currents_1[c]
        imag = math.sin(turn[0]) * currents_0[c] + math.sin(turn[1]) * currents_1[c]
        by_node[0, rows] = real * node_weight
        by_node[1, rows] = imag * -node_weight
    for n in range(FACE):
        at = slice(n * SLOTS, (n + 1) * SLOTS)
        real = by_node[0, pl.ds(n, 6, stride=FACE_PAD), :]
        imag = by_node[1, pl.ds(n, 6, stride=FACE_PAD), :]
        weighted[0, 0:6, at] = real * COS_GAIN
        weighted[0, 8:14, at] = imag * COS_GAIN
        weighted[1, 0:6, at] = imag * -SIN_GAIN
        weighted[1, 8:14, at] = real * SIN_GAIN
    for which in range(2):
        high, low = split2(weighted[which])
        weighted_parts[which, 0:16, :] = high
        weighted_parts[which, 16:32, :] = low
    far_rows[...] = jnp.zeros_like(far_rows)

    def project(nth, first_row, rows):
        table = tables[nth]
        total = far_rows[nth]
        for which in range(2):
            weights = weighted_parts[which, :, pl.ds(first_row, rows)]
            fine = dot(weights, table[which, pl.ds(first_row, rows), :])
            rest = dot(weights[0:16], table[2 + which, pl.ds(first_row, rows), :])
            total += fine[0:16] + fine[16:32] + rest
        far_rows[nth] = total

    def pack(nth):
        for half in range(2):
            at = slice(half * SLOTS, (half + 1) * SLOTS)
            far_part[nth, half * 12 : half * 12 + 6] = far_rows[nth, 0:6, at]
            far_part[nth, half * 12 + 6 : half * 12 + 12] = far_rows[nth, 8:14, at]

    def far_copy(stage, i, peer, source, target):
        copy = pltpu.make_async_remote_copy(
            src_ref=source,
            dst_ref=target,
            send_sem=far_send_sem.at[stage, i],
            recv_sem=far_recv_sem.at[stage, i],
            device_id=peer,
            device_id_type=MESH,
        )
        copy.start()
        return copy

    def first_beside():
        project(0, 0, POINTS)

    def second_beside():
        project(1, 0, POINTS)
        project(2, 0, PAIR_ROWS)

    def third_beside():
        project(2, PAIR_ROWS, PAIR_ROWS)

    fill_table(2, (first_beside, second_beside, third_beside))
    project(2, 2 * PAIR_ROWS, PAIR_ROWS)
    stage_a = []
    for nth in range(3):
        pack(nth)
        stage_a.append(far_copy(0, nth, sect_peers[nth], far_part.at[nth], far_a.at[nth]))
    fill_table(3)
    project(3, 0, POINTS)
    pack(3)

    local_part(1)
    for copy in stage_a:
        copy.wait_recv()
    far_b[place_at] = far_part[3] + far_a[0] + far_a[1] + far_a[2]
    stage_b = [
        far_copy(1, i, peer, far_b.at[place_at], far_b.at[place_at])
        for i, peer in enumerate(in_peers)
    ]
    for copy in transfers_1:
        copy.wait_recv()
    advance(1)
    for copy in stage_b:
        copy.wait_recv()
    total = far_b[0]
    for i in range(1, 8):
        total = total + far_b[i]
    far_c[block] = total
    stage_c = [
        far_copy(2, i, peer, far_c.at[block], far_c.at[block]) for i, peer in enumerate(block_peers)
    ]
    for copy in transfers_0 + transfers_1 + stage_a + stage_b:
        copy.wait_send()
    for copy in stage_c:
        copy.wait()
    total = far_c[0]
    for i in range(1, 8):
        total = total + far_c[i]
    far_out[:, 0:SLOTS] = total[0:12]
    far_out[:, SLOTS:] = total[12:24]


def hand_over(fields, residual, far, fields_out, residual_out, far_out, sem):
    pairs = [
        (fields, fields_out.at[:, :, 0, :]),
        (residual, residual_out.at[:, :, 0, :]),
        (far, far_out),
    ]
    copies = [pltpu.make_async_copy(a, b, sem.at[i]) for i, (a, b) in enumerate(pairs)]
    for copy in copies:
        copy.start()
    for copy in copies:
        copy.wait()


def on_device(
    fields,
    residual,
    geometry,
    normals,
    face_scale,
    derivatives,
    lift_matrix,
    face_source,
    face_perm,
    send_cycle,
    send_layer,
    surface_faces,
    surface_count,
    surface_points,
    surface_weights,
    angles,
):
    pick, place, place_lift, node_table = constant_matrices()
    hbm = pl.BlockSpec(memory_space=pltpu.HBM)
    vmem = pl.BlockSpec(memory_space=pltpu.VMEM)
    fields_out, residual_out, far = pl.pallas_call(
        kernel,
        out_shape=(
            pltpu.VMEM((6, NODES, ELEMS), F32),
            pltpu.VMEM((6, NODES, ELEMS), F32),
            pltpu.VMEM((12, ELEMS), F32),
        ),
        in_specs=[hbm] * 20,
        out_specs=(vmem, vmem, vmem),
        scratch_shapes=[
            pltpu.VMEM((6, SPLIT_PAD, ELEMS), F32),
            pltpu.VMEM((6, NODE_PAD, ELEMS), F32),
            pltpu.VMEM((6, NODES, ELEMS), F32),
            pltpu.VMEM((6, NODES, ELEMS), F32),
            pltpu.VMEM((9, ELEMS), F32),
            pltpu.VMEM((3, 4, ELEMS), F32),
            pltpu.VMEM((4, ELEMS), F32),
            pltpu.VMEM((3, NODES, NODES), F32),
            pltpu.VMEM((NODES, 60), F32),
            pltpu.VMEM((1, FACES), jnp.int32),
            pltpu.VMEM((1, FACES), jnp.int32),
            pltpu.VMEM((1, 9 * SLOTS), jnp.int32),
            pltpu.VMEM((1, 1), jnp.int32),
            pltpu.VMEM((3, POINTS), F32),
            pltpu.VMEM((1, POINTS), F32),
            pltpu.VMEM((2, ANGLES), F32),
            pltpu.VMEM((64, 5 * SPLIT_PAD), F32),
            pltpu.VMEM((256, 5 * SPLIT_PAD), F32),
            pltpu.VMEM((256, 192), F32),
            pltpu.VMEM((FACE_PAD, 8), jnp.int32),
            pltpu.VMEM((5 * SPLIT_PAD, 6 * ELEMS), BF16),
            pltpu.VMEM((128, 128), F32),
            pltpu.VMEM((128, 5 * SPLIT_PAD), BF16),
            pltpu.VMEM((SPLIT_PAD, 192), BF16),
            pltpu.VMEM((96, FACES), F32),
            pltpu.VMEM((192, FACES), BF16),
            pltpu.VMEM((192, 8 * SLOTS), BF16),
            pltpu.VMEM((FACES, 9 * SLOTS), BF16),
            pltpu.VMEM((2 * FACES, FACES), BF16),
            pltpu.VMEM((FACE_PAD, FACES), jnp.int32),
            pltpu.VMEM((2, 8, 96, SLOTS), F32),
            pltpu.VMEM((2, 8, 96, SLOTS), F32),
            pltpu.VMEM((TABLE_ROWS, SECTOR), F32),
            pltpu.VMEM((TABLE_ROWS, SECTOR), F32),
            pltpu.VMEM((4, POINTS, SECTOR), BF16),
            pltpu.VMEM((4, POINTS, SECTOR), BF16),
            pltpu.VMEM((4, POINTS, SECTOR), BF16),
            pltpu.VMEM((4, POINTS, SECTOR), BF16),
            pltpu.VMEM((POINTS, 48), BF16),
            pltpu.VMEM((48, ANGLES), BF16),
            pltpu.VMEM((2, 96, SLOTS), F32),
            pltpu.VMEM((2, 16, POINTS), F32),
            pltpu.VMEM((2, 32, POINTS), BF16),
            pltpu.VMEM((4, 16, SECTOR), F32),
            pltpu.VMEM((128, 6 * ELEMS), F32),
            pltpu.VMEM((96, FACES), F32),
            pltpu.VMEM((4, 24, SLOTS), F32),
            pltpu.VMEM((3, 24, SLOTS), F32),
            pltpu.VMEM((8, 24, SLOTS), F32),
            pltpu.VMEM((8, 24, SLOTS), F32),
            pltpu.SemaphoreType.DMA((30,)),
            pltpu.SemaphoreType.DMA((2, 8)),
            pltpu.SemaphoreType.DMA((2, 8)),
            pltpu.SemaphoreType.DMA((3, 7)),
            pltpu.SemaphoreType.DMA((3, 7)),
        ],
        compiler_params=pltpu.CompilerParams(
            collective_id=0, has_side_effects=True, vmem_limit_bytes=63 * 1024 * 1024
        ),
    )(
        fields[0].transpose(1, 2, 0, 3),
        residual[0].transpose(1, 2, 0, 3),
        geometry[0].transpose(1, 0, 2),
        normals[0, 0],
        face_scale[0, 0],
        derivatives,
        lift_matrix,
        face_source[0],
        face_perm[0],
        send_cycle[0],
        send_layer[0],
        surface_faces[0],
        surface_count,
        surface_points[0].transpose(1, 0, 2),
        surface_weights[0],
        angles,
        pick,
        place,
        place_lift,
        node_table,
    )
    fields_out, residual_out, far = pl.pallas_call(
        hand_over,
        out_shape=(
            jax.ShapeDtypeStruct((6, NODES, 1, ELEMS), F32),
            jax.ShapeDtypeStruct((6, NODES, 1, ELEMS), F32),
            jax.ShapeDtypeStruct((12, ELEMS), F32),
        ),
        in_specs=[vmem] * 3,
        out_specs=(hbm, hbm, hbm),
        scratch_shapes=[pltpu.SemaphoreType.DMA((3,))],
        compiler_params=pltpu.CompilerParams(vmem_limit_bytes=1024 * 1024),
    )(fields_out, residual_out, far)
    return (fields_out.transpose(2, 0, 1, 3)[None], residual_out.transpose(2, 0, 1, 3)[None], far)


def solution(mesh):
    in_specs = (
        P("dom", "sect", None, None, None),
        P("dom", "sect", None, None, None),
        P("dom", "sect", None, None),
        P("dom", "sect", None, None, None),
        P("dom", "sect", None, None),
        P(),
        P(),
        P("dom", "sect", None),
        P("dom", "sect", None),
        P("dom", "sect", None),
        P("dom", "sect", None),
        P("dom", "sect", None),
        P("dom", "sect"),
        P("dom", "sect", None, None),
        P("dom", "sect", None),
        P(),
    )
    out_specs = (
        P("dom", "sect", None, None, None),
        P("dom", "sect", None, None, None),
        P(None, "sect"),
    )
    return jax.shard_map(
        on_device, mesh=mesh, in_specs=in_specs, out_specs=out_specs, check_vma=False
    )
```
